256 devices in a mesh: gx: 16 (over z, core), gy: 16 (over y, x).
Axes of the slice: x: 4, y: 4, z: 8, core: 2. Of those that a mesh axis runs over, the one named last changes fastest.
Arguments:
- diffusivity: float32 [64, 512, 16], P('gx', 'gy'), may hold values from 0.2 to 27
- labels: int32 [64, 512, 16], P('gx', 'gy'), may hold values from 0 to 64, as said below
- obstacles: int32 [64, 512, 16], P('gx', 'gy'), may hold values 0 or 1
Outputs:
- solution: float32 [64, 512, 1024], P('gx', 'gy')
- residual: float32 [64, 512, 1024], P('gx', 'gy')
The draws below stay inside these ranges and needn't reach their ends.
Inputs may be any that keep to these rules, and one draw needn't show every extreme that they name: `labels`: 0 marks a voxel without receptors, k marks a voxel of receptor cluster k; on obstacle voxels the label has no effect.
All inputs are finite; a program needn't handle non-finite values. No bound on the sum of `obstacles` on one device may be relied on, other than what follows from the above.
Results may differ from the reference program's by a relative error of at most 0.0003.
Values sent between devices are 32-bit elements; how exact they have to be, the bound alone decides.
No kernel may reach another device: no remote copies, remote signals or barrier semaphores. Data moves between devices by JAX's collectives and lax.ppermute only.
A program may use at most 64 MiB of HBM per device.

```python
import jax
import jax.numpy as jnp
from jax import lax

NZ = 16
K = 64
ITERS = 3
NX = 64
NY = 512


def draw_labels(key, part):
    key = jax.random.fold_in(key, 11)
    first_key, second_key = jax.random.split(key)
    hitter = jax.random.randint(first_key, (NX, NY, NZ), 0, 8)
    cluster = jax.random.randint(second_key, (NX, NY, NZ), 1, K + 1)
    return jnp.where(hitter == 0, cluster, 0).astype(jnp.int32)


def draw_diffusivity(key, part):
    key = jax.random.fold_in(key, 23)
    rows_pos = (jnp.arange(NX, dtype=jnp.float32) / NX)[:, None, None]
    cols_pos = (jnp.arange(NY, dtype=jnp.float32) / NY)[None, :, None]
    rough = jnp.exp(jax.random.uniform(key, (NX, NY, NZ), jnp.float32, jnp.log(0.3), jnp.log(3.0)))
    trend = jnp.exp(jnp.log(3.0) * (rows_pos + cols_pos))
    return (rough * trend).astype(jnp.float32)


def place_ends(array, rng, least, high):
    shape = array.shape
    place = [jax.random.randint(jax.random.fold_in(rng, axis), (), 0, shape[axis]) for axis in range(len(shape))]
    array = array.at[tuple(place)].set(least)
    longest = shape.index(max(shape))
    place[longest] = (place[longest] + 1) % shape[longest]
    return array.at[tuple(place)].set(high)


def setup_inputs(seed: int = 0) -> dict:
    seeds = jax.random.split(jax.random.key(seed), 4)
    diffusivity = draw_diffusivity(jax.random.fold_in(seeds[3], 71), 0)
    labels = draw_labels(jax.random.fold_in(seeds[3], 71), 0)
    obstacles = place_ends((jax.random.randint(seeds[2], (NX, NY, NZ), 0, 5) < 1).astype(jnp.int32), jax.random.fold_in(seeds[2], 1), 0, 1)
    return {"diffusivity": diffusivity, "labels": labels, "obstacles": obstacles}


HIGH = lax.Precision.HIGHEST

def neighbour_views(padded):
    return [padded[2:, 1:-1, 1:-1], padded[:-2, 1:-1, 1:-1], padded[1:-1, 2:, 1:-1], padded[1:-1, :-2, 1:-1], padded[1:-1, 1:-1, 2:], padded[1:-1, 1:-1, :-2]]

def assemble(padded_cond, padded_label, free_cells, cluster_ids):
    center = padded_cond[1:-1, 1:-1, 1:-1]
    face_cond = []
    for neighbour in neighbour_views(padded_cond):
        product = center * neighbour
        face_cond.append(2.0 * product / jnp.where(product > 0, center + neighbour, 1.0))
    label_nbrs = neighbour_views(padded_label)
    diagonal = free_cells * (face_cond[0] + face_cond[1] + face_cond[2] + face_cond[3] + face_cond[4] + face_cond[5]) + (1.0 - free_cells)
    couple = [free_cells * conduct * (label_nbr == 0).astype(jnp.float32) for conduct, label_nbr in zip(face_cond, label_nbrs)]
    source = jnp.zeros(center.shape + (cluster_ids.shape[0],), jnp.float32)
    for conduct, label_nbr in zip(face_cond, label_nbrs):
        hits = (label_nbr[..., None] == cluster_ids).astype(jnp.float32)
        source = source + (free_cells * conduct)[..., None] * hits
    return (diagonal, couple, source)

def apply_operator(padded4, diagonal, couple):
    center = padded4[1:-1, 1:-1]
    zpad = jnp.pad(center, ((0, 0), (0, 0), (1, 1), (0, 0)))
    result = diagonal[..., None] * center
    result = result - couple[0][..., None] * padded4[2:, 1:-1]
    result = result - couple[1][..., None] * padded4[:-2, 1:-1]
    result = result - couple[2][..., None] * padded4[1:-1, 2:]
    result = result - couple[3][..., None] * padded4[1:-1, :-2]
    result = result - couple[4][..., None] * zpad[:, :, 2:]
    result = result - couple[5][..., None] * zpad[:, :, :-2]
    return result

def inner_block(first_block, second_block):
    width = first_block.shape[-1]
    return lax.dot_general(first_block.reshape(-1, width), second_block.reshape(-1, width), (((0,), (0,)), ((), ())), precision=HIGH)

def times_block(field, matrix):
    width = field.shape[-1]
    return jnp.dot(field.reshape(-1, width), matrix, precision=HIGH).reshape(field.shape)

def solve_gram(matrix, right_side):
    factor = jnp.linalg.cholesky(matrix)
    return jax.scipy.linalg.cho_solve((factor, True), right_side)

def reference(diffusivity, labels, obstacles):
    conductive = diffusivity * (1 - obstacles).astype(jnp.float32)
    free_cells = ((obstacles == 0) & (labels == 0)).astype(jnp.float32)
    padded_cond = jnp.pad(conductive, 1)
    padded_label = jnp.pad(labels, 1)
    cluster_ids = (jnp.arange(K) + 1).astype(jnp.int32)
    diagonal, couple, source = assemble(padded_cond, padded_label, free_cells, cluster_ids)
    solution = jnp.zeros_like(source)
    residual = source
    search = source
    norm_now = inner_block(residual, residual)
    for iteration in range(ITERS):
        padded4 = jnp.pad(search, ((1, 1), (1, 1), (0, 0), (0, 0)))
        image_block = apply_operator(padded4, diagonal, couple)
        step_size = solve_gram(inner_block(search, image_block), norm_now)
        solution = solution + times_block(search, step_size)
        residual = residual - times_block(image_block, step_size)
        if iteration + 1 < ITERS:
            norm_next = inner_block(residual, residual)
            direction_mix = solve_gram(norm_now, norm_next)
            search = residual + times_block(search, direction_mix)
            norm_now = norm_next
    return (solution.reshape(NX, NY, NZ * K), residual.reshape(NX, NY, NZ * K))
```

```python
import jax
import jax.numpy as jnp
from jax import lax
from jax.experimental import pallas as pl
from jax.experimental.pallas import tpu as pltpu
from jax.sharding import PartitionSpec as P

NZ = 16
K = 64
ITERS = 3
DEEP = ITERS + 1

HIGH = lax.Precision.HIGHEST
F32 = jnp.float32


def face(here, there):
    product = here * there
    return 2.0 * product / jnp.where(product > 0, here + there, 1.0)


def krylov_kernel(
    up_ref, here_ref, down_ref, fields_ref, moments_ref,
    cond, label, couple, weight, nbr, diag, v0, v1, v2, v3,
):
    rows = here_ref.shape[1]
    lanes = here_ref.shape[2]
    own = fields_ref.shape[1] // rows
    tall = rows + 2 * DEEP
    for plane, ref in ((0, cond), (1, label)):
        ref[0:DEEP, :] = up_ref[plane]
        ref[DEEP:DEEP + rows, :] = here_ref[plane]
        ref[DEEP + rows:tall, :] = down_ref[plane]
    inner = tall - 2
    lane = lax.broadcasted_iota(jnp.int32, (inner, lanes), 1)
    depth = lane & (NZ - 1)
    center = cond[1:1 + inner, :]
    free = jnp.where((center > 0) & (label[1:1 + inner, :] == 0), 1.0, 0.0)

    def views(ref):
        mid = ref[1:1 + inner, :]
        return [
            ref[2:2 + inner, :],
            ref[0:inner, :],
            pltpu.roll(mid, lanes - NZ, 1),
            pltpu.roll(mid, NZ, 1),
            jnp.where(depth == NZ - 1, 0.0, pltpu.roll(mid, lanes - 1, 1)),
            jnp.where(depth == 0, 0.0, pltpu.roll(mid, 1, 1)),
        ]

    total = jnp.zeros((inner, lanes), F32)
    for side, (there, mark) in enumerate(zip(views(cond), views(label))):
        conduct = face(center, there)
        total = total + conduct
        weight[side] = free * conduct
        nbr[side] = mark
        couple[side] = jnp.where(mark == 0, free * conduct, 0.0)
    diag[...] = free * total + (1.0 - free)

    step = 16
    cluster = lax.broadcasted_iota(jnp.int32, (step, lanes), 0)

    def fill(row, carry):
        for part in range(0, K, step):
            ids = (cluster + (part + 1)).astype(F32)
            acc = jnp.zeros((step, lanes), F32)
            for side in range(6):
                hit = nbr[side, pl.ds(row, 1), :] == ids
                acc = acc + jnp.where(hit, weight[side, pl.ds(row, 1), :], 0.0)
            v0[row, part:part + step, :] = acc
        return carry

    lax.fori_loop(0, inner, fill, 0)

    def power(source, target, offset, count):
        def body(row, carry):
            at = row + offset + 1
            for part in range(0, K, step):
                cut = slice(part, part + step)
                mid = source[row + 1, cut, :]
                acc = diag[pl.ds(at, 1), :] * mid
                acc = acc - couple[0, pl.ds(at, 1), :] * source[row + 2, cut, :]
                acc = acc - couple[1, pl.ds(at, 1), :] * source[row, cut, :]
                acc = acc - couple[2, pl.ds(at, 1), :] * pltpu.roll(mid, lanes - NZ, 1)
                acc = acc - couple[3, pl.ds(at, 1), :] * pltpu.roll(mid, NZ, 1)
                acc = acc - couple[4, pl.ds(at, 1), :] * pltpu.roll(mid, lanes - 1, 1)
                acc = acc - couple[5, pl.ds(at, 1), :] * pltpu.roll(mid, 1, 1)
                target[row, cut, :] = acc
            return carry

        lax.fori_loop(0, count, body, 0)

    power(v0, v1, 0, inner - 2)
    power(v1, v2, 1, inner - 4)
    power(v2, v3, 2, inner - 6)
    for order, ref in enumerate((v0, v1, v2, v3)):
        for row in range(rows):
            fields_ref[order * K:(order + 1) * K, row * own:(row + 1) * own] = ref[
                row + ITERS - order, :, 0:own
            ]
    chunk = 256
    wide = fields_ref.shape[1]
    for pair in range(ITERS):
        parts = []
        for at in range(0, wide, chunk):
            left = fields_ref[pair * K:(pair + 1) * K, at:at + chunk]
            right = fields_ref[pair * K:(pair + 2) * K, at:at + chunk]
            parts.append(lax.dot_general(
                left, right, (((1,), (1,)), ((), ())), precision=HIGH, preferred_element_type=F32
            ))
        while len(parts) > 1:
            parts = [parts[i] + parts[i + 1] for i in range(0, len(parts), 2)]
        moments_ref[pair * K:(pair + 1) * K, :] = parts[0]


def krylov(up, here, down):
    rows, lanes = here.shape[1:]
    own = lanes - 2 * DEEP * NZ
    tall = rows + 2 * DEEP
    inner = tall - 2
    return pl.pallas_call(
        krylov_kernel,
        out_shape=(
            jax.ShapeDtypeStruct(((ITERS + 1) * K, rows * own), F32),
            jax.ShapeDtypeStruct((ITERS * K, 2 * K), F32),
        ),
        in_specs=[pl.BlockSpec(memory_space=pltpu.VMEM)] * 3,
        out_specs=[pl.BlockSpec(memory_space=pltpu.VMEM)] * 2,
        scratch_shapes=[
            pltpu.VMEM((tall, lanes), F32),
            pltpu.VMEM((tall, lanes), F32),
            pltpu.VMEM((6, inner, lanes), F32),
            pltpu.VMEM((6, inner, lanes), F32),
            pltpu.VMEM((6, inner, lanes), F32),
            pltpu.VMEM((inner, lanes), F32),
            pltpu.VMEM((inner, K, lanes), F32),
            pltpu.VMEM((inner - 2, K, lanes), F32),
            pltpu.VMEM((inner - 4, K, lanes), F32),
            pltpu.VMEM((inner - 6, K, lanes), F32),
        ],
        compiler_params=pltpu.CompilerParams(vmem_limit_bytes=40 * 1024 * 1024),
    )(up, here, down)


def gauss_jordan(work, size, panel=8):
    total = work.shape[1]
    sub = lax.broadcasted_iota(jnp.int32, (panel, 128), 0)
    for at in range(0, size, panel):
        tiles = [t for t in range(0, total, 128) if t + 128 > at + panel]
        base = at // 128 * 128
        column = work[:, base:base + 128]
        spread = [
            jnp.broadcast_to(column[:, at - base + j:at - base + j + 1], (size, 128))
            for j in range(panel)
        ]
        small = [s[at:at + panel] for s in spread]
        rows = [work[at:at + panel, t:t + 128] for t in tiles]
        for j in range(panel):
            inverse = 1.0 / jnp.broadcast_to(small[j][j:j + 1], (panel, 128))
            mine = sub == j
            factor = small[j]
            for m in range(j + 1, panel):
                scaled = jnp.broadcast_to(small[m][j:j + 1], (panel, 128)) * inverse
                small[m] = jnp.where(mine, scaled, small[m] - factor * scaled)
            for i, value in enumerate(rows):
                scaled = jnp.broadcast_to(value[j:j + 1], (panel, 128)) * inverse
                rows[i] = jnp.where(mine, scaled, value - factor * scaled)
        for i, t in enumerate(tiles):
            for first, last in ((0, at), (at + panel, size)):
                if first == last:
                    continue
                acc = work[first:last, t:t + 128]
                for j in range(panel):
                    acc = acc - spread[j][first:last] * rows[i][j:j + 1]
                work[first:last, t:t + 128] = acc
            work[at:at + panel, t:t + 128] = rows[i]


def finish_kernel(moments_ref, fields_ref, solution_ref, residual_ref, work, coeff, mixed):
    rows, cols = solution_ref.shape[:2]
    size = ITERS * K

    def moment(k):
        pair, half = divmod(k, 2)
        return moments_ref[pair * K:(pair + 1) * K, half * K:(half + 1) * K]

    moments = []
    for k in range(2 * ITERS):
        value = moment(k)
        moments.append(0.5 * (value + value.T))
    for i in range(ITERS):
        for j in range(ITERS):
            work[i * K:(i + 1) * K, j * K:(j + 1) * K] = moments[i + j + 1]
        work[i * K:(i + 1) * K, size:size + K] = moments[i]
    gauss_jordan(work, size)
    answer = work[:, size:size + K]
    coeff[0:size, 0:K] = answer
    coeff[size:size + K, 0:K] = jnp.zeros((K, K), F32)
    coeff[0:K, K:2 * K] = (
        lax.broadcasted_iota(jnp.int32, (K, K), 0) == lax.broadcasted_iota(jnp.int32, (K, K), 1)
    ).astype(F32)
    coeff[K:K + size, K:2 * K] = -answer
    own = cols * NZ
    low = lax.broadcasted_iota(jnp.int32, (cols, 2 * K), 1) < K
    for row in range(rows):
        mixed[...] = lax.dot_general(
            fields_ref[:, row * own:(row + 1) * own], coeff[...], (((0,), (0,)), ((), ())),
            precision=HIGH, preferred_element_type=F32,
        )
        for z in range(0, NZ, 2):
            even = mixed[pl.ds(z, cols, stride=NZ), :]
            odd = mixed[pl.ds(z + 1, cols, stride=NZ), :]
            solution_ref[row, :, z * K:(z + 2) * K] = jnp.where(low, even, pltpu.roll(odd, K, 1))
            residual_ref[row, :, z * K:(z + 2) * K] = jnp.where(low, pltpu.roll(even, K, 1), odd)


def finish(moments, fields, rows, cols):
    out = jax.ShapeDtypeStruct((rows, cols, NZ * K), F32)
    return pl.pallas_call(
        finish_kernel,
        out_shape=(out, out),
        in_specs=[pl.BlockSpec(memory_space=pltpu.VMEM)] * 2,
        out_specs=[pl.BlockSpec(memory_space=pltpu.VMEM)] * 2,
        scratch_shapes=[
            pltpu.VMEM((ITERS * K, (ITERS + 1) * K), F32),
            pltpu.VMEM(((ITERS + 1) * K, 2 * K), F32),
            pltpu.VMEM((cols * NZ, 2 * K), F32),
        ],
        compiler_params=pltpu.CompilerParams(vmem_limit_bytes=40 * 1024 * 1024),
    )(moments, fields)


def total_over(value, axis):
    count = lax.axis_size(axis)
    stride = 1
    while stride < count:
        value = value + lax.ppermute(value, axis, [(i, i ^ stride) for i in range(count)])
        stride *= 2
    return value


def from_both(first, last, axis):
    count = lax.axis_size(axis)
    forward = [(i, i + 1) for i in range(count - 1)]
    backward = [(target, source) for source, target in forward]
    return lax.ppermute(last, axis, forward), lax.ppermute(first, axis, backward)


def shards(diffusivity, labels, obstacles):
    rows, cols = diffusivity.shape[:2]
    conductive = diffusivity * (1 - obstacles).astype(F32)
    cells = jnp.stack([conductive, labels.astype(F32)]).reshape(2, rows, cols * NZ)
    edge = DEEP * NZ
    before, after = from_both(cells[:, :, :edge], cells[:, :, -edge:], "gy")
    here = jnp.concatenate([cells, after, before], axis=2)
    up, down = from_both(here[:, :DEEP], here[:, rows - DEEP:], "gx")
    fields, moments = krylov(up, here, down)
    moments = total_over(total_over(moments, "gx"), "gy")
    return finish(moments, fields, rows, cols)


def solution(mesh):
    in_specs = (P("gx", "gy", None), P("gx", "gy", None), P("gx", "gy", None))
    out_specs = (P("gx", "gy", None), P("gx", "gy", None))
    return jax.shard_map(shards, mesh=mesh, in_specs=in_specs, out_specs=out_specs, check_vma=False)
```

```python
import math

import jax
import jax.numpy as jnp
from jax import lax
from jax.experimental import pallas as pl
from jax.experimental.pallas import tpu as pltpu
from jax.sharding import PartitionSpec as P

NZ = 16
K = 64
ITERS = 3
DEEP = ITERS + 1

BODY = 3 * K // 4
TAIL = 8

HIGH = lax.Precision.HIGHEST
F32 = jnp.float32


def face(here, there):
    product = here * there
    return 2.0 * product / jnp.where(product > 0, here + there, 1.0)


def krylov_kernel(
    up_ref, here_ref, down_ref, fields_ref, keep_ref, send_ref, unit_ref,
    cond, label, couple, weight, nbr, diag, v0, v1, v2, v3, gram,
):
    rows = here_ref.shape[1]
    lanes = here_ref.shape[2]
    own = fields_ref.shape[1] // rows
    tall = rows + 2 * DEEP
    for plane, ref in ((0, cond), (1, label)):
        ref[0:DEEP, :] = up_ref[plane]
        ref[DEEP:DEEP + rows, :] = here_ref[plane]
        ref[DEEP + rows:tall, :] = down_ref[plane]
    inner = tall - 2
    lane = lax.broadcasted_iota(jnp.int32, (inner, lanes), 1)
    depth = lane & (NZ - 1)
    center = cond[1:1 + inner, :]
    free = jnp.where((center > 0) & (label[1:1 + inner, :] == 0), 1.0, 0.0)

    def views(ref):
        mid = ref[1:1 + inner, :]
        return [
            ref[2:2 + inner, :],
            ref[0:inner, :],
            pltpu.roll(mid, lanes - NZ, 1),
            pltpu.roll(mid, NZ, 1),
            jnp.where(depth == NZ - 1, 0.0, pltpu.roll(mid, lanes - 1, 1)),
            jnp.where(depth == 0, 0.0, pltpu.roll(mid, 1, 1)),
        ]

    total = jnp.zeros((inner, lanes), F32)
    for side, (there, mark) in enumerate(zip(views(cond), views(label))):
        conduct = face(center, there)
        total = total + conduct
        weight[side] = free * conduct
        nbr[side] = mark
        couple[side] = jnp.where(mark == 0, free * conduct, 0.0)
    mean = jnp.sum(free * total, keepdims=True) / jnp.maximum(jnp.sum(free, keepdims=True), 1.0)
    unit, inverse = power_of_two(1.5 * mean)
    unit_ref[...] = jnp.broadcast_to(unit, unit_ref.shape)
    diag[...] = free * (total * inverse - 1.0)
    for side in range(6):
        couple[side] = couple[side] * inverse

    step = 16
    cluster = lax.broadcasted_iota(jnp.int32, (step, lanes), 0)

    def fill(row, carry):
        for part in range(0, K, step):
            ids = (cluster + (part + 1)).astype(F32)
            acc = jnp.zeros((step, lanes), F32)
            for side in range(6):
                hit = nbr[side, pl.ds(row, 1), :] == ids
                acc = acc + jnp.where(hit, weight[side, pl.ds(row, 1), :], 0.0)
            v0[row, part:part + step, :] = acc
        return carry

    lax.fori_loop(0, inner, fill, 0)

    def power(source, target, offset, count):
        def body(row, carry):
            at = row + offset + 1
            for part in range(0, K, step):
                cut = slice(part, part + step)
                mid = source[row + 1, cut, :]
                acc = diag[pl.ds(at, 1), :] * mid
                acc = acc - couple[0, pl.ds(at, 1), :] * source[row + 2, cut, :]
                acc = acc - couple[1, pl.ds(at, 1), :] * source[row, cut, :]
                acc = acc - couple[2, pl.ds(at, 1), :] * pltpu.roll(mid, lanes - NZ, 1)
                acc = acc - couple[3, pl.ds(at, 1), :] * pltpu.roll(mid, NZ, 1)
                acc = acc - couple[4, pl.ds(at, 1), :] * pltpu.roll(mid, lanes - 1, 1)
                acc = acc - couple[5, pl.ds(at, 1), :] * pltpu.roll(mid, 1, 1)
                target[row, cut, :] = acc
            return carry

        lax.fori_loop(0, count, body, 0)

    power(v0, v1, 0, inner - 2)
    power(v1, v2, 1, inner - 4)
    power(v2, v3, 2, inner - 6)
    for order, ref in enumerate((v0, v1, v2, v3)):
        for row in range(rows):
            fields_ref[order * K:(order + 1) * K, row * own:(row + 1) * own] = ref[
                row + ITERS - order, :, 0:own
            ]
    chunk = 256
    wide = fields_ref.shape[1]
    for at in range(0, wide, chunk):
        part = lax.dot_general(
            fields_ref[0:ITERS * K, at:at + chunk], fields_ref[:, at:at + chunk],
            (((1,), (1,)), ((), ())), precision=HIGH, preferred_element_type=F32,
        )
        gram[...] = part if at == 0 else gram[...] + part
    pack(gram, unit, keep_ref, send_ref)


def power_of_two(value):
    unit = jnp.full(value.shape, 2.0 ** -4, F32)
    inverse = jnp.full(value.shape, 2.0 ** 4, F32)
    for exponent in range(-4, 9):
        more = value > 2.0 ** (exponent + 0.5)
        unit = jnp.where(more, 2.0 ** (exponent + 1), unit)
        inverse = jnp.where(more, 2.0 ** (-exponent - 1), inverse)
    return unit, inverse


def pair_add(pair, value):
    high, low = pair
    total = high + value
    back = total - high
    return total, low + ((high - (total - back)) + (value - back))


EXPANSION = []
for k in range(2 * ITERS):
    first, second = k // 2, k - k // 2
    terms = {}
    for a in range(first + 1):
        for b in range(second + 1):
            terms[a, b] = math.comb(first, a) * math.comb(second, b)
    EXPANSION.append(sorted(terms.items(), reverse=True))


def pack(gram, unit, keep_ref, send_ref):
    row = lax.broadcasted_iota(jnp.int32, (K, K), 0)
    col = lax.broadcasted_iota(jnp.int32, (K, K), 1)
    blocks = {}
    lines = {}
    for k in range(2 * ITERS):
        for at, _ in EXPANSION[k]:
            if at not in blocks:
                a, b = at
                blocks[at] = gram[a * K:(a + 1) * K, b * K:(b + 1) * K]
                lines[at] = jnp.sum(jnp.where(row == col, blocks[at], 0.0), axis=0, keepdims=True)
    scale = jnp.ones_like(unit)
    moments, highs, lows = [], [], []
    for k in range(2 * ITERS):
        moment = jnp.zeros((K, K), F32)
        pair = (jnp.zeros((1, K), F32), jnp.zeros((1, K), F32))
        for at, factor in EXPANSION[k]:
            moment = moment + float(factor) * blocks[at]
            bit = 1
            while bit <= factor:
                if factor & bit:
                    pair = pair_add(pair, float(bit) * lines[at])
                bit *= 2
        moments.append(moment * scale)
        highs.append(pair[0] * scale)
        lows.append(pair[1] * scale)
        scale = scale * unit
    packs = [
        jnp.where(row > col, moments[i], jnp.where(row < col, moments[i + 1], 0.0))
        for i in range(0, 2 * ITERS, 2)
    ]
    first = jnp.concatenate(packs[:2], axis=1)
    second = jnp.concatenate([packs[2][:K // 2], packs[2][K // 2:]], axis=1)
    gap = jnp.zeros((1, K), F32)
    rest = jnp.zeros((2, 2 * K), F32)

    def tail(at):
        return [
            jnp.concatenate([highs[at], highs[at + 1]], axis=1),
            jnp.concatenate([highs[at + 2], gap], axis=1),
            rest,
            jnp.concatenate([lows[at], lows[at + 1]], axis=1),
            jnp.concatenate([lows[at + 2], gap], axis=1),
            rest,
        ]

    top = jnp.concatenate([first[:BODY]] + tail(0), axis=0)
    bottom = jnp.concatenate([first[BODY:], second] + tail(3), axis=0)
    low_core = lax.rem(lax.axis_index("gx"), 2) == 0
    keep_ref[...] = jnp.where(low_core, top, bottom)
    send_ref[...] = jnp.where(low_core, bottom, top)


def unpack(top, bottom):
    row = lax.broadcasted_iota(jnp.int32, (K, K), 0)
    col = lax.broadcasted_iota(jnp.int32, (K, K), 1)
    first = jnp.concatenate([top[:BODY], bottom[:K - BODY]], axis=0)
    second = bottom[K - BODY:BODY]
    packs = [first[:, :K], first[:, K:], jnp.concatenate([second[:, :K], second[:, K:]], axis=0)]
    moments, pairs = [], []
    for value in packs:
        flip = value.T
        moments.append(jnp.where(row > col, value, flip))
        moments.append(jnp.where(row < col, value, flip))
    for half in (top, bottom):
        for at in ((0, 0), (0, K), (1, 0)):
            pairs.append(tuple(
                half[BODY + shift + at[0]:BODY + shift + at[0] + 1, at[1]:at[1] + K]
                for shift in (0, TAIL // 2)
            ))
    return moments, pairs


def krylov(up, here, down):
    rows, lanes = here.shape[1:]
    own = lanes - 2 * DEEP * NZ
    tall = rows + 2 * DEEP
    inner = tall - 2
    return pl.pallas_call(
        krylov_kernel,
        out_shape=(
            jax.ShapeDtypeStruct(((ITERS + 1) * K, rows * own), F32),
            jax.ShapeDtypeStruct((BODY + TAIL, 2 * K), F32),
            jax.ShapeDtypeStruct((BODY + TAIL, 2 * K), F32),
            jax.ShapeDtypeStruct((8, 2 * K), F32),
        ),
        in_specs=[pl.BlockSpec(memory_space=pltpu.VMEM)] * 3,
        out_specs=[pl.BlockSpec(memory_space=pltpu.VMEM)] * 4,
        scratch_shapes=[
            pltpu.VMEM((tall, lanes), F32),
            pltpu.VMEM((tall, lanes), F32),
            pltpu.VMEM((6, inner, lanes), F32),
            pltpu.VMEM((6, inner, lanes), F32),
            pltpu.VMEM((6, inner, lanes), F32),
            pltpu.VMEM((inner, lanes), F32),
            pltpu.VMEM((inner, K, lanes), F32),
            pltpu.VMEM((inner - 2, K, lanes), F32),
            pltpu.VMEM((inner - 4, K, lanes), F32),
            pltpu.VMEM((inner - 6, K, lanes), F32),
            pltpu.VMEM((ITERS * K, (ITERS + 1) * K), F32),
        ],
        compiler_params=pltpu.CompilerParams(vmem_limit_bytes=40 * 1024 * 1024),
    )(up, here, down)


def gauss_jordan(work, size, panel=8):
    total = work.shape[1]
    sub = lax.broadcasted_iota(jnp.int32, (panel, 128), 0)
    for at in range(0, size, panel):
        tiles = [t for t in range(0, total, 128) if t + 128 > at + panel]
        base = at // 128 * 128
        column = work[:, base:base + 128]
        spread = [
            jnp.broadcast_to(column[:, at - base + j:at - base + j + 1], (size, 128))
            for j in range(panel)
        ]
        small = [s[at:at + panel] for s in spread]
        rows = [work[at:at + panel, t:t + 128] for t in tiles]
        for j in range(panel):
            inverse = 1.0 / jnp.broadcast_to(small[j][j:j + 1], (panel, 128))
            mine = sub == j
            factor = small[j]
            for m in range(j + 1, panel):
                scaled = jnp.broadcast_to(small[m][j:j + 1], (panel, 128)) * inverse
                small[m] = jnp.where(mine, scaled, small[m] - factor * scaled)
            for i, value in enumerate(rows):
                scaled = jnp.broadcast_to(value[j:j + 1], (panel, 128)) * inverse
                rows[i] = jnp.where(mine, scaled, value - factor * scaled)
        for i, t in enumerate(tiles):
            for first, last in ((0, at), (at + panel, size)):
                if first == last:
                    continue
                acc = work[first:last, t:t + 128]
                for j in range(panel):
                    acc = acc - spread[j][first:last] * rows[i][j:j + 1]
                work[first:last, t:t + 128] = acc
            work[at:at + panel, t:t + 128] = rows[i]


def finish_kernel(
    mine_ref, other_ref, unit_ref, fields_ref, solution_ref, residual_ref, work, coeff, mixed
):
    rows, cols = solution_ref.shape[:2]
    size = ITERS * K
    low_core = lax.rem(lax.axis_index("gx"), 2) == 0
    mine, other = mine_ref[...], other_ref[...]
    moments, pairs = unpack(
        jnp.where(low_core, mine, other), jnp.where(low_core, other, mine)
    )
    common, inverse = power_of_two(
        jnp.sum(pairs[1][0], keepdims=True) / jnp.sum(pairs[0][0], keepdims=True)
    )
    scale = jnp.ones_like(common)
    for k in range(2 * ITERS):
        moments[k] = moments[k] * scale
        pairs[k] = (pairs[k][0] * scale, pairs[k][1] * scale)
        scale = scale * inverse
    eye = (
        lax.broadcasted_iota(jnp.int32, (K, K), 0) == lax.broadcasted_iota(jnp.int32, (K, K), 1)
    )

    def whole(k):
        return jnp.where(eye, pairs[k][0] + pairs[k][1], moments[k])

    for level in range(2 * ITERS - 1):
        if level < ITERS:
            work[level * K:(level + 1) * K, size:size + K] = whole(0)
        block = whole(1)
        for i in range(ITERS):
            j = level - i
            if 0 <= j < ITERS:
                work[i * K:(i + 1) * K, j * K:(j + 1) * K] = block
        for k in range(len(moments) - 1):
            high, low = pair_add(pairs[k + 1], -pairs[k][0])
            pairs[k] = (high, low - pairs[k][1])
            moments[k] = moments[k + 1] - moments[k]
        moments.pop()
        pairs.pop()
    gauss_jordan(work, size)
    unit = unit_ref[0:1, 0:1]
    ratio = unit * inverse
    shift = ratio - 1.0
    y0, y1, y2 = (work[i * K:(i + 1) * K, size:size + K] * inverse for i in range(ITERS))
    y0 = y0 + shift * y1 + (shift * shift) * y2
    y1 = ratio * y1 + (2.0 * ratio * shift) * y2
    y2 = (ratio * ratio) * y2
    coeff[0:K, 0:K] = y0
    coeff[K:2 * K, 0:K] = y1
    coeff[2 * K:3 * K, 0:K] = y2
    coeff[3 * K:4 * K, 0:K] = jnp.zeros((K, K), F32)
    coeff[0:K, K:2 * K] = eye.astype(F32) - unit * y0
    coeff[K:2 * K, K:2 * K] = -unit * (y0 + y1)
    coeff[2 * K:3 * K, K:2 * K] = -unit * (y1 + y2)
    coeff[3 * K:4 * K, K:2 * K] = -unit * y2
    own = cols * NZ
    low = lax.broadcasted_iota(jnp.int32, (cols, 2 * K), 1) < K
    for row in range(rows):
        mixed[...] = lax.dot_general(
            fields_ref[:, row * own:(row + 1) * own], coeff[...], (((0,), (0,)), ((), ())),
            precision=HIGH, preferred_element_type=F32,
        )
        for z in range(0, NZ, 2):
            even = mixed[pl.ds(z, cols, stride=NZ), :]
            odd = mixed[pl.ds(z + 1, cols, stride=NZ), :]
            solution_ref[row, :, z * K:(z + 2) * K] = jnp.where(low, even, pltpu.roll(odd, K, 1))
            residual_ref[row, :, z * K:(z + 2) * K] = jnp.where(low, pltpu.roll(even, K, 1), odd)


def finish(mine, other, unit, fields, rows, cols):
    out = jax.ShapeDtypeStruct((rows, cols, NZ * K), F32)
    return pl.pallas_call(
        finish_kernel,
        out_shape=(out, out),
        in_specs=[pl.BlockSpec(memory_space=pltpu.VMEM)] * 4,
        out_specs=[pl.BlockSpec(memory_space=pltpu.VMEM)] * 2,
        scratch_shapes=[
            pltpu.VMEM((ITERS * K, (ITERS + 1) * K), F32),
            pltpu.VMEM(((ITERS + 1) * K, 2 * K), F32),
            pltpu.VMEM((cols * NZ, 2 * K), F32),
        ],
        compiler_params=pltpu.CompilerParams(vmem_limit_bytes=40 * 1024 * 1024),
    )(mine, other, unit, fields)


def add_parts(value, *others):
    for other in others:
        total = value + other
        back = total - value
        error = (value - (total - back)) + (other - back)
        half = BODY + TAIL // 2
        value = jnp.concatenate([total[:half], total[half:] + error[BODY:half]], axis=0)
    return value


def from_ahead(value, axis, distance, stride, ring):
    def place(i, d):
        low, high = i % stride, i // (stride * ring)
        return (high * ring + (i // stride + d) % ring) * stride + low

    count = lax.axis_size(axis)
    return lax.ppermute(value, axis, [(i, place(i, -distance)) for i in range(count)])


def sum_of_four(value, axis, stride):
    return add_parts(value, *(from_ahead(value, axis, d, stride, 4) for d in (1, -1, 2)))


def sum_of_eight(value, axis, stride):
    ahead, behind = (from_ahead(value, axis, d, stride, 8) for d in (1, -1))
    two = add_parts(value, ahead)
    three = add_parts(two, behind)
    return add_parts(
        three, from_ahead(three, axis, 3, stride, 8), from_ahead(two, axis, -3, stride, 8)
    )


def swap_cores(value):
    return lax.ppermute(value, "gx", [(i, i ^ 1) for i in range(lax.axis_size("gx"))])


def from_both(first, last, axis):
    count = lax.axis_size(axis)
    forward = [(i, i + 1) for i in range(count - 1)]
    backward = [(target, source) for source, target in forward]
    return lax.ppermute(last, axis, forward), lax.ppermute(first, axis, backward)


def shards(diffusivity, labels, obstacles):
    rows, cols = diffusivity.shape[:2]
    conductive = diffusivity * (1 - obstacles).astype(F32)
    cells = jnp.stack([conductive, labels.astype(F32)]).reshape(2, rows, cols * NZ)
    edge = DEEP * NZ
    before, after = from_both(cells[:, :, :edge], cells[:, :, -edge:], "gy")
    here = jnp.concatenate([cells, after, before], axis=2)
    up, down = from_both(here[:, :DEEP], here[:, rows - DEEP:], "gx")
    fields, keep, send, unit = krylov(up, here, down)
    mine = add_parts(keep, swap_cores(send))
    mine = sum_of_eight(mine, "gx", 2)
    mine = sum_of_four(mine, "gy", 1)
    mine = sum_of_four(mine, "gy", 4)
    return finish(mine, swap_cores(mine), unit, fields, rows, cols)


def solution(mesh):
    in_specs = (P("gx", "gy", None), P("gx", "gy", None), P("gx", "gy", None))
    out_specs = (P("gx", "gy", None), P("gx", "gy", None))
    return jax.shard_map(shards, mesh=mesh, in_specs=in_specs, out_specs=out_specs, check_vma=False)
```

```python
import math

import jax
import jax.numpy as jnp
from jax import lax
from jax.experimental import pallas as pl
from jax.experimental.pallas import tpu as pltpu
from jax.sharding import PartitionSpec as P

NZ = 16
K = 64
ITERS = 3
DEEP = ITERS + 1

BODY = 3 * K // 4
TAIL = 8
PANEL = 8

HIGH = lax.Precision.HIGHEST
F32 = jnp.float32


def face(here, there):
    product = here * there
    return 2.0 * product / jnp.where(product > 0, here + there, 1.0)


def krylov_kernel(
    up_ref, here_ref, down_ref, fields_ref, keep_ref, send_ref, unit_ref,
    cond, label, couple, weight, nbr, diag, v0, v1, v2, v3, gram,
):
    rows = here_ref.shape[1]
    lanes = here_ref.shape[2]
    own = fields_ref.shape[1] // rows
    tall = rows + 2 * DEEP
    for plane, ref in ((0, cond), (1, label)):
        ref[0:DEEP, :] = up_ref[plane]
        ref[DEEP:DEEP + rows, :] = here_ref[plane]
        ref[DEEP + rows:tall, :] = down_ref[plane]
    inner = tall - 2
    lane = lax.broadcasted_iota(jnp.int32, (inner, lanes), 1)
    depth = lane & (NZ - 1)
    center = cond[1:1 + inner, :]
    free = jnp.where((center > 0) & (label[1:1 + inner, :] == 0), 1.0, 0.0)

    def views(ref):
        mid = ref[1:1 + inner, :]
        return [
            ref[2:2 + inner, :],
            ref[0:inner, :],
            pltpu.roll(mid, lanes - NZ, 1),
            pltpu.roll(mid, NZ, 1),
            jnp.where(depth == NZ - 1, 0.0, pltpu.roll(mid, lanes - 1, 1)),
            jnp.where(depth == 0, 0.0, pltpu.roll(mid, 1, 1)),
        ]

    total = jnp.zeros((inner, lanes), F32)
    for side, (there, mark) in enumerate(zip(views(cond), views(label))):
        conduct = face(center, there)
        total = total + conduct
        weight[side] = free * conduct
        nbr[side] = mark
        couple[side] = jnp.where(mark == 0, free * conduct, 0.0)
    mean = jnp.sum(free * total, keepdims=True) / jnp.maximum(jnp.sum(free, keepdims=True), 1.0)
    unit, inverse = power_of_two(1.5 * mean)
    unit_ref[...] = jnp.broadcast_to(unit, unit_ref.shape)
    diag[...] = free * (total * inverse - 1.0)
    for side in range(6):
        couple[side] = couple[side] * inverse

    step = 16
    cluster = lax.broadcasted_iota(jnp.int32, (step, lanes), 0)

    def fill(row, carry):
        for part in range(0, K, step):
            ids = (cluster + (part + 1)).astype(F32)
            acc = jnp.zeros((step, lanes), F32)
            for side in range(6):
                hit = nbr[side, pl.ds(row, 1), :] == ids
                acc = acc + jnp.where(hit, weight[side, pl.ds(row, 1), :], 0.0)
            v0[row, part:part + step, :] = acc
        return carry

    lax.fori_loop(0, inner, fill, 0, unroll=True)

    def power(source, target, offset, count):
        def body(row, carry):
            at = row + offset + 1
            for part in range(0, K, step):
                cut = slice(part, part + step)
                mid = source[row + 1, cut, :]
                acc = diag[pl.ds(at, 1), :] * mid
                acc = acc - couple[0, pl.ds(at, 1), :] * source[row + 2, cut, :]
                acc = acc - couple[1, pl.ds(at, 1), :] * source[row, cut, :]
                acc = acc - couple[2, pl.ds(at, 1), :] * pltpu.roll(mid, lanes - NZ, 1)
                acc = acc - couple[3, pl.ds(at, 1), :] * pltpu.roll(mid, NZ, 1)
                acc = acc - couple[4, pl.ds(at, 1), :] * pltpu.roll(mid, lanes - 1, 1)
                acc = acc - couple[5, pl.ds(at, 1), :] * pltpu.roll(mid, 1, 1)
                target[row, cut, :] = acc
            return carry

        lax.fori_loop(0, count, body, 0, unroll=True)

    power(v0, v1, 0, inner - 2)
    power(v1, v2, 1, inner - 4)
    power(v2, v3, 2, inner - 6)
    for order, ref in enumerate((v0, v1, v2, v3)):
        for row in range(rows):
            fields_ref[order * K:(order + 1) * K, row * own:(row + 1) * own] = ref[
                row + ITERS - order, :, 0:own
            ]
    chunk = 256
    wide = fields_ref.shape[1]
    for at in range(0, wide, chunk):
        part = lax.dot_general(
            fields_ref[0:ITERS * K, at:at + chunk], fields_ref[:, at:at + chunk],
            (((1,), (1,)), ((), ())), precision=HIGH, preferred_element_type=F32,
        )
        gram[...] = part if at == 0 else gram[...] + part
    pack(gram, unit, keep_ref, send_ref)


def power_of_two(value):
    unit = jnp.full(value.shape, 2.0 ** -4, F32)
    inverse = jnp.full(value.shape, 2.0 ** 4, F32)
    for exponent in range(-4, 9):
        more = value > 2.0 ** (exponent + 0.5)
        unit = jnp.where(more, 2.0 ** (exponent + 1), unit)
        inverse = jnp.where(more, 2.0 ** (-exponent - 1), inverse)
    return unit, inverse


def pair_add(pair, value):
    high, low = pair
    total = high + value
    back = total - high
    return total, low + ((high - (total - back)) + (value - back))


EXPANSION = []
for k in range(2 * ITERS):
    first, second = k // 2, k - k // 2
    terms = {}
    for a in range(first + 1):
        for b in range(second + 1):
            terms[a, b] = math.comb(first, a) * math.comb(second, b)
    EXPANSION.append(sorted(terms.items(), reverse=True))


def pack(gram, unit, keep_ref, send_ref):
    row = lax.broadcasted_iota(jnp.int32, (K, K), 0)
    col = lax.broadcasted_iota(jnp.int32, (K, K), 1)
    blocks = {}
    lines = {}
    for k in range(2 * ITERS):
        for at, _ in EXPANSION[k]:
            if at not in blocks:
                a, b = at
                blocks[at] = gram[a * K:(a + 1) * K, b * K:(b + 1) * K]
                lines[at] = jnp.sum(jnp.where(row == col, blocks[at], 0.0), axis=0, keepdims=True)
    scale = jnp.ones_like(unit)
    moments, highs, lows = [], [], []
    for k in range(2 * ITERS):
        moment = jnp.zeros((K, K), F32)
        pair = (jnp.zeros((1, K), F32), jnp.zeros((1, K), F32))
        for at, factor in EXPANSION[k]:
            moment = moment + float(factor) * blocks[at]
            bit = 1
            while bit <= factor:
                if factor & bit:
                    pair = pair_add(pair, float(bit) * lines[at])
                bit *= 2
        moments.append(moment * scale)
        highs.append(pair[0] * scale)
        lows.append(pair[1] * scale)
        scale = scale * unit
    packs = [
        jnp.where(row > col, moments[i], jnp.where(row < col, moments[i + 1], 0.0))
        for i in range(0, 2 * ITERS, 2)
    ]
    first = jnp.concatenate(packs[:2], axis=1)
    second = jnp.concatenate([packs[2][:K // 2], packs[2][K // 2:]], axis=1)
    gap = jnp.zeros((1, K), F32)
    rest = jnp.zeros((2, 2 * K), F32)

    def tail(at):
        return [
            jnp.concatenate([highs[at], highs[at + 1]], axis=1),
            jnp.concatenate([highs[at + 2], gap], axis=1),
            rest,
            jnp.concatenate([lows[at], lows[at + 1]], axis=1),
            jnp.concatenate([lows[at + 2], gap], axis=1),
            rest,
        ]

    top = jnp.concatenate([first[:BODY]] + tail(0), axis=0)
    bottom = jnp.concatenate([first[BODY:], second] + tail(3), axis=0)
    low_core = lax.rem(lax.axis_index("gx"), 2) == 0
    keep_ref[...] = jnp.where(low_core, top, bottom)
    send_ref[...] = jnp.where(low_core, bottom, top)


def unpack(top, bottom):
    row = lax.broadcasted_iota(jnp.int32, (K, K), 0)
    col = lax.broadcasted_iota(jnp.int32, (K, K), 1)
    first = jnp.concatenate([top[:BODY], bottom[:K - BODY]], axis=0)
    second = bottom[K - BODY:BODY]
    packs = [first[:, :K], first[:, K:], jnp.concatenate([second[:, :K], second[:, K:]], axis=0)]
    moments, pairs = [], []
    for value in packs:
        flip = value.T
        moments.append(jnp.where(row > col, value, flip))
        moments.append(jnp.where(row < col, value, flip))
    for half in (top, bottom):
        for at in ((0, 0), (0, K), (1, 0)):
            pairs.append(tuple(
                half[BODY + shift + at[0]:BODY + shift + at[0] + 1, at[1]:at[1] + K]
                for shift in (0, TAIL // 2)
            ))
    return moments, pairs


def krylov(up, here, down):
    rows, lanes = here.shape[1:]
    own = lanes - 2 * DEEP * NZ
    tall = rows + 2 * DEEP
    inner = tall - 2
    return pl.pallas_call(
        krylov_kernel,
        out_shape=(
            jax.ShapeDtypeStruct(((ITERS + 1) * K, rows * own), F32),
            jax.ShapeDtypeStruct((BODY + TAIL, 2 * K), F32),
            jax.ShapeDtypeStruct((BODY + TAIL, 2 * K), F32),
            jax.ShapeDtypeStruct((8, 2 * K), F32),
        ),
        in_specs=[pl.BlockSpec(memory_space=pltpu.VMEM)] * 3,
        out_specs=[pl.BlockSpec(memory_space=pltpu.VMEM)] * 4,
        scratch_shapes=[
            pltpu.VMEM((tall, lanes), F32),
            pltpu.VMEM((tall, lanes), F32),
            pltpu.VMEM((6, inner, lanes), F32),
            pltpu.VMEM((6, inner, lanes), F32),
            pltpu.VMEM((6, inner, lanes), F32),
            pltpu.VMEM((inner, lanes), F32),
            pltpu.VMEM((inner, K, lanes), F32),
            pltpu.VMEM((inner - 2, K, lanes), F32),
            pltpu.VMEM((inner - 4, K, lanes), F32),
            pltpu.VMEM((inner - 6, K, lanes), F32),
            pltpu.VMEM((ITERS * K, (ITERS + 1) * K), F32),
        ],
        compiler_params=pltpu.CompilerParams(vmem_limit_bytes=40 * 1024 * 1024),
    )(up, here, down)


def splat(value, j):
    return jnp.broadcast_to(value[:, j:j + 1], (value.shape[0], 128))


def line(value, j):
    return jnp.broadcast_to(value[j:j + 1], (PANEL, 128))


def gauss_jordan(work, start, stop):
    total = work.shape[1]
    sub = lax.broadcasted_iota(jnp.int32, (PANEL, 128), 0)
    small = None
    for at in range(start, stop, PANEL):
        base = at // 128 * 128
        column = work[start:stop, base:base + 128]
        spread = [splat(column, at - base + j) for j in range(PANEL)]
        if small is None:
            small = [value[at - start:at - start + PANEL] for value in spread]
        after = at + PANEL
        ahead, below = [], []
        if after < stop:
            base = after // 128 * 128
            strip = work[at:after, base:base + 128]
            ahead = [splat(strip, after - base + j) for j in range(PANEL)]
            strip = work[after:after + PANEL, base:base + 128]
            below = [splat(strip, after - base + j) for j in range(PANEL)]
        tiles = [t for t in range(0, total, 128) if t + 128 > after]
        values = small + ahead + [work[at:after, t:t + 128] for t in tiles]
        for j in range(PANEL):
            factor = values[j]
            inverse = 1.0 / line(factor, j)
            for i in range(j + 1, len(values)):
                scaled = line(values[i], j) * inverse
                values[i] = jnp.where(sub == j, scaled, values[i] - factor * scaled)
        ahead = values[PANEL:PANEL + len(ahead)]
        rows = values[PANEL + len(ahead):]
        if after < stop:
            small = []
            for value, column in zip(below, ahead):
                for j in range(PANEL):
                    value = value - spread[j][after - start:after - start + PANEL] * line(column, j)
                small.append(value)
        for row, t in zip(rows, tiles):
            for first, last in ((after, min(after + PANEL, stop)), (after + PANEL, stop), (start, at)):
                if first >= last:
                    continue
                acc = work[first:last, t:t + 128]
                for j in range(PANEL):
                    acc = acc - spread[j][first - start:last - start] * row[j:j + 1]
                work[first:last, t:t + 128] = acc
            work[at:after, t:t + 128] = row


def solve(work, size):
    total = work.shape[1]
    for start in range(0, size, K):
        stop = start + K
        gauss_jordan(work, start, stop)
        if stop < size:
            base = stop // 128 * 128
            work[stop:size, base:total] = work[stop:size, base:total] - jnp.dot(
                work[stop:size, start:stop], work[start:stop, base:total],
                precision=HIGH, preferred_element_type=F32,
            )
    for start in range(size - 2 * K, -1, -K):
        stop = start + K
        work[start:stop, size:total] = work[start:stop, size:total] - jnp.dot(
            work[start:stop, stop:size], work[stop:size, size:total],
            precision=HIGH, preferred_element_type=F32,
        )


def finish_kernel(
    mine_ref, other_ref, unit_ref, fields_ref, solution_ref, residual_ref, work, coeff, mixed
):
    rows, cols = solution_ref.shape[:2]
    size = ITERS * K
    low_core = lax.rem(lax.axis_index("gx"), 2) == 0
    mine, other = mine_ref[...], other_ref[...]
    moments, pairs = unpack(
        jnp.where(low_core, mine, other), jnp.where(low_core, other, mine)
    )
    common, inverse = power_of_two(
        jnp.sum(pairs[1][0], keepdims=True) / jnp.sum(pairs[0][0], keepdims=True)
    )
    scale = jnp.ones_like(common)
    for k in range(2 * ITERS):
        moments[k] = moments[k] * scale
        pairs[k] = (pairs[k][0] * scale, pairs[k][1] * scale)
        scale = scale * inverse
    eye = (
        lax.broadcasted_iota(jnp.int32, (K, K), 0) == lax.broadcasted_iota(jnp.int32, (K, K), 1)
    )

    def whole(k):
        return jnp.where(eye, pairs[k][0] + pairs[k][1], moments[k])

    for level in range(2 * ITERS - 1):
        if level < ITERS:
            work[level * K:(level + 1) * K, size:size + K] = whole(0)
        block = whole(1)
        for i in range(ITERS):
            j = level - i
            if 0 <= j < ITERS:
                work[i * K:(i + 1) * K, j * K:(j + 1) * K] = block
        for k in range(len(moments) - 1):
            high, low = pair_add(pairs[k + 1], -pairs[k][0])
            pairs[k] = (high, low - pairs[k][1])
            moments[k] = moments[k + 1] - moments[k]
        moments.pop()
        pairs.pop()
    solve(work, size)
    unit = unit_ref[0:1, 0:1]
    ratio = unit * inverse
    shift = ratio - 1.0
    y0, y1, y2 = (work[i * K:(i + 1) * K, size:size + K] * inverse for i in range(ITERS))
    y0 = y0 + shift * y1 + (shift * shift) * y2
    y1 = ratio * y1 + (2.0 * ratio * shift) * y2
    y2 = (ratio * ratio) * y2
    coeff[0:K, 0:K] = y0
    coeff[K:2 * K, 0:K] = y1
    coeff[2 * K:3 * K, 0:K] = y2
    coeff[3 * K:4 * K, 0:K] = jnp.zeros((K, K), F32)
    coeff[0:K, K:2 * K] = eye.astype(F32) - unit * y0
    coeff[K:2 * K, K:2 * K] = -unit * (y0 + y1)
    coeff[2 * K:3 * K, K:2 * K] = -unit * (y1 + y2)
    coeff[3 * K:4 * K, K:2 * K] = -unit * y2
    own = cols * NZ
    low = lax.broadcasted_iota(jnp.int32, (cols, 2 * K), 1) < K
    for row in range(rows):
        mixed[...] = lax.dot_general(
            coeff[...], fields_ref[:, row * own:(row + 1) * own], (((0,), (0,)), ((), ())),
            precision=HIGH, preferred_element_type=F32,
        ).T
        for z in range(0, NZ, 2):
            even = mixed[pl.ds(z, cols, stride=NZ), :]
            odd = mixed[pl.ds(z + 1, cols, stride=NZ), :]
            solution_ref[row, :, z * K:(z + 2) * K] = jnp.where(low, even, pltpu.roll(odd, K, 1))
            residual_ref[row, :, z * K:(z + 2) * K] = jnp.where(low, pltpu.roll(even, K, 1), odd)


def finish(mine, other, unit, fields, rows, cols):
    out = jax.ShapeDtypeStruct((rows, cols, NZ * K), F32)
    return pl.pallas_call(
        finish_kernel,
        out_shape=(out, out),
        in_specs=[pl.BlockSpec(memory_space=pltpu.VMEM)] * 4,
        out_specs=[pl.BlockSpec(memory_space=pltpu.VMEM)] * 2,
        scratch_shapes=[
            pltpu.VMEM((ITERS * K, (ITERS + 1) * K), F32),
            pltpu.VMEM(((ITERS + 1) * K, 2 * K), F32),
            pltpu.VMEM((cols * NZ, 2 * K), F32),
        ],
        compiler_params=pltpu.CompilerParams(vmem_limit_bytes=40 * 1024 * 1024),
    )(mine, other, unit, fields)


def add_parts(value, *others):
    half = BODY + TAIL // 2
    lost = jnp.zeros_like(value[BODY:half])
    for other in others:
        total = value + other
        old, new, add = value[BODY:half], total[BODY:half], other[BODY:half]
        back = new - old
        lost = lost + ((old - (new - back)) + (add - back))
        value = total
    return jnp.concatenate([value[:half], value[half:] + lost], axis=0)


def flipped(value, axis, *masks):
    count = lax.axis_size(axis)
    return [lax.ppermute(value, axis, [(i, i ^ mask) for i in range(count)]) for mask in masks]


def sum_of_all(value, axis):
    count = lax.axis_size(axis)
    parts = lax.all_to_all(jnp.broadcast_to(value[None], (count,) + value.shape), axis, 0, 0)
    return add_parts(*(parts[i] for i in range(count)))


def from_both(first, last, axis):
    count = lax.axis_size(axis)
    forward = [(i, i + 1) for i in range(count - 1)]
    backward = [(target, source) for source, target in forward]
    return lax.ppermute(last, axis, forward), lax.ppermute(first, axis, backward)


def shards(diffusivity, labels, obstacles):
    rows, cols = diffusivity.shape[:2]
    conductive = diffusivity * (1 - obstacles).astype(F32)
    plane = lax.broadcasted_iota(jnp.int32, (2,) + conductive.shape, 0)
    cells = jnp.where(plane == 0, conductive[None], labels.astype(F32)[None])
    cells = cells.reshape(2, rows, cols * NZ)
    edge = DEEP * NZ
    before, after = from_both(cells[:, :, :edge], cells[:, :, -edge:], "gy")
    here = jnp.concatenate([cells, after, before], axis=2)
    up, down = from_both(here[:, :DEEP], here[:, rows - DEEP:], "gx")
    fields, keep, send, unit = krylov(up, here, down)
    mine = add_parts(keep, *flipped(send, "gx", 1))
    mine = add_parts(mine, *flipped(mine, "gx", 2, 4, 6))
    mine = add_parts(mine, *flipped(mine, "gx", 8))
    mine = sum_of_all(mine, "gy")
    return finish(mine, *flipped(mine, "gx", 1), unit, fields, rows, cols)


def solution(mesh):
    in_specs = (P("gx", "gy", None), P("gx", "gy", None), P("gx", "gy", None))
    out_specs = (P("gx", "gy", None), P("gx", "gy", None))
    return jax.shard_map(shards, mesh=mesh, in_specs=in_specs, out_specs=out_specs, check_vma=False)
```

```python
import math

import jax
import jax.numpy as jnp
from jax import lax
from jax.experimental import pallas as pl
from jax.experimental.pallas import tpu as pltpu
from jax.sharding import PartitionSpec as P

NZ = 16
K = 64
ITERS = 3
DEEP = ITERS + 1

BODY = 3 * K // 4
TAIL = 8
PANEL = 8

HIGH = lax.Precision.HIGHEST
F32 = jnp.float32


def face(here, there):
    product = here * there
    return 2.0 * product / jnp.where(product > 0, here + there, 1.0)


def krylov_kernel(
    up_ref, here_ref, down_ref, fields_ref, keep_ref, send_ref, unit_ref,
    cond, label, couple, weight, nbr, diag, v0, v1, v2, v3, gram,
):
    rows = here_ref.shape[1]
    lanes = here_ref.shape[2]
    own = fields_ref.shape[1] // rows
    tall = rows + 2 * DEEP
    for plane, ref in ((0, cond), (1, label)):
        ref[0:DEEP, :] = up_ref[plane]
        ref[DEEP:DEEP + rows, :] = here_ref[plane]
        ref[DEEP + rows:tall, :] = down_ref[plane]
    inner = tall - 2
    lane = lax.broadcasted_iota(jnp.int32, (inner, lanes), 1)
    depth = lane & (NZ - 1)
    center = cond[1:1 + inner, :]
    free = jnp.where((center > 0) & (label[1:1 + inner, :] == 0), 1.0, 0.0)

    def views(ref):
        mid = ref[1:1 + inner, :]
        return [
            ref[2:2 + inner, :],
            ref[0:inner, :],
            pltpu.roll(mid, lanes - NZ, 1),
            pltpu.roll(mid, NZ, 1),
            jnp.where(depth == NZ - 1, 0.0, pltpu.roll(mid, lanes - 1, 1)),
            jnp.where(depth == 0, 0.0, pltpu.roll(mid, 1, 1)),
        ]

    total = jnp.zeros((inner, lanes), F32)
    for side, (there, mark) in enumerate(zip(views(cond), views(label))):
        conduct = face(center, there)
        total = total + conduct
        weight[side] = free * conduct
        nbr[side] = mark
        couple[side] = jnp.where(mark == 0, free * conduct, 0.0)
    mean = jnp.sum(free * total, keepdims=True) / jnp.maximum(jnp.sum(free, keepdims=True), 1.0)
    unit, inverse = power_of_two(1.5 * mean)
    unit_ref[...] = jnp.broadcast_to(unit, unit_ref.shape)
    diag[...] = free * (total * inverse - 1.0)
    for side in range(6):
        couple[side] = couple[side] * inverse

    step = 16
    cluster = lax.broadcasted_iota(jnp.int32, (step, lanes), 0)

    def fill(row, carry):
        for part in range(0, K, step):
            ids = (cluster + (part + 1)).astype(F32)
            acc = jnp.zeros((step, lanes), F32)
            for side in range(6):
                hit = nbr[side, pl.ds(row, 1), :] == ids
                acc = acc + jnp.where(hit, weight[side, pl.ds(row, 1), :], 0.0)
            v0[row, part:part + step, :] = acc
        return carry

    lax.fori_loop(0, inner, fill, 0, unroll=True)

    def power(source, target, offset, count):
        def body(row, carry):
            at = row + offset + 1
            for part in range(0, K, step):
                cut = slice(part, part + step)
                mid = source[row + 1, cut, :]
                acc = diag[pl.ds(at, 1), :] * mid
                acc = acc - couple[0, pl.ds(at, 1), :] * source[row + 2, cut, :]
                acc = acc - couple[1, pl.ds(at, 1), :] * source[row, cut, :]
                acc = acc - couple[2, pl.ds(at, 1), :] * pltpu.roll(mid, lanes - NZ, 1)
                acc = acc - couple[3, pl.ds(at, 1), :] * pltpu.roll(mid, NZ, 1)
                acc = acc - couple[4, pl.ds(at, 1), :] * pltpu.roll(mid, lanes - 1, 1)
                acc = acc - couple[5, pl.ds(at, 1), :] * pltpu.roll(mid, 1, 1)
                target[row, cut, :] = acc
            return carry

        lax.fori_loop(0, count, body, 0, unroll=True)

    power(v0, v1, 0, inner - 2)
    power(v1, v2, 1, inner - 4)
    power(v2, v3, 2, inner - 6)
    for order, ref in enumerate((v0, v1, v2, v3)):
        for row in range(rows):
            fields_ref[order * K:(order + 1) * K, row * own:(row + 1) * own] = ref[
                row + ITERS - order, :, 0:own
            ]
    chunk = 256
    wide = fields_ref.shape[1]
    for at in range(0, wide, chunk):
        part = lax.dot_general(
            fields_ref[0:ITERS * K, at:at + chunk], fields_ref[:, at:at + chunk],
            (((1,), (1,)), ((), ())), precision=HIGH, preferred_element_type=F32,
        )
        gram[...] = part if at == 0 else gram[...] + part
    pack(gram, unit, keep_ref, send_ref)


def power_of_two(value):
    unit = jnp.full(value.shape, 2.0 ** -4, F32)
    inverse = jnp.full(value.shape, 2.0 ** 4, F32)
    for exponent in range(-4, 9):
        more = value > 2.0 ** (exponent + 0.5)
        unit = jnp.where(more, 2.0 ** (exponent + 1), unit)
        inverse = jnp.where(more, 2.0 ** (-exponent - 1), inverse)
    return unit, inverse


def pair_add(pair, value):
    high, low = pair
    total = high + value
    back = total - high
    return total, low + ((high - (total - back)) + (value - back))


EXPANSION = []
for k in range(2 * ITERS):
    first, second = k // 2, k - k // 2
    terms = {}
    for a in range(first + 1):
        for b in range(second + 1):
            terms[a, b] = math.comb(first, a) * math.comb(second, b)
    EXPANSION.append(sorted(terms.items(), reverse=True))


def pack(gram, unit, keep_ref, send_ref):
    row = lax.broadcasted_iota(jnp.int32, (K, K), 0)
    col = lax.broadcasted_iota(jnp.int32, (K, K), 1)
    blocks = {}
    lines = {}
    for k in range(2 * ITERS):
        for at, _ in EXPANSION[k]:
            if at not in blocks:
                a, b = at
                blocks[at] = gram[a * K:(a + 1) * K, b * K:(b + 1) * K]
                lines[at] = jnp.sum(jnp.where(row == col, blocks[at], 0.0), axis=0, keepdims=True)
    scale = jnp.ones_like(unit)
    moments, highs, lows = [], [], []
    for k in range(2 * ITERS):
        moment = jnp.zeros((K, K), F32)
        pair = (jnp.zeros((1, K), F32), jnp.zeros((1, K), F32))
        for at, factor in EXPANSION[k]:
            moment = moment + float(factor) * blocks[at]
            bit = 1
            while bit <= factor:
                if factor & bit:
                    pair = pair_add(pair, float(bit) * lines[at])
                bit *= 2
        moments.append(moment * scale)
        highs.append(pair[0] * scale)
        lows.append(pair[1] * scale)
        scale = scale * unit
    packs = [
        jnp.where(row > col, moments[i], jnp.where(row < col, moments[i + 1], 0.0))
        for i in range(0, 2 * ITERS, 2)
    ]
    first = jnp.concatenate(packs[:2], axis=1)
    second = jnp.concatenate([packs[2][:K // 2], packs[2][K // 2:]], axis=1)
    gap = jnp.zeros((1, K), F32)
    rest = jnp.zeros((2, 2 * K), F32)

    def tail(at):
        return [
            jnp.concatenate([highs[at], highs[at + 1]], axis=1),
            jnp.concatenate([highs[at + 2], gap], axis=1),
            rest,
            jnp.concatenate([lows[at], lows[at + 1]], axis=1),
            jnp.concatenate([lows[at + 2], gap], axis=1),
            rest,
        ]

    top = jnp.concatenate([first[:BODY]] + tail(0), axis=0)
    bottom = jnp.concatenate([first[BODY:], second] + tail(3), axis=0)
    low_core = lax.rem(lax.axis_index("gx"), 2) == 0
    keep_ref[...] = jnp.where(low_core, top, bottom)
    send_ref[...] = jnp.where(low_core, bottom, top)


def unpack(top, bottom):
    row = lax.broadcasted_iota(jnp.int32, (K, K), 0)
    col = lax.broadcasted_iota(jnp.int32, (K, K), 1)
    first = jnp.concatenate([top[:BODY], bottom[:K - BODY]], axis=0)
    second = bottom[K - BODY:BODY]
    packs = [first[:, :K], first[:, K:], jnp.concatenate([second[:, :K], second[:, K:]], axis=0)]
    moments, pairs = [], []
    for value in packs:
        flip = value.T
        moments.append(jnp.where(row > col, value, flip))
        moments.append(jnp.where(row < col, value, flip))
    for half in (top, bottom):
        for at in ((0, 0), (0, K), (1, 0)):
            pairs.append(tuple(
                half[BODY + shift + at[0]:BODY + shift + at[0] + 1, at[1]:at[1] + K]
                for shift in (0, TAIL // 2)
            ))
    return moments, pairs


def krylov(up, here, down):
    rows, lanes = here.shape[1:]
    own = lanes - 2 * DEEP * NZ
    tall = rows + 2 * DEEP
    inner = tall - 2
    return pl.pallas_call(
        krylov_kernel,
        out_shape=(
            jax.ShapeDtypeStruct(((ITERS + 1) * K, rows * own), F32),
            jax.ShapeDtypeStruct((BODY + TAIL, 2 * K), F32),
            jax.ShapeDtypeStruct((BODY + TAIL, 2 * K), F32),
            jax.ShapeDtypeStruct((8, 2 * K), F32),
        ),
        in_specs=[pl.BlockSpec(memory_space=pltpu.VMEM)] * 3,
        out_specs=[pl.BlockSpec(memory_space=pltpu.VMEM)] * 4,
        scratch_shapes=[
            pltpu.VMEM((tall, lanes), F32),
            pltpu.VMEM((tall, lanes), F32),
            pltpu.VMEM((6, inner, lanes), F32),
            pltpu.VMEM((6, inner, lanes), F32),
            pltpu.VMEM((6, inner, lanes), F32),
            pltpu.VMEM((inner, lanes), F32),
            pltpu.VMEM((inner, K, lanes), F32),
            pltpu.VMEM((inner - 2, K, lanes), F32),
            pltpu.VMEM((inner - 4, K, lanes), F32),
            pltpu.VMEM((inner - 6, K, lanes), F32),
            pltpu.VMEM((ITERS * K, (ITERS + 1) * K), F32),
        ],
        compiler_params=pltpu.CompilerParams(vmem_limit_bytes=40 * 1024 * 1024),
    )(up, here, down)


def splat(value, j):
    return jnp.broadcast_to(value[:, j:j + 1], (value.shape[0], 128))


def line(value, j):
    return jnp.broadcast_to(value[j:j + 1], (PANEL, 128))


def gauss_jordan(work, start, stop):
    total = work.shape[1]
    sub = lax.broadcasted_iota(jnp.int32, (PANEL, 128), 0)
    small = None
    for at in range(start, stop, PANEL):
        base = at // 128 * 128
        column = work[start:stop, base:base + 128]
        spread = [splat(column, at - base + j) for j in range(PANEL)]
        if small is None:
            small = [value[at - start:at - start + PANEL] for value in spread]
        after = at + PANEL
        ahead, below = [], []
        if after < stop:
            base = after // 128 * 128
            strip = work[at:after, base:base + 128]
            ahead = [splat(strip, after - base + j) for j in range(PANEL)]
            strip = work[after:after + PANEL, base:base + 128]
            below = [splat(strip, after - base + j) for j in range(PANEL)]
        tiles = [t for t in range(0, total, 128) if t + 128 > after]
        values = small + ahead + [work[at:after, t:t + 128] for t in tiles]
        scale = jnp.ones((PANEL, 128), F32)
        for j in range(PANEL):
            inverse = 1.0 / line(values[j], j)
            scale = jnp.where(sub == j, inverse, scale)
            factor = jnp.where(sub == j, 0.0, values[j]) * inverse
            for i in range(j + 1, len(values)):
                values[i] = values[i] - factor * line(values[i], j)
        values = [value * scale for value in values]
        ahead = values[PANEL:PANEL + len(ahead)]
        rows = values[PANEL + len(ahead):]
        if after < stop:
            small = []
            for value, column in zip(below, ahead):
                for j in range(PANEL):
                    value = value - spread[j][after - start:after - start + PANEL] * line(column, j)
                small.append(value)
        for row, t in zip(rows, tiles):
            for first, last in ((after, min(after + PANEL, stop)), (after + PANEL, stop), (start, at)):
                if first >= last:
                    continue
                acc = work[first:last, t:t + 128]
                for j in range(PANEL):
                    acc = acc - spread[j][first - start:last - start] * row[j:j + 1]
                work[first:last, t:t + 128] = acc
            work[at:after, t:t + 128] = row


def solve(work, size):
    total = work.shape[1]
    for start in range(0, size, K):
        stop = start + K
        gauss_jordan(work, start, stop)
        if stop < size:
            base = stop // 128 * 128
            work[stop:size, base:total] = work[stop:size, base:total] - jnp.dot(
                work[stop:size, start:stop], work[start:stop, base:total],
                precision=HIGH, preferred_element_type=F32,
            )
    for start in range(size - 2 * K, -1, -K):
        stop = start + K
        work[start:stop, size:total] = work[start:stop, size:total] - jnp.dot(
            work[start:stop, stop:size], work[stop:size, size:total],
            precision=HIGH, preferred_element_type=F32,
        )


def finish_kernel(
    mine_ref, other_ref, unit_ref, fields_ref, solution_out, residual_out,
    work, coeff, mixed, solution_ref, residual_ref, sems,
):
    rows, cols = solution_ref.shape[:2]
    size = ITERS * K
    low_core = lax.rem(lax.axis_index("gx"), 2) == 0
    mine, other = mine_ref[...], other_ref[...]
    moments, pairs = unpack(
        jnp.where(low_core, mine, other), jnp.where(low_core, other, mine)
    )
    common, inverse = power_of_two(
        jnp.sum(pairs[1][0], keepdims=True) / jnp.sum(pairs[0][0], keepdims=True)
    )
    scale = jnp.ones_like(common)
    for k in range(2 * ITERS):
        moments[k] = moments[k] * scale
        pairs[k] = (pairs[k][0] * scale, pairs[k][1] * scale)
        scale = scale * inverse
    eye = (
        lax.broadcasted_iota(jnp.int32, (K, K), 0) == lax.broadcasted_iota(jnp.int32, (K, K), 1)
    )

    def whole(k):
        return jnp.where(eye, pairs[k][0] + pairs[k][1], moments[k])

    for level in range(2 * ITERS - 1):
        if level < ITERS:
            work[level * K:(level + 1) * K, size:size + K] = whole(0)
        block = whole(1)
        for i in range(ITERS):
            j = level - i
            if 0 <= j < ITERS:
                work[i * K:(i + 1) * K, j * K:(j + 1) * K] = block
        for k in range(len(moments) - 1):
            high, low = pair_add(pairs[k + 1], -pairs[k][0])
            pairs[k] = (high, low - pairs[k][1])
            moments[k] = moments[k + 1] - moments[k]
        moments.pop()
        pairs.pop()
    solve(work, size)
    unit = unit_ref[0:1, 0:1]
    ratio = unit * inverse
    shift = ratio - 1.0
    y0, y1, y2 = (work[i * K:(i + 1) * K, size:size + K] * inverse for i in range(ITERS))
    y0 = y0 + shift * y1 + (shift * shift) * y2
    y1 = ratio * y1 + (2.0 * ratio * shift) * y2
    y2 = (ratio * ratio) * y2
    coeff[0:K, 0:K] = y0
    coeff[K:2 * K, 0:K] = y1
    coeff[2 * K:3 * K, 0:K] = y2
    coeff[3 * K:4 * K, 0:K] = jnp.zeros((K, K), F32)
    coeff[0:K, K:2 * K] = eye.astype(F32) - unit * y0
    coeff[K:2 * K, K:2 * K] = -unit * (y0 + y1)
    coeff[2 * K:3 * K, K:2 * K] = -unit * (y1 + y2)
    coeff[3 * K:4 * K, K:2 * K] = -unit * y2
    own = cols * NZ
    low = lax.broadcasted_iota(jnp.int32, (cols, 2 * K), 1) < K
    copies = []
    for row in range(rows):
        mixed[...] = lax.dot_general(
            coeff[...], fields_ref[:, row * own:(row + 1) * own], (((0,), (0,)), ((), ())),
            precision=HIGH, preferred_element_type=F32,
        ).T
        for z in range(0, NZ, 2):
            even = mixed[pl.ds(z, cols, stride=NZ), :]
            odd = mixed[pl.ds(z + 1, cols, stride=NZ), :]
            solution_ref[row, :, z * K:(z + 2) * K] = jnp.where(low, even, pltpu.roll(odd, K, 1))
            residual_ref[row, :, z * K:(z + 2) * K] = jnp.where(low, pltpu.roll(even, K, 1), odd)
        for side, (here, there) in enumerate(
            ((solution_ref, solution_out), (residual_ref, residual_out))
        ):
            copy = pltpu.make_async_copy(here.at[row], there.at[row], sems.at[side, row])
            copy.start()
            copies.append(copy)
    for copy in copies:
        copy.wait()


def finish(mine, other, unit, fields, rows, cols):
    out = jax.ShapeDtypeStruct((rows, cols, NZ * K), F32)
    return pl.pallas_call(
        finish_kernel,
        out_shape=(out, out),
        in_specs=[pl.BlockSpec(memory_space=pltpu.VMEM)] * 4,
        out_specs=[pl.BlockSpec(memory_space=pl.ANY)] * 2,
        scratch_shapes=[
            pltpu.VMEM((ITERS * K, (ITERS + 1) * K), F32),
            pltpu.VMEM(((ITERS + 1) * K, 2 * K), F32),
            pltpu.VMEM((cols * NZ, 2 * K), F32),
            pltpu.VMEM((rows, cols, NZ * K), F32),
            pltpu.VMEM((rows, cols, NZ * K), F32),
            pltpu.SemaphoreType.DMA((2, rows)),
        ],
        compiler_params=pltpu.CompilerParams(vmem_limit_bytes=40 * 1024 * 1024),
    )(mine, other, unit, fields)


def add_parts(value, *others):
    half = BODY + TAIL // 2
    lost = jnp.zeros_like(value[BODY:half])
    for other in others:
        total = value + other
        old, new, add = value[BODY:half], total[BODY:half], other[BODY:half]
        back = new - old
        lost = lost + ((old - (new - back)) + (add - back))
        value = total
    return jnp.concatenate([value[:half], value[half:] + lost], axis=0)


def flipped(value, axis, *masks):
    count = lax.axis_size(axis)
    return [lax.ppermute(value, axis, [(i, i ^ mask) for i in range(count)]) for mask in masks]


def sum_of_all(value, axis):
    count = lax.axis_size(axis)
    parts = lax.all_to_all(jnp.broadcast_to(value[None], (count,) + value.shape), axis, 0, 0)
    return add_parts(*(parts[i] for i in range(count)))


def from_both(first, last, axis):
    count = lax.axis_size(axis)
    even = lax.rem(lax.axis_index(axis), 2) == 0
    outer = [(i, ((i + 1) ^ 1) - 1) for i in range(1, count - 1)]
    inner = [(i, i ^ 1) for i in range(count)]
    one = lax.ppermute(jnp.where(even, first, last), axis, outer)
    two = lax.ppermute(jnp.where(even, last, first), axis, inner)
    return jnp.where(even, one, two), jnp.where(even, two, one)


def shards(diffusivity, labels, obstacles):
    rows, cols = diffusivity.shape[:2]
    conductive = diffusivity * (1 - obstacles).astype(F32)
    plane = lax.broadcasted_iota(jnp.int32, (2,) + conductive.shape, 0)
    cells = jnp.where(plane == 0, conductive[None], labels.astype(F32)[None])
    cells = lax.optimization_barrier(cells).reshape(2, rows, cols * NZ)
    edge = DEEP * NZ
    before, after = from_both(cells[:, :, :edge], cells[:, :, -edge:], "gy")
    here = jnp.concatenate([cells, after, before], axis=2)
    up, down = from_both(here[:, :DEEP], here[:, rows - DEEP:], "gx")
    fields, keep, send, unit = krylov(up, here, down)
    mine = add_parts(keep, *flipped(send, "gx", 1))
    mine = add_parts(mine, *flipped(mine, "gx", 2, 4, 6))
    mine = add_parts(mine, *flipped(mine, "gx", 8))
    mine = sum_of_all(mine, "gy")
    return finish(mine, *flipped(mine, "gx", 1), unit, fields, rows, cols)


def solution(mesh):
    in_specs = (P("gx", "gy", None), P("gx", "gy", None), P("gx", "gy", None))
    out_specs = (P("gx", "gy", None), P("gx", "gy", None))
    return jax.shard_map(shards, mesh=mesh, in_specs=in_specs, out_specs=out_specs, check_vma=False)
```

```python
import math

import jax
import jax.numpy as jnp
from jax import lax
from jax.experimental import pallas as pl
from jax.experimental.pallas import tpu as pltpu
from jax.sharding import PartitionSpec as P

NZ = 16
K = 64
ITERS = 3
DEEP = ITERS + 1

BODY = 3 * K // 4
TAIL = 8
PANEL = 8

HIGH = lax.Precision.HIGHEST
F32 = jnp.float32


def face(here, there):
    product = here * there
    return 2.0 * product / jnp.where(product > 0, here + there, 1.0)


def krylov_kernel(
    up_ref, here_ref, down_ref, fields_ref, keep_ref, send_ref, unit_ref,
    cond, label, couple, weight, nbr, diag, v0, v1, v2, gram,
):
    rows = here_ref.shape[1]
    lanes = here_ref.shape[2]
    own = fields_ref.shape[1] // rows
    tall = rows + 2 * DEEP
    for plane, ref in ((0, cond), (1, label)):
        ref[0:DEEP, :] = up_ref[plane]
        ref[DEEP:DEEP + rows, :] = here_ref[plane]
        ref[DEEP + rows:tall, :] = down_ref[plane]
    inner = tall - 2
    lane = lax.broadcasted_iota(jnp.int32, (inner, lanes), 1)
    depth = lane & (NZ - 1)
    center = cond[1:1 + inner, :]
    free = jnp.where((center > 0) & (label[1:1 + inner, :] == 0), 1.0, 0.0)

    def views(ref):
        mid = ref[1:1 + inner, :]
        return [
            ref[2:2 + inner, :],
            ref[0:inner, :],
            pltpu.roll(mid, lanes - NZ, 1),
            pltpu.roll(mid, NZ, 1),
            jnp.where(depth == NZ - 1, 0.0, pltpu.roll(mid, lanes - 1, 1)),
            jnp.where(depth == 0, 0.0, pltpu.roll(mid, 1, 1)),
        ]

    total = jnp.zeros((inner, lanes), F32)
    for side, (there, mark) in enumerate(zip(views(cond), views(label))):
        conduct = face(center, there)
        total = total + conduct
        weight[side] = free * conduct
        nbr[side] = mark
        couple[side] = jnp.where(mark == 0, free * conduct, 0.0)
    mean = jnp.sum(free * total, keepdims=True) / jnp.maximum(jnp.sum(free, keepdims=True), 1.0)
    unit, inverse = power_of_two(1.5 * mean)
    unit_ref[...] = jnp.broadcast_to(unit, unit_ref.shape)
    diag[...] = free * (total * inverse - 1.0)
    for side in range(6):
        couple[side] = couple[side] * inverse

    step = 32
    cluster = lax.broadcasted_iota(jnp.int32, (step, lanes), 0)
    powers = (v0, v1, v2)

    def store(order, row, cut, value):
        if order < ITERS:
            powers[order][row, cut, :] = value
        at = row - (ITERS - order)
        if 0 <= at < rows:
            fields_ref[order * K + cut.start:order * K + cut.stop, at * own:(at + 1) * own] = (
                value[:, 0:own]
            )

    def fill(row):
        for part in range(0, K, step):
            ids = (cluster + (part + 1)).astype(F32)
            acc = jnp.zeros((step, lanes), F32)
            for side in range(6):
                hit = nbr[side, row:row + 1, :] == ids
                acc = acc + jnp.where(hit, weight[side, row:row + 1, :], 0.0)
            store(0, row, slice(part, part + step), acc)

    def power(order, row):
        source = powers[order - 1]
        at = row + order
        for part in range(0, K, step):
            cut = slice(part, part + step)
            mid = source[row + 1, cut, :]
            acc = diag[at:at + 1, :] * mid
            acc = acc - couple[0, at:at + 1, :] * source[row + 2, cut, :]
            acc = acc - couple[1, at:at + 1, :] * source[row, cut, :]
            acc = acc - couple[2, at:at + 1, :] * pltpu.roll(mid, lanes - NZ, 1)
            acc = acc - couple[3, at:at + 1, :] * pltpu.roll(mid, NZ, 1)
            acc = acc - couple[4, at:at + 1, :] * pltpu.roll(mid, lanes - 1, 1)
            acc = acc - couple[5, at:at + 1, :] * pltpu.roll(mid, 1, 1)
            store(order, row, cut, acc)

    for front in range(inner):
        fill(front)
        for order in range(1, ITERS + 1):
            if front >= 2 * order:
                power(order, front - 2 * order)
        at = front - 2 * ITERS
        if at >= 0:
            part = lax.dot_general(
                fields_ref[0:ITERS * K, at * own:(at + 1) * own],
                fields_ref[:, at * own:(at + 1) * own],
                (((1,), (1,)), ((), ())), precision=HIGH, preferred_element_type=F32,
            )
            gram[...] = part if at == 0 else gram[...] + part
    pack(gram, unit, keep_ref, send_ref)


def power_of_two(value):
    unit = jnp.full(value.shape, 2.0 ** -4, F32)
    inverse = jnp.full(value.shape, 2.0 ** 4, F32)
    for exponent in range(-4, 9):
        more = value > 2.0 ** (exponent + 0.5)
        unit = jnp.where(more, 2.0 ** (exponent + 1), unit)
        inverse = jnp.where(more, 2.0 ** (-exponent - 1), inverse)
    return unit, inverse


def pair_add(pair, value):
    high, low = pair
    total = high + value
    back = total - high
    return total, low + ((high - (total - back)) + (value - back))


EXPANSION = []
for k in range(2 * ITERS):
    first, second = k // 2, k - k // 2
    terms = {}
    for a in range(first + 1):
        for b in range(second + 1):
            terms[a, b] = math.comb(first, a) * math.comb(second, b)
    EXPANSION.append(sorted(terms.items(), reverse=True))


def pack(gram, unit, keep_ref, send_ref):
    row = lax.broadcasted_iota(jnp.int32, (K, K), 0)
    col = lax.broadcasted_iota(jnp.int32, (K, K), 1)
    blocks = {}
    lines = {}
    for k in range(2 * ITERS):
        for at, _ in EXPANSION[k]:
            if at not in blocks:
                a, b = at
                blocks[at] = gram[a * K:(a + 1) * K, b * K:(b + 1) * K]
                lines[at] = jnp.sum(jnp.where(row == col, blocks[at], 0.0), axis=0, keepdims=True)
    scale = jnp.ones_like(unit)
    moments, highs, lows = [], [], []
    for k in range(2 * ITERS):
        moment = jnp.zeros((K, K), F32)
        pair = (jnp.zeros((1, K), F32), jnp.zeros((1, K), F32))
        for at, factor in EXPANSION[k]:
            moment = moment + float(factor) * blocks[at]
            bit = 1
            while bit <= factor:
                if factor & bit:
                    pair = pair_add(pair, float(bit) * lines[at])
                bit *= 2
        moments.append(moment * scale)
        highs.append(pair[0] * scale)
        lows.append(pair[1] * scale)
        scale = scale * unit
    packs = [
        jnp.where(row > col, moments[i], jnp.where(row < col, moments[i + 1], 0.0))
        for i in range(0, 2 * ITERS, 2)
    ]
    first = jnp.concatenate(packs[:2], axis=1)
    second = jnp.concatenate([packs[2][:K // 2], packs[2][K // 2:]], axis=1)
    gap = jnp.zeros((1, K), F32)
    rest = jnp.zeros((2, 2 * K), F32)

    def tail(at):
        return [
            jnp.concatenate([highs[at], highs[at + 1]], axis=1),
            jnp.concatenate([highs[at + 2], gap], axis=1),
            rest,
            jnp.concatenate([lows[at], lows[at + 1]], axis=1),
            jnp.concatenate([lows[at + 2], gap], axis=1),
            rest,
        ]

    top = jnp.concatenate([first[:BODY]] + tail(0), axis=0)
    bottom = jnp.concatenate([first[BODY:], second] + tail(3), axis=0)
    low_core = lax.rem(lax.axis_index("gx"), 2) == 0
    keep_ref[...] = jnp.where(low_core, top, bottom)
    send_ref[...] = jnp.where(low_core, bottom, top)


def unpack(top, bottom):
    row = lax.broadcasted_iota(jnp.int32, (K, K), 0)
    col = lax.broadcasted_iota(jnp.int32, (K, K), 1)
    first = jnp.concatenate([top[:BODY], bottom[:K - BODY]], axis=0)
    second = bottom[K - BODY:BODY]
    packs = [first[:, :K], first[:, K:], jnp.concatenate([second[:, :K], second[:, K:]], axis=0)]
    moments, pairs = [], []
    for value in packs:
        flip = value.T
        moments.append(jnp.where(row > col, value, flip))
        moments.append(jnp.where(row < col, value, flip))
    for half in (top, bottom):
        for at in ((0, 0), (0, K), (1, 0)):
            pairs.append(tuple(
                half[BODY + shift + at[0]:BODY + shift + at[0] + 1, at[1]:at[1] + K]
                for shift in (0, TAIL // 2)
            ))
    return moments, pairs


def krylov(up, here, down):
    rows, lanes = here.shape[1:]
    own = lanes - 2 * DEEP * NZ
    tall = rows + 2 * DEEP
    inner = tall - 2
    return pl.pallas_call(
        krylov_kernel,
        out_shape=(
            jax.ShapeDtypeStruct(((ITERS + 1) * K, rows * own), F32),
            jax.ShapeDtypeStruct((BODY + TAIL, 2 * K), F32),
            jax.ShapeDtypeStruct((BODY + TAIL, 2 * K), F32),
            jax.ShapeDtypeStruct((8, 2 * K), F32),
        ),
        in_specs=[pl.BlockSpec(memory_space=pltpu.VMEM)] * 3,
        out_specs=[pl.BlockSpec(memory_space=pltpu.VMEM)] * 4,
        scratch_shapes=[
            pltpu.VMEM((tall, lanes), F32),
            pltpu.VMEM((tall, lanes), F32),
            pltpu.VMEM((6, inner, lanes), F32),
            pltpu.VMEM((6, inner, lanes), F32),
            pltpu.VMEM((6, inner, lanes), F32),
            pltpu.VMEM((inner, lanes), F32),
            pltpu.VMEM((inner, K, lanes), F32),
            pltpu.VMEM((inner - 2, K, lanes), F32),
            pltpu.VMEM((inner - 4, K, lanes), F32),
            pltpu.VMEM((ITERS * K, (ITERS + 1) * K), F32),
        ],
        compiler_params=pltpu.CompilerParams(vmem_limit_bytes=40 * 1024 * 1024),
    )(up, here, down)


def splat(value, j):
    return jnp.broadcast_to(value[:, j:j + 1], (value.shape[0], 128))


def line(value, j):
    return jnp.broadcast_to(value[j:j + 1], (PANEL, 128))


def gauss_jordan(work, start, stop):
    total = work.shape[1]
    sub = lax.broadcasted_iota(jnp.int32, (PANEL, 128), 0)
    small = None
    for at in range(start, stop, PANEL):
        base = at // 128 * 128
        column = work[start:stop, base:base + 128]
        spread = [splat(column, at - base + j) for j in range(PANEL)]
        if small is None:
            small = [value[at - start:at - start + PANEL] for value in spread]
        after = at + PANEL
        ahead, below = [], []
        if after < stop:
            base = after // 128 * 128
            strip = work[at:after, base:base + 128]
            ahead = [splat(strip, after - base + j) for j in range(PANEL)]
            strip = work[after:after + PANEL, base:base + 128]
            below = [splat(strip, after - base + j) for j in range(PANEL)]
        tiles = [t for t in range(0, total, 128) if t + 128 > after]
        values = small + ahead + [work[at:after, t:t + 128] for t in tiles]
        scale = jnp.ones((PANEL, 128), F32)
        for j in range(PANEL):
            inverse = 1.0 / line(values[j], j)
            scale = jnp.where(sub == j, inverse, scale)
            factor = jnp.where(sub == j, 0.0, values[j]) * inverse
            for i in range(j + 1, len(values)):
                values[i] = values[i] - factor * line(values[i], j)
        values = [value * scale for value in values]
        ahead = values[PANEL:PANEL + len(ahead)]
        rows = values[PANEL + len(ahead):]
        if after < stop:
            small = []
            for value, column in zip(below, ahead):
                for j in range(PANEL):
                    value = value - spread[j][after - start:after - start + PANEL] * line(column, j)
                small.append(value)
        for row, t in zip(rows, tiles):
            for first, last in ((after, min(after + PANEL, stop)), (after + PANEL, stop), (start, at)):
                if first >= last:
                    continue
                acc = work[first:last, t:t + 128]
                for j in range(PANEL):
                    acc = acc - spread[j][first - start:last - start] * row[j:j + 1]
                work[first:last, t:t + 128] = acc
            work[at:after, t:t + 128] = row


def solve(work, size):
    total = work.shape[1]
    for start in range(0, size, K):
        stop = start + K
        gauss_jordan(work, start, stop)
        if stop < size:
            base = stop // 128 * 128
            work[stop:size, base:total] = work[stop:size, base:total] - jnp.dot(
                work[stop:size, start:stop], work[start:stop, base:total],
                precision=HIGH, preferred_element_type=F32,
            )
    for start in range(size - 2 * K, -1, -K):
        stop = start + K
        work[start:stop, size:total] = work[start:stop, size:total] - jnp.dot(
            work[start:stop, stop:size], work[stop:size, size:total],
            precision=HIGH, preferred_element_type=F32,
        )


def finish_kernel(
    mine_ref, other_ref, unit_ref, fields_ref, solution_out, residual_out,
    work, coeff, mixed, solution_ref, residual_ref, sems,
):
    rows, cols = solution_ref.shape[:2]
    size = ITERS * K
    low_core = lax.rem(lax.axis_index("gx"), 2) == 0
    mine, other = mine_ref[...], other_ref[...]
    moments, pairs = unpack(
        jnp.where(low_core, mine, other), jnp.where(low_core, other, mine)
    )
    common, inverse = power_of_two(
        jnp.sum(pairs[1][0], keepdims=True) / jnp.sum(pairs[0][0], keepdims=True)
    )
    scale = jnp.ones_like(common)
    for k in range(2 * ITERS):
        moments[k] = moments[k] * scale
        pairs[k] = (pairs[k][0] * scale, pairs[k][1] * scale)
        scale = scale * inverse
    eye = (
        lax.broadcasted_iota(jnp.int32, (K, K), 0) == lax.broadcasted_iota(jnp.int32, (K, K), 1)
    )

    def whole(k):
        return jnp.where(eye, pairs[k][0] + pairs[k][1], moments[k])

    for level in range(2 * ITERS - 1):
        if level < ITERS:
            work[level * K:(level + 1) * K, size:size + K] = whole(0)
        block = whole(1)
        for i in range(ITERS):
            j = level - i
            if 0 <= j < ITERS:
                work[i * K:(i + 1) * K, j * K:(j + 1) * K] = block
        for k in range(len(moments) - 1):
            high, low = pair_add(pairs[k + 1], -pairs[k][0])
            pairs[k] = (high, low - pairs[k][1])
            moments[k] = moments[k + 1] - moments[k]
        moments.pop()
        pairs.pop()
    solve(work, size)
    unit = unit_ref[0:1, 0:1]
    ratio = unit * inverse
    shift = ratio - 1.0
    y0, y1, y2 = (work[i * K:(i + 1) * K, size:size + K] * inverse for i in range(ITERS))
    y0 = y0 + shift * y1 + (shift * shift) * y2
    y1 = ratio * y1 + (2.0 * ratio * shift) * y2
    y2 = (ratio * ratio) * y2
    coeff[0:K, 0:K] = y0
    coeff[K:2 * K, 0:K] = y1
    coeff[2 * K:3 * K, 0:K] = y2
    coeff[3 * K:4 * K, 0:K] = jnp.zeros((K, K), F32)
    coeff[0:K, K:2 * K] = eye.astype(F32) - unit * y0
    coeff[K:2 * K, K:2 * K] = -unit * (y0 + y1)
    coeff[2 * K:3 * K, K:2 * K] = -unit * (y1 + y2)
    coeff[3 * K:4 * K, K:2 * K] = -unit * y2
    own = cols * NZ
    low = lax.broadcasted_iota(jnp.int32, (cols, 2 * K), 1) < K
    copies = []
    for row in range(rows):
        mixed[...] = lax.dot_general(
            coeff[...], fields_ref[:, row * own:(row + 1) * own], (((0,), (0,)), ((), ())),
            precision=HIGH, preferred_element_type=F32,
        ).T
        for z in range(0, NZ, 2):
            even = mixed[pl.ds(z, cols, stride=NZ), :]
            odd = mixed[pl.ds(z + 1, cols, stride=NZ), :]
            solution_ref[row, :, z * K:(z + 2) * K] = jnp.where(low, even, pltpu.roll(odd, K, 1))
            residual_ref[row, :, z * K:(z + 2) * K] = jnp.where(low, pltpu.roll(even, K, 1), odd)
        for side, (here, there) in enumerate(
            ((solution_ref, solution_out), (residual_ref, residual_out))
        ):
            copy = pltpu.make_async_copy(here.at[row], there.at[row], sems.at[side, row])
            copy.start()
            copies.append(copy)
    for copy in copies:
        copy.wait()


def finish(mine, other, unit, fields, rows, cols):
    out = jax.ShapeDtypeStruct((rows, cols, NZ * K), F32)
    return pl.pallas_call(
        finish_kernel,
        out_shape=(out, out),
        in_specs=[pl.BlockSpec(memory_space=pltpu.VMEM)] * 4,
        out_specs=[pl.BlockSpec(memory_space=pl.ANY)] * 2,
        scratch_shapes=[
            pltpu.VMEM((ITERS * K, (ITERS + 1) * K), F32),
            pltpu.VMEM(((ITERS + 1) * K, 2 * K), F32),
            pltpu.VMEM((cols * NZ, 2 * K), F32),
            pltpu.VMEM((rows, cols, NZ * K), F32),
            pltpu.VMEM((rows, cols, NZ * K), F32),
            pltpu.SemaphoreType.DMA((2, rows)),
        ],
        compiler_params=pltpu.CompilerParams(vmem_limit_bytes=40 * 1024 * 1024),
    )(mine, other, unit, fields)


def add_parts(value, *others):
    half = BODY + TAIL // 2
    lost = jnp.zeros_like(value[BODY:half])
    for other in others:
        total = value + other
        old, new, add = value[BODY:half], total[BODY:half], other[BODY:half]
        back = new - old
        lost = lost + ((old - (new - back)) + (add - back))
        value = total
    return jnp.concatenate([value[:half], value[half:] + lost], axis=0)


def flipped(value, axis, *masks):
    count = lax.axis_size(axis)
    return [lax.ppermute(value, axis, [(i, i ^ mask) for i in range(count)]) for mask in masks]


def sum_of_all(value, axis):
    count = lax.axis_size(axis)
    parts = lax.all_to_all(jnp.broadcast_to(value[None], (count,) + value.shape), axis, 0, 0)
    return add_parts(*(parts[i] for i in range(count)))


def from_both(first, last, axis):
    count = lax.axis_size(axis)
    here = lax.axis_index(axis)
    even = lax.rem(here, 2) == 0
    outer = [(i, (((i + 1) ^ 1) - 1) % count) for i in range(count)]
    inner = [(i, i ^ 1) for i in range(count)]
    one = lax.ppermute(jnp.where(even, first, last), axis, outer)
    two = lax.ppermute(jnp.where(even, last, first), axis, inner)
    odd = ~even
    before, after = jnp.where(odd, two, one), jnp.where(odd, one, two)
    return jnp.where(here == 0, 0.0, before), jnp.where(here == count - 1, 0.0, after)


def shards(diffusivity, labels, obstacles):
    rows, cols = diffusivity.shape[:2]
    diffusivity, labels, obstacles = (
        jnp.transpose(value, (0, 2, 1)) for value in (diffusivity, labels, obstacles)
    )
    conductive = diffusivity * (1 - obstacles).astype(F32)
    plane = lax.broadcasted_iota(jnp.int32, (2,) + conductive.shape, 0)
    cells = jnp.where(plane == 0, conductive[None], labels.astype(F32)[None])
    cells = jnp.transpose(lax.optimization_barrier(cells), (0, 1, 3, 2))
    cells = cells.reshape(2, rows, cols * NZ)
    edge = DEEP * NZ
    before, after = from_both(cells[:, :, :edge], cells[:, :, -edge:], "gy")
    here = jnp.concatenate([cells, after, before], axis=2)
    up, down = from_both(here[:, :DEEP], here[:, rows - DEEP:], "gx")
    fields, keep, send, unit = krylov(up, here, down)
    mine = add_parts(keep, *flipped(send, "gx", 1))
    mine = add_parts(mine, *flipped(mine, "gx", 2, 4, 6))
    mine = add_parts(mine, *flipped(mine, "gx", 8))
    mine = sum_of_all(mine, "gy")
    return finish(mine, *flipped(mine, "gx", 1), unit, fields, rows, cols)


def solution(mesh):
    in_specs = (P("gx", "gy", None), P("gx", "gy", None), P("gx", "gy", None))
    out_specs = (P("gx", "gy", None), P("gx", "gy", None))
    return jax.shard_map(shards, mesh=mesh, in_specs=in_specs, out_specs=out_specs, check_vma=False)
```

```python
import math

import jax
import jax.numpy as jnp
from jax import lax
from jax.experimental import pallas as pl
from jax.experimental.pallas import tpu as pltpu
from jax.sharding import PartitionSpec as P

NZ = 16
K = 64
ITERS = 3
DEEP = ITERS + 1

BODY = 3 * K // 4
TAIL = 8
PANEL = 8

HIGH = lax.Precision.HIGHEST
F32 = jnp.float32


def face(here, there):
    product = here * there
    return 2.0 * product / jnp.where(product > 0, here + there, 1.0)


def cells_kernel(
    diffusivity_hbm, labels_hbm, obstacles_hbm, cells_ref,
    diffusivity_ref, labels_ref, obstacles_ref, sems,
):
    copies = [
        pltpu.make_async_copy(there, here, sems.at[i])
        for i, (there, here) in enumerate((
            (obstacles_hbm, obstacles_ref),
            (diffusivity_hbm, diffusivity_ref),
            (labels_hbm, labels_ref),
        ))
    ]
    for copy in copies:
        copy.start()
    for copy in copies:
        copy.wait()
    for row in range(diffusivity_ref.shape[0]):
        clear = obstacles_ref[row] == 0
        cells_ref[0, row] = jnp.where(clear, diffusivity_ref[row], 0.0).T
        cells_ref[1, row] = labels_ref[row].astype(F32).T


def cells_of(diffusivity, labels, obstacles):
    views = [jnp.transpose(value, (0, 2, 1)) for value in (diffusivity, labels, obstacles)]
    return pl.pallas_call(
        cells_kernel,
        out_shape=jax.ShapeDtypeStruct((2,) + diffusivity.shape, F32),
        in_specs=[pl.BlockSpec(memory_space=pltpu.HBM)] * 3,
        out_specs=pl.BlockSpec(memory_space=pltpu.VMEM),
        scratch_shapes=[pltpu.VMEM(view.shape, view.dtype) for view in views]
        + [pltpu.SemaphoreType.DMA((3,))],
    )(*views)


def krylov_kernel(
    up_ref, here_ref, down_ref, fields_ref, keep_ref, send_ref, unit_ref,
    cond, label, couple, weight, nbr, diag, v0, v1, v2, gram,
):
    rows = here_ref.shape[1]
    lanes = here_ref.shape[2]
    own = fields_ref.shape[1] // rows
    tall = rows + 2 * DEEP
    for plane, ref in ((0, cond), (1, label)):
        ref[0:DEEP, :] = up_ref[plane]
        ref[DEEP:DEEP + rows, :] = here_ref[plane]
        ref[DEEP + rows:tall, :] = down_ref[plane]
    inner = tall - 2
    lane = lax.broadcasted_iota(jnp.int32, (inner, lanes), 1)
    depth = lane & (NZ - 1)
    center = cond[1:1 + inner, :]
    free = jnp.where((center > 0) & (label[1:1 + inner, :] == 0), 1.0, 0.0)

    def views(ref):
        mid = ref[1:1 + inner, :]
        return [
            ref[2:2 + inner, :],
            ref[0:inner, :],
            pltpu.roll(mid, lanes - NZ, 1),
            pltpu.roll(mid, NZ, 1),
            jnp.where(depth == NZ - 1, 0.0, pltpu.roll(mid, lanes - 1, 1)),
            jnp.where(depth == 0, 0.0, pltpu.roll(mid, 1, 1)),
        ]

    total = jnp.zeros((inner, lanes), F32)
    for side, (there, mark) in enumerate(zip(views(cond), views(label))):
        conduct = face(center, there)
        total = total + conduct
        weight[side] = free * conduct
        nbr[side] = mark
        couple[side] = jnp.where(mark == 0, free * conduct, 0.0)
    mean = jnp.sum(free * total, keepdims=True) / jnp.maximum(jnp.sum(free, keepdims=True), 1.0)
    unit, inverse = power_of_two(1.5 * mean)
    unit_ref[...] = jnp.broadcast_to(unit, unit_ref.shape)
    diag[...] = free * (total * inverse - 1.0)
    for side in range(6):
        couple[side] = couple[side] * inverse

    step = 32
    cluster = lax.broadcasted_iota(jnp.int32, (step, lanes), 0)
    powers = (v0, v1, v2)

    def store(order, row, cut, value):
        if order < ITERS:
            powers[order][row, cut, :] = value
        at = row - (ITERS - order)
        if 0 <= at < rows:
            fields_ref[order * K + cut.start:order * K + cut.stop, at * own:(at + 1) * own] = (
                value[:, 0:own]
            )

    def fill(row):
        for part in range(0, K, step):
            ids = (cluster + (part + 1)).astype(F32)
            acc = jnp.zeros((step, lanes), F32)
            for side in range(6):
                hit = nbr[side, row:row + 1, :] == ids
                acc = acc + jnp.where(hit, weight[side, row:row + 1, :], 0.0)
            store(0, row, slice(part, part + step), acc)

    def power(order, row):
        source = powers[order - 1]
        at = row + order
        for part in range(0, K, step):
            cut = slice(part, part + step)
            mid = source[row + 1, cut, :]
            acc = diag[at:at + 1, :] * mid
            acc = acc - couple[0, at:at + 1, :] * source[row + 2, cut, :]
            acc = acc - couple[1, at:at + 1, :] * source[row, cut, :]
            acc = acc - couple[2, at:at + 1, :] * pltpu.roll(mid, lanes - NZ, 1)
            acc = acc - couple[3, at:at + 1, :] * pltpu.roll(mid, NZ, 1)
            acc = acc - couple[4, at:at + 1, :] * pltpu.roll(mid, lanes - 1, 1)
            acc = acc - couple[5, at:at + 1, :] * pltpu.roll(mid, 1, 1)
            store(order, row, cut, acc)

    for front in range(inner):
        fill(front)
        for order in range(1, ITERS + 1):
            if front >= 2 * order:
                power(order, front - 2 * order)
        at = front - 2 * ITERS
        if at >= 0:
            part = lax.dot_general(
                fields_ref[0:ITERS * K, at * own:(at + 1) * own],
                fields_ref[:, at * own:(at + 1) * own],
                (((1,), (1,)), ((), ())), precision=HIGH, preferred_element_type=F32,
            )
            gram[...] = part if at == 0 else gram[...] + part
    pack(gram, unit, keep_ref, send_ref)


def power_of_two(value):
    unit = jnp.full(value.shape, 2.0 ** -4, F32)
    inverse = jnp.full(value.shape, 2.0 ** 4, F32)
    for exponent in range(-4, 9):
        more = value > 2.0 ** (exponent + 0.5)
        unit = jnp.where(more, 2.0 ** (exponent + 1), unit)
        inverse = jnp.where(more, 2.0 ** (-exponent - 1), inverse)
    return unit, inverse


def pair_add(pair, value):
    high, low = pair
    total = high + value
    back = total - high
    return total, low + ((high - (total - back)) + (value - back))


EXPANSION = []
for k in range(2 * ITERS):
    first, second = k // 2, k - k // 2
    terms = {}
    for a in range(first + 1):
        for b in range(second + 1):
            terms[a, b] = math.comb(first, a) * math.comb(second, b)
    EXPANSION.append(sorted(terms.items(), reverse=True))


def pack(gram, unit, keep_ref, send_ref):
    row = lax.broadcasted_iota(jnp.int32, (K, K), 0)
    col = lax.broadcasted_iota(jnp.int32, (K, K), 1)
    blocks = {}
    lines = {}
    for k in range(2 * ITERS):
        for at, _ in EXPANSION[k]:
            if at not in blocks:
                a, b = at
                blocks[at] = gram[a * K:(a + 1) * K, b * K:(b + 1) * K]
                lines[at] = jnp.sum(jnp.where(row == col, blocks[at], 0.0), axis=0, keepdims=True)
    scale = jnp.ones_like(unit)
    moments, highs, lows = [], [], []
    for k in range(2 * ITERS):
        moment = jnp.zeros((K, K), F32)
        pair = (jnp.zeros((1, K), F32), jnp.zeros((1, K), F32))
        for at, factor in EXPANSION[k]:
            moment = moment + float(factor) * blocks[at]
            bit = 1
            while bit <= factor:
                if factor & bit:
                    pair = pair_add(pair, float(bit) * lines[at])
                bit *= 2
        moments.append(moment * scale)
        highs.append(pair[0] * scale)
        lows.append(pair[1] * scale)
        scale = scale * unit
    packs = [
        jnp.where(row > col, moments[i], jnp.where(row < col, moments[i + 1], 0.0))
        for i in range(0, 2 * ITERS, 2)
    ]
    first = jnp.concatenate(packs[:2], axis=1)
    second = jnp.concatenate([packs[2][:K // 2], packs[2][K // 2:]], axis=1)
    gap = jnp.zeros((1, K), F32)
    rest = jnp.zeros((2, 2 * K), F32)

    def tail(at):
        return [
            jnp.concatenate([highs[at], highs[at + 1]], axis=1),
            jnp.concatenate([highs[at + 2], gap], axis=1),
            rest,
            jnp.concatenate([lows[at], lows[at + 1]], axis=1),
            jnp.concatenate([lows[at + 2], gap], axis=1),
            rest,
        ]

    top = jnp.concatenate([first[:BODY]] + tail(0), axis=0)
    bottom = jnp.concatenate([first[BODY:], second] + tail(3), axis=0)
    low_core = lax.rem(lax.axis_index("gx"), 2) == 0
    keep_ref[...] = jnp.where(low_core, top, bottom)
    send_ref[...] = jnp.where(low_core, bottom, top)


def unpack(top, bottom):
    row = lax.broadcasted_iota(jnp.int32, (K, K), 0)
    col = lax.broadcasted_iota(jnp.int32, (K, K), 1)
    first = jnp.concatenate([top[:BODY], bottom[:K - BODY]], axis=0)
    second = bottom[K - BODY:BODY]
    packs = [first[:, :K], first[:, K:], jnp.concatenate([second[:, :K], second[:, K:]], axis=0)]
    moments, pairs = [], []
    for value in packs:
        flip = value.T
        moments.append(jnp.where(row > col, value, flip))
        moments.append(jnp.where(row < col, value, flip))
    for half in (top, bottom):
        for at in ((0, 0), (0, K), (1, 0)):
            pairs.append(tuple(
                half[BODY + shift + at[0]:BODY + shift + at[0] + 1, at[1]:at[1] + K]
                for shift in (0, TAIL // 2)
            ))
    return moments, pairs


def krylov(up, here, down):
    rows, lanes = here.shape[1:]
    own = lanes - 2 * DEEP * NZ
    tall = rows + 2 * DEEP
    inner = tall - 2
    return pl.pallas_call(
        krylov_kernel,
        out_shape=(
            jax.ShapeDtypeStruct(((ITERS + 1) * K, rows * own), F32),
            jax.ShapeDtypeStruct((BODY + TAIL, 2 * K), F32),
            jax.ShapeDtypeStruct((BODY + TAIL, 2 * K), F32),
            jax.ShapeDtypeStruct((8, 2 * K), F32),
        ),
        in_specs=[pl.BlockSpec(memory_space=pltpu.VMEM)] * 3,
        out_specs=[pl.BlockSpec(memory_space=pltpu.VMEM)] * 4,
        scratch_shapes=[
            pltpu.VMEM((tall, lanes), F32),
            pltpu.VMEM((tall, lanes), F32),
            pltpu.VMEM((6, inner, lanes), F32),
            pltpu.VMEM((6, inner, lanes), F32),
            pltpu.VMEM((6, inner, lanes), F32),
            pltpu.VMEM((inner, lanes), F32),
            pltpu.VMEM((inner, K, lanes), F32),
            pltpu.VMEM((inner - 2, K, lanes), F32),
            pltpu.VMEM((inner - 4, K, lanes), F32),
            pltpu.VMEM((ITERS * K, (ITERS + 1) * K), F32),
        ],
        compiler_params=pltpu.CompilerParams(vmem_limit_bytes=40 * 1024 * 1024),
    )(up, here, down)


def splat(value, j):
    return jnp.broadcast_to(value[:, j:j + 1], (value.shape[0], 128))


def line(value, j):
    return jnp.broadcast_to(value[j:j + 1], (PANEL, 128))


def gauss_jordan(work, start, stop):
    total = work.shape[1]
    sub = lax.broadcasted_iota(jnp.int32, (PANEL, 128), 0)
    small = None
    for at in range(start, stop, PANEL):
        base = at // 128 * 128
        column = work[start:stop, base:base + 128]
        spread = [splat(column, at - base + j) for j in range(PANEL)]
        if small is None:
            small = [value[at - start:at - start + PANEL] for value in spread]
        after = at + PANEL
        ahead, below = [], []
        if after < stop:
            base = after // 128 * 128
            strip = work[at:after, base:base + 128]
            ahead = [splat(strip, after - base + j) for j in range(PANEL)]
            strip = work[after:after + PANEL, base:base + 128]
            below = [splat(strip, after - base + j) for j in range(PANEL)]
        tiles = [t for t in range(0, total, 128) if t + 128 > after]
        values = small + ahead + [work[at:after, t:t + 128] for t in tiles]
        scale = jnp.ones((PANEL, 128), F32)
        for j in range(PANEL):
            inverse = 1.0 / line(values[j], j)
            scale = jnp.where(sub == j, inverse, scale)
            factor = jnp.where(sub == j, 0.0, values[j]) * inverse
            for i in range(j + 1, len(values)):
                values[i] = values[i] - factor * line(values[i], j)
        values = [value * scale for value in values]
        ahead = values[PANEL:PANEL + len(ahead)]
        rows = values[PANEL + len(ahead):]
        if after < stop:
            small = []
            for value, column in zip(below, ahead):
                for j in range(PANEL):
                    value = value - spread[j][after - start:after - start + PANEL] * line(column, j)
                small.append(value)
        for row, t in zip(rows, tiles):
            for first, last in ((after, min(after + PANEL, stop)), (after + PANEL, stop), (start, at)):
                if first >= last:
                    continue
                acc = work[first:last, t:t + 128]
                for j in range(PANEL):
                    acc = acc - spread[j][first - start:last - start] * row[j:j + 1]
                work[first:last, t:t + 128] = acc
            work[at:after, t:t + 128] = row


def solve(work, size):
    total = work.shape[1]
    for start in range(0, size, K):
        stop = start + K
        gauss_jordan(work, start, stop)
        if stop < size:
            base = stop // 128 * 128
            work[stop:size, base:total] = work[stop:size, base:total] - jnp.dot(
                work[stop:size, start:stop], work[start:stop, base:total],
                precision=HIGH, preferred_element_type=F32,
            )
    for start in range(size - 2 * K, -1, -K):
        stop = start + K
        work[start:stop, size:total] = work[start:stop, size:total] - jnp.dot(
            work[start:stop, stop:size], work[stop:size, size:total],
            precision=HIGH, preferred_element_type=F32,
        )


def finish_kernel(
    mine_ref, other_ref, unit_ref, fields_ref, solution_out, residual_out,
    work, coeff, mixed, solution_ref, residual_ref, sems,
):
    rows, cols = solution_ref.shape[:2]
    size = ITERS * K
    low_core = lax.rem(lax.axis_index("gx"), 2) == 0
    mine, other = mine_ref[...], other_ref[...]
    moments, pairs = unpack(
        jnp.where(low_core, mine, other), jnp.where(low_core, other, mine)
    )
    common, inverse = power_of_two(
        jnp.sum(pairs[1][0], keepdims=True) / jnp.sum(pairs[0][0], keepdims=True)
    )
    scale = jnp.ones_like(common)
    for k in range(2 * ITERS):
        moments[k] = moments[k] * scale
        pairs[k] = (pairs[k][0] * scale, pairs[k][1] * scale)
        scale = scale * inverse
    eye = (
        lax.broadcasted_iota(jnp.int32, (K, K), 0) == lax.broadcasted_iota(jnp.int32, (K, K), 1)
    )

    def whole(k):
        return jnp.where(eye, pairs[k][0] + pairs[k][1], moments[k])

    for level in range(2 * ITERS - 1):
        if level < ITERS:
            work[level * K:(level + 1) * K, size:size + K] = whole(0)
        block = whole(1)
        for i in range(ITERS):
            j = level - i
            if 0 <= j < ITERS:
                work[i * K:(i + 1) * K, j * K:(j + 1) * K] = block
        for k in range(len(moments) - 1):
            high, low = pair_add(pairs[k + 1], -pairs[k][0])
            pairs[k] = (high, low - pairs[k][1])
            moments[k] = moments[k + 1] - moments[k]
        moments.pop()
        pairs.pop()
    solve(work, size)
    unit = unit_ref[0:1, 0:1]
    ratio = unit * inverse
    shift = ratio - 1.0
    y0, y1, y2 = (work[i * K:(i + 1) * K, size:size + K] * inverse for i in range(ITERS))
    y0 = y0 + shift * y1 + (shift * shift) * y2
    y1 = ratio * y1 + (2.0 * ratio * shift) * y2
    y2 = (ratio * ratio) * y2
    coeff[0:K, 0:K] = y0
    coeff[K:2 * K, 0:K] = y1
    coeff[2 * K:3 * K, 0:K] = y2
    coeff[3 * K:4 * K, 0:K] = jnp.zeros((K, K), F32)
    coeff[0:K, K:2 * K] = eye.astype(F32) - unit * y0
    coeff[K:2 * K, K:2 * K] = -unit * (y0 + y1)
    coeff[2 * K:3 * K, K:2 * K] = -unit * (y1 + y2)
    coeff[3 * K:4 * K, K:2 * K] = -unit * y2
    own = cols * NZ
    low = lax.broadcasted_iota(jnp.int32, (cols, 2 * K), 1) < K
    copies = []
    for row in range(rows):
        mixed[...] = lax.dot_general(
            coeff[...], fields_ref[:, row * own:(row + 1) * own], (((0,), (0,)), ((), ())),
            precision=HIGH, preferred_element_type=F32,
        ).T
        for z in range(0, NZ, 2):
            even = mixed[pl.ds(z, cols, stride=NZ), :]
            odd = mixed[pl.ds(z + 1, cols, stride=NZ), :]
            solution_ref[row, :, z * K:(z + 2) * K] = jnp.where(low, even, pltpu.roll(odd, K, 1))
            residual_ref[row, :, z * K:(z + 2) * K] = jnp.where(low, pltpu.roll(even, K, 1), odd)
        for side, (here, there) in enumerate(
            ((solution_ref, solution_out), (residual_ref, residual_out))
        ):
            copy = pltpu.make_async_copy(here.at[row], there.at[row], sems.at[side, row])
            copy.start()
            copies.append(copy)
    for copy in copies:
        copy.wait()


def finish(mine, other, unit, fields, rows, cols):
    out = jax.ShapeDtypeStruct((rows, cols, NZ * K), F32)
    return pl.pallas_call(
        finish_kernel,
        out_shape=(out, out),
        in_specs=[pl.BlockSpec(memory_space=pltpu.VMEM)] * 4,
        out_specs=[pl.BlockSpec(memory_space=pl.ANY)] * 2,
        scratch_shapes=[
            pltpu.VMEM((ITERS * K, (ITERS + 1) * K), F32),
            pltpu.VMEM(((ITERS + 1) * K, 2 * K), F32),
            pltpu.VMEM((cols * NZ, 2 * K), F32),
            pltpu.VMEM((rows, cols, NZ * K), F32),
            pltpu.VMEM((rows, cols, NZ * K), F32),
            pltpu.SemaphoreType.DMA((2, rows)),
        ],
        compiler_params=pltpu.CompilerParams(vmem_limit_bytes=40 * 1024 * 1024),
    )(mine, other, unit, fields)


def add_parts(value, *others):
    half = BODY + TAIL // 2
    lost = jnp.zeros_like(value[BODY:half])
    for other in others:
        total = value + other
        old, new, add = value[BODY:half], total[BODY:half], other[BODY:half]
        back = new - old
        lost = lost + ((old - (new - back)) + (add - back))
        value = total
    return jnp.concatenate([value[:half], value[half:] + lost], axis=0)


def flipped(value, axis, *masks):
    count = lax.axis_size(axis)
    return [lax.ppermute(value, axis, [(i, i ^ mask) for i in range(count)]) for mask in masks]


def sum_of_all(value, axis):
    count = lax.axis_size(axis)
    parts = lax.all_to_all(jnp.broadcast_to(value[None], (count,) + value.shape), axis, 0, 0)
    return add_parts(*(parts[i] for i in range(count)))


def from_both(first, last, axis):
    count = lax.axis_size(axis)
    here = lax.axis_index(axis)
    even = lax.rem(here, 2) == 0
    outer = [(i, (((i + 1) ^ 1) - 1) % count) for i in range(count)]
    inner = [(i, i ^ 1) for i in range(count)]
    one = lax.ppermute(jnp.where(even, first, last), axis, outer)
    two = lax.ppermute(jnp.where(even, last, first), axis, inner)
    odd = ~even
    before, after = jnp.where(odd, two, one), jnp.where(odd, one, two)
    return jnp.where(here == 0, 0.0, before), jnp.where(here == count - 1, 0.0, after)


def shards(diffusivity, labels, obstacles):
    rows, cols = diffusivity.shape[:2]
    cells = cells_of(diffusivity, labels, obstacles).reshape(2, rows, cols * NZ)
    edge = DEEP * NZ
    before, after = from_both(cells[:, :, :edge], cells[:, :, -edge:], "gy")
    here = jnp.concatenate([cells, after, before], axis=2)
    up, down = from_both(here[:, :DEEP], here[:, rows - DEEP:], "gx")
    fields, keep, send, unit = krylov(up, here, down)
    mine = add_parts(keep, *flipped(send, "gx", 1))
    mine = add_parts(mine, *flipped(mine, "gx", 2, 4, 6))
    mine = add_parts(mine, *flipped(mine, "gx", 12))
    mine = sum_of_all(mine, "gy")
    return finish(mine, *flipped(mine, "gx", 1), unit, fields, rows, cols)


def solution(mesh):
    in_specs = (P("gx", "gy", None), P("gx", "gy", None), P("gx", "gy", None))
    out_specs = (P("gx", "gy", None), P("gx", "gy", None))
    return jax.shard_map(shards, mesh=mesh, in_specs=in_specs, out_specs=out_specs, check_vma=False)
```

```python
import math

import jax
import jax.numpy as jnp
from jax import lax
from jax.experimental import pallas as pl
from jax.experimental.pallas import tpu as pltpu
from jax.sharding import PartitionSpec as P

NZ = 16
K = 64
ITERS = 3
DEEP = ITERS + 1

BODY = 3 * K // 4
TAIL = 8
PANEL = 8

HIGH = lax.Precision.HIGHEST
F32 = jnp.float32


def face(here, there):
    product = here * there
    return 2.0 * product / jnp.where(product > 0, here + there, 1.0)


def cells_kernel(
    diffusivity_hbm, labels_hbm, obstacles_hbm, cells_ref,
    diffusivity_ref, labels_ref, obstacles_ref, sems,
):
    copies = [
        pltpu.make_async_copy(there, here, sems.at[i])
        for i, (there, here) in enumerate((
            (obstacles_hbm, obstacles_ref),
            (diffusivity_hbm, diffusivity_ref),
            (labels_hbm, labels_ref),
        ))
    ]
    for copy in copies:
        copy.start()
    for copy in copies:
        copy.wait()
    for row in range(diffusivity_ref.shape[0]):
        clear = obstacles_ref[row] == 0
        cells_ref[0, row] = jnp.where(clear, diffusivity_ref[row], 0.0).T
        cells_ref[1, row] = labels_ref[row].astype(F32).T


def cells_of(diffusivity, labels, obstacles):
    views = [jnp.transpose(value, (0, 2, 1)) for value in (diffusivity, labels, obstacles)]
    return pl.pallas_call(
        cells_kernel,
        out_shape=jax.ShapeDtypeStruct((2,) + diffusivity.shape, F32),
        in_specs=[pl.BlockSpec(memory_space=pltpu.HBM)] * 3,
        out_specs=pl.BlockSpec(memory_space=pltpu.VMEM),
        scratch_shapes=[pltpu.VMEM(view.shape, view.dtype) for view in views]
        + [pltpu.SemaphoreType.DMA((3,))],
        compiler_params=pltpu.CompilerParams(vmem_limit_bytes=2 * 1024 * 1024),
    )(*views)


def krylov_kernel(
    up_ref, here_ref, down_ref, fields_ref, keep_ref, send_ref, unit_ref,
    cond, label, couple, weight, nbr, diag, v0, v1, v2, gram,
):
    rows = here_ref.shape[1]
    lanes = here_ref.shape[2]
    own = fields_ref.shape[1] // rows
    tall = rows + 2 * DEEP
    for plane, ref in ((0, cond), (1, label)):
        ref[0:DEEP, :] = up_ref[plane]
        ref[DEEP:DEEP + rows, :] = here_ref[plane]
        ref[DEEP + rows:tall, :] = down_ref[plane]
    inner = tall - 2
    lane = lax.broadcasted_iota(jnp.int32, (inner, lanes), 1)
    depth = lane & (NZ - 1)
    center = cond[1:1 + inner, :]
    free = jnp.where((center > 0) & (label[1:1 + inner, :] == 0), 1.0, 0.0)

    def views(ref):
        mid = ref[1:1 + inner, :]
        return [
            ref[2:2 + inner, :],
            ref[0:inner, :],
            pltpu.roll(mid, lanes - NZ, 1),
            pltpu.roll(mid, NZ, 1),
            jnp.where(depth == NZ - 1, 0.0, pltpu.roll(mid, lanes - 1, 1)),
            jnp.where(depth == 0, 0.0, pltpu.roll(mid, 1, 1)),
        ]

    total = jnp.zeros((inner, lanes), F32)
    for side, (there, mark) in enumerate(zip(views(cond), views(label))):
        conduct = face(center, there)
        total = total + conduct
        weight[side] = free * conduct
        nbr[side] = mark
        couple[side] = jnp.where(mark == 0, free * conduct, 0.0)
    mean = jnp.sum(free * total, keepdims=True) / jnp.maximum(jnp.sum(free, keepdims=True), 1.0)
    unit, inverse = power_of_two(1.5 * mean)
    unit_ref[...] = jnp.broadcast_to(unit, unit_ref.shape)
    diag[...] = free * (total * inverse - 1.0)
    for side in range(6):
        couple[side] = couple[side] * inverse

    step = 32
    cluster = lax.broadcasted_iota(jnp.int32, (step, lanes), 0)
    powers = (v0, v1, v2)

    def store(order, row, cut, value):
        if order < ITERS:
            powers[order][row, cut, :] = value
        at = row - (ITERS - order)
        if 0 <= at < rows:
            fields_ref[order * K + cut.start:order * K + cut.stop, at * own:(at + 1) * own] = (
                value[:, 0:own]
            )

    def fill(row):
        for part in range(0, K, step):
            ids = (cluster + (part + 1)).astype(F32)
            acc = jnp.zeros((step, lanes), F32)
            for side in range(6):
                hit = nbr[side, row:row + 1, :] == ids
                acc = acc + jnp.where(hit, weight[side, row:row + 1, :], 0.0)
            store(0, row, slice(part, part + step), acc)

    def power(order, row):
        source = powers[order - 1]
        at = row + order
        for part in range(0, K, step):
            cut = slice(part, part + step)
            mid = source[row + 1, cut, :]
            acc = diag[at:at + 1, :] * mid
            acc = acc - couple[0, at:at + 1, :] * source[row + 2, cut, :]
            acc = acc - couple[1, at:at + 1, :] * source[row, cut, :]
            acc = acc - couple[2, at:at + 1, :] * pltpu.roll(mid, lanes - NZ, 1)
            acc = acc - couple[3, at:at + 1, :] * pltpu.roll(mid, NZ, 1)
            acc = acc - couple[4, at:at + 1, :] * pltpu.roll(mid, lanes - 1, 1)
            acc = acc - couple[5, at:at + 1, :] * pltpu.roll(mid, 1, 1)
            store(order, row, cut, acc)

    for front in range(inner):
        fill(front)
        for order in range(1, ITERS + 1):
            if front >= 2 * order:
                power(order, front - 2 * order)
        at = front - 2 * ITERS
        if at >= 0:
            part = lax.dot_general(
                fields_ref[0:ITERS * K, at * own:(at + 1) * own],
                fields_ref[:, at * own:(at + 1) * own],
                (((1,), (1,)), ((), ())), precision=HIGH, preferred_element_type=F32,
            )
            gram[...] = part if at == 0 else gram[...] + part
    pack(gram, unit, keep_ref, send_ref)


def power_of_two(value):
    unit = jnp.full(value.shape, 2.0 ** -4, F32)
    inverse = jnp.full(value.shape, 2.0 ** 4, F32)
    for exponent in range(-4, 9):
        more = value > 2.0 ** (exponent + 0.5)
        unit = jnp.where(more, 2.0 ** (exponent + 1), unit)
        inverse = jnp.where(more, 2.0 ** (-exponent - 1), inverse)
    return unit, inverse


def pair_add(pair, value):
    high, low = pair
    total = high + value
    back = total - high
    return total, low + ((high - (total - back)) + (value - back))


EXPANSION = []
for k in range(2 * ITERS):
    first, second = k // 2, k - k // 2
    terms = {}
    for a in range(first + 1):
        for b in range(second + 1):
            terms[a, b] = math.comb(first, a) * math.comb(second, b)
    EXPANSION.append(sorted(terms.items(), reverse=True))


def pack(gram, unit, keep_ref, send_ref):
    row = lax.broadcasted_iota(jnp.int32, (K, K), 0)
    col = lax.broadcasted_iota(jnp.int32, (K, K), 1)
    blocks = {}
    lines = {}
    for k in range(2 * ITERS):
        for at, _ in EXPANSION[k]:
            if at not in blocks:
                a, b = at
                blocks[at] = gram[a * K:(a + 1) * K, b * K:(b + 1) * K]
                lines[at] = jnp.sum(jnp.where(row == col, blocks[at], 0.0), axis=0, keepdims=True)
    scale = jnp.ones_like(unit)
    moments, highs, lows = [], [], []
    for k in range(2 * ITERS):
        moment = jnp.zeros((K, K), F32)
        pair = (jnp.zeros((1, K), F32), jnp.zeros((1, K), F32))
        for at, factor in EXPANSION[k]:
            moment = moment + float(factor) * blocks[at]
            bit = 1
            while bit <= factor:
                if factor & bit:
                    pair = pair_add(pair, float(bit) * lines[at])
                bit *= 2
        moments.append(moment * scale)
        highs.append(pair[0] * scale)
        lows.append(pair[1] * scale)
        scale = scale * unit
    packs = [
        jnp.where(row > col, moments[i], jnp.where(row < col, moments[i + 1], 0.0))
        for i in range(0, 2 * ITERS, 2)
    ]
    first = jnp.concatenate(packs[:2], axis=1)
    second = jnp.concatenate([packs[2][:K // 2], packs[2][K // 2:]], axis=1)
    gap = jnp.zeros((1, K), F32)
    rest = jnp.zeros((2, 2 * K), F32)

    def tail(at):
        return [
            jnp.concatenate([highs[at], highs[at + 1]], axis=1),
            jnp.concatenate([highs[at + 2], gap], axis=1),
            rest,
            jnp.concatenate([lows[at], lows[at + 1]], axis=1),
            jnp.concatenate([lows[at + 2], gap], axis=1),
            rest,
        ]

    top = jnp.concatenate([first[:BODY]] + tail(0), axis=0)
    bottom = jnp.concatenate([first[BODY:], second] + tail(3), axis=0)
    low_core = lax.rem(lax.axis_index("gx"), 2) == 0
    keep_ref[...] = jnp.where(low_core, top, bottom)
    send_ref[...] = jnp.where(low_core, bottom, top)


def unpack(top, bottom):
    row = lax.broadcasted_iota(jnp.int32, (K, K), 0)
    col = lax.broadcasted_iota(jnp.int32, (K, K), 1)
    first = jnp.concatenate([top[:BODY], bottom[:K - BODY]], axis=0)
    second = bottom[K - BODY:BODY]
    packs = [first[:, :K], first[:, K:], jnp.concatenate([second[:, :K], second[:, K:]], axis=0)]
    moments, pairs = [], []
    for value in packs:
        flip = value.T
        moments.append(jnp.where(row > col, value, flip))
        moments.append(jnp.where(row < col, value, flip))
    for half in (top, bottom):
        for at in ((0, 0), (0, K), (1, 0)):
            pairs.append(tuple(
                half[BODY + shift + at[0]:BODY + shift + at[0] + 1, at[1]:at[1] + K]
                for shift in (0, TAIL // 2)
            ))
    return moments, pairs


def krylov(up, here, down):
    rows, lanes = here.shape[1:]
    own = lanes - 2 * DEEP * NZ
    tall = rows + 2 * DEEP
    inner = tall - 2
    return pl.pallas_call(
        krylov_kernel,
        out_shape=(
            jax.ShapeDtypeStruct(((ITERS + 1) * K, rows * own), F32),
            jax.ShapeDtypeStruct((BODY + TAIL, 2 * K), F32),
            jax.ShapeDtypeStruct((BODY + TAIL, 2 * K), F32),
            jax.ShapeDtypeStruct((8, 2 * K), F32),
        ),
        in_specs=[pl.BlockSpec(memory_space=pltpu.VMEM)] * 3,
        out_specs=[pl.BlockSpec(memory_space=pltpu.VMEM)] * 4,
        scratch_shapes=[
            pltpu.VMEM((tall, lanes), F32),
            pltpu.VMEM((tall, lanes), F32),
            pltpu.VMEM((6, inner, lanes), F32),
            pltpu.VMEM((6, inner, lanes), F32),
            pltpu.VMEM((6, inner, lanes), F32),
            pltpu.VMEM((inner, lanes), F32),
            pltpu.VMEM((inner, K, lanes), F32),
            pltpu.VMEM((inner - 2, K, lanes), F32),
            pltpu.VMEM((inner - 4, K, lanes), F32),
            pltpu.VMEM((ITERS * K, (ITERS + 1) * K), F32),
        ],
        compiler_params=pltpu.CompilerParams(vmem_limit_bytes=40 * 1024 * 1024),
    )(up, here, down)


def splat(value, j):
    return jnp.broadcast_to(value[:, j:j + 1], (value.shape[0], 128))


def line(value, j):
    return jnp.broadcast_to(value[j:j + 1], (PANEL, 128))


def gauss_jordan(work, start, stop):
    total = work.shape[1]
    sub = lax.broadcasted_iota(jnp.int32, (PANEL, 128), 0)
    small = None
    for at in range(start, stop, PANEL):
        base = at // 128 * 128
        column = work[start:stop, base:base + 128]
        spread = [splat(column, at - base + j) for j in range(PANEL)]
        if small is None:
            small = [value[at - start:at - start + PANEL] for value in spread]
        after = at + PANEL
        ahead, below = [], []
        if after < stop:
            base = after // 128 * 128
            strip = work[at:after, base:base + 128]
            ahead = [splat(strip, after - base + j) for j in range(PANEL)]
            strip = work[after:after + PANEL, base:base + 128]
            below = [splat(strip, after - base + j) for j in range(PANEL)]
        tiles = [t for t in range(0, total, 128) if t + 128 > after]
        values = small + ahead + [work[at:after, t:t + 128] for t in tiles]
        scale = jnp.ones((PANEL, 128), F32)
        for j in range(PANEL):
            inverse = 1.0 / line(values[j], j)
            scale = jnp.where(sub == j, inverse, scale)
            factor = jnp.where(sub == j, 0.0, values[j]) * inverse
            for i in range(j + 1, len(values)):
                values[i] = values[i] - factor * line(values[i], j)
        values = [value * scale for value in values]
        ahead = values[PANEL:PANEL + len(ahead)]
        rows = values[PANEL + len(ahead):]
        if after < stop:
            small = []
            for value, column in zip(below, ahead):
                for j in range(PANEL):
                    value = value - spread[j][after - start:after - start + PANEL] * line(column, j)
                small.append(value)
        for row, t in zip(rows, tiles):
            for first, last in ((after, min(after + PANEL, stop)), (after + PANEL, stop), (start, at)):
                if first >= last:
                    continue
                acc = work[first:last, t:t + 128]
                for j in range(PANEL):
                    acc = acc - spread[j][first - start:last - start] * row[j:j + 1]
                work[first:last, t:t + 128] = acc
            work[at:after, t:t + 128] = row


def solve(work, size):
    total = work.shape[1]
    for start in range(0, size, K):
        stop = start + K
        gauss_jordan(work, start, stop)
        if stop < size:
            base = stop // 128 * 128
            work[stop:size, base:total] = work[stop:size, base:total] - jnp.dot(
                work[stop:size, start:stop], work[start:stop, base:total],
                precision=HIGH, preferred_element_type=F32,
            )
    for start in range(size - 2 * K, -1, -K):
        stop = start + K
        work[start:stop, size:total] = work[start:stop, size:total] - jnp.dot(
            work[start:stop, stop:size], work[stop:size, size:total],
            precision=HIGH, preferred_element_type=F32,
        )


def finish_kernel(
    mine_ref, other_ref, unit_ref, fields_ref, solution_out, residual_out,
    work, coeff, mixed, solution_ref, residual_ref, sems,
):
    rows, cols = solution_ref.shape[:2]
    size = ITERS * K
    low_core = lax.rem(lax.axis_index("gx"), 2) == 0
    mine, other = mine_ref[...], other_ref[...]
    moments, pairs = unpack(
        jnp.where(low_core, mine, other), jnp.where(low_core, other, mine)
    )
    common, inverse = power_of_two(
        jnp.sum(pairs[1][0], keepdims=True) / jnp.sum(pairs[0][0], keepdims=True)
    )
    scale = jnp.ones_like(common)
    for k in range(2 * ITERS):
        moments[k] = moments[k] * scale
        pairs[k] = (pairs[k][0] * scale, pairs[k][1] * scale)
        scale = scale * inverse
    eye = (
        lax.broadcasted_iota(jnp.int32, (K, K), 0) == lax.broadcasted_iota(jnp.int32, (K, K), 1)
    )

    def whole(k):
        return jnp.where(eye, pairs[k][0] + pairs[k][1], moments[k])

    for level in range(2 * ITERS - 1):
        if level < ITERS:
            work[level * K:(level + 1) * K, size:size + K] = whole(0)
        block = whole(1)
        for i in range(ITERS):
            j = level - i
            if 0 <= j < ITERS:
                work[i * K:(i + 1) * K, j * K:(j + 1) * K] = block
        for k in range(len(moments) - 1):
            high, low = pair_add(pairs[k + 1], -pairs[k][0])
            pairs[k] = (high, low - pairs[k][1])
            moments[k] = moments[k + 1] - moments[k]
        moments.pop()
        pairs.pop()
    solve(work, size)
    unit = unit_ref[0:1, 0:1]
    ratio = unit * inverse
    shift = ratio - 1.0
    y0, y1, y2 = (work[i * K:(i + 1) * K, size:size + K] * inverse for i in range(ITERS))
    y0 = y0 + shift * y1 + (shift * shift) * y2
    y1 = ratio * y1 + (2.0 * ratio * shift) * y2
    y2 = (ratio * ratio) * y2
    coeff[0:K, 0:K] = y0
    coeff[K:2 * K, 0:K] = y1
    coeff[2 * K:3 * K, 0:K] = y2
    coeff[3 * K:4 * K, 0:K] = jnp.zeros((K, K), F32)
    coeff[0:K, K:2 * K] = eye.astype(F32) - unit * y0
    coeff[K:2 * K, K:2 * K] = -unit * (y0 + y1)
    coeff[2 * K:3 * K, K:2 * K] = -unit * (y1 + y2)
    coeff[3 * K:4 * K, K:2 * K] = -unit * y2
    own = cols * NZ
    low = lax.broadcasted_iota(jnp.int32, (cols, 2 * K), 1) < K
    copies = []
    for row in range(rows):
        mixed[...] = lax.dot_general(
            coeff[...], fields_ref[:, row * own:(row + 1) * own], (((0,), (0,)), ((), ())),
            precision=HIGH, preferred_element_type=F32,
        ).T
        for z in range(0, NZ, 2):
            even = mixed[pl.ds(z, cols, stride=NZ), :]
            odd = mixed[pl.ds(z + 1, cols, stride=NZ), :]
            solution_ref[row, :, z * K:(z + 2) * K] = jnp.where(low, even, pltpu.roll(odd, K, 1))
            residual_ref[row, :, z * K:(z + 2) * K] = jnp.where(low, pltpu.roll(even, K, 1), odd)
        for side, (here, there) in enumerate(
            ((solution_ref, solution_out), (residual_ref, residual_out))
        ):
            copy = pltpu.make_async_copy(here.at[row], there.at[row], sems.at[side, row])
            copy.start()
            copies.append(copy)
    for copy in copies:
        copy.wait()


def finish(mine, other, unit, fields, rows, cols):
    out = jax.ShapeDtypeStruct((rows, cols, NZ * K), F32)
    return pl.pallas_call(
        finish_kernel,
        out_shape=(out, out),
        in_specs=[pl.BlockSpec(memory_space=pltpu.VMEM)] * 4,
        out_specs=[pl.BlockSpec(memory_space=pl.ANY)] * 2,
        scratch_shapes=[
            pltpu.VMEM((ITERS * K, (ITERS + 1) * K), F32),
            pltpu.VMEM(((ITERS + 1) * K, 2 * K), F32),
            pltpu.VMEM((cols * NZ, 2 * K), F32),
            pltpu.VMEM((rows, cols, NZ * K), F32),
            pltpu.VMEM((rows, cols, NZ * K), F32),
            pltpu.SemaphoreType.DMA((2, rows)),
        ],
        compiler_params=pltpu.CompilerParams(vmem_limit_bytes=40 * 1024 * 1024),
    )(mine, other, unit, fields)


def add_parts(value, *others):
    half = BODY + TAIL // 2
    lost = jnp.zeros_like(value[BODY:half])
    for other in others:
        total = value + other
        old, new, add = value[BODY:half], total[BODY:half], other[BODY:half]
        back = new - old
        lost = lost + ((old - (new - back)) + (add - back))
        value = total
    return jnp.concatenate([value[:half], value[half:] + lost], axis=0)


def flipped(value, axis, *masks):
    count = lax.axis_size(axis)
    return [lax.ppermute(value, axis, [(i, i ^ mask) for i in range(count)]) for mask in masks]


def sum_of_all(value, axis):
    count = lax.axis_size(axis)
    parts = lax.all_to_all(jnp.broadcast_to(value[None], (count,) + value.shape), axis, 0, 0)
    return add_parts(*(parts[i] for i in range(count)))


def from_both(first, last, axis):
    count = lax.axis_size(axis)
    here = lax.axis_index(axis)
    even = lax.rem(here, 2) == 0
    outer = [(i, i if i in (0, count - 1) else ((i + 1) ^ 1) - 1) for i in range(count)]
    inner = [(i, i ^ 1) for i in range(count)]
    one = lax.ppermute(jnp.where(even, first, last), axis, outer)
    two = lax.ppermute(jnp.where(even, last, first), axis, inner)
    odd = ~even
    before, after = jnp.where(odd, two, one), jnp.where(odd, one, two)
    return jnp.where(here == 0, 0.0, before), jnp.where(here == count - 1, 0.0, after)


def shards(diffusivity, labels, obstacles):
    rows, cols = diffusivity.shape[:2]
    cells = cells_of(diffusivity, labels, obstacles).reshape(2, rows, cols * NZ)
    edge = DEEP * NZ
    before, after = from_both(cells[:, :, :edge], cells[:, :, -edge:], "gy")
    here = jnp.concatenate([cells, after, before], axis=2)
    up, down = from_both(here[:, :DEEP], here[:, rows - DEEP:], "gx")
    fields, keep, send, unit = krylov(up, here, down)
    mine = add_parts(keep, *flipped(send, "gx", 1))
    mine = add_parts(mine, *flipped(mine, "gx", 2, 4, 6))
    mine = add_parts(mine, *flipped(mine, "gx", 12))
    mine = sum_of_all(mine, "gy")
    return finish(mine, *flipped(mine, "gx", 1), unit, fields, rows, cols)


def solution(mesh):
    in_specs = (P("gx", "gy", None), P("gx", "gy", None), P("gx", "gy", None))
    out_specs = (P("gx", "gy", None), P("gx", "gy", None))
    return jax.shard_map(shards, mesh=mesh, in_specs=in_specs, out_specs=out_specs, check_vma=False)
```

```python
import math

import jax
import jax.numpy as jnp
from jax import lax
from jax.experimental import pallas as pl
from jax.experimental.pallas import tpu as pltpu
from jax.sharding import PartitionSpec as P

NZ = 16
K = 64
ITERS = 3
DEEP = ITERS + 1

BODY = 3 * K // 4
TAIL = 8
PANEL = 8

HIGH = lax.Precision.HIGHEST
F32 = jnp.float32


def face(here, there):
    product = here * there
    return 2.0 * product / jnp.where(product > 0, here + there, 1.0)


def krylov_kernel(
    up_ref, here_ref, down_ref, fields_ref, keep_ref, send_ref, unit_ref,
    cond, label, couple, weight, nbr, diag, v0, v1, v2, gram,
):
    rows = here_ref.shape[1]
    lanes = here_ref.shape[2]
    own = fields_ref.shape[1] // rows
    tall = rows + 2 * DEEP
    for plane, ref in ((0, cond), (1, label)):
        ref[0:DEEP, :] = up_ref[plane]
        ref[DEEP:DEEP + rows, :] = here_ref[plane]
        ref[DEEP + rows:tall, :] = down_ref[plane]
    inner = tall - 2
    lane = lax.broadcasted_iota(jnp.int32, (inner, lanes), 1)
    depth = lane & (NZ - 1)
    center = cond[1:1 + inner, :]
    free = jnp.where((center > 0) & (label[1:1 + inner, :] == 0), 1.0, 0.0)

    def views(ref):
        mid = ref[1:1 + inner, :]
        return [
            ref[2:2 + inner, :],
            ref[0:inner, :],
            pltpu.roll(mid, lanes - NZ, 1),
            pltpu.roll(mid, NZ, 1),
            jnp.where(depth == NZ - 1, 0.0, pltpu.roll(mid, lanes - 1, 1)),
            jnp.where(depth == 0, 0.0, pltpu.roll(mid, 1, 1)),
        ]

    total = jnp.zeros((inner, lanes), F32)
    for side, (there, mark) in enumerate(zip(views(cond), views(label))):
        conduct = face(center, there)
        total = total + conduct
        weight[side] = free * conduct
        nbr[side] = mark
        couple[side] = jnp.where(mark == 0, free * conduct, 0.0)
    mean = jnp.sum(free * total, keepdims=True) / jnp.maximum(jnp.sum(free, keepdims=True), 1.0)
    unit, inverse = power_of_two(1.5 * mean)
    unit_ref[...] = jnp.broadcast_to(unit, unit_ref.shape)
    diag[...] = free * (total * inverse - 1.0)
    for side in range(6):
        couple[side] = couple[side] * inverse

    step = 32
    cluster = lax.broadcasted_iota(jnp.int32, (step, lanes), 0)
    powers = (v0, v1, v2)

    def store(order, row, cut, value):
        if order < ITERS:
            powers[order][row, cut, :] = value
        at = row - (ITERS - order)
        if 0 <= at < rows:
            fields_ref[order * K + cut.start:order * K + cut.stop, at * own:(at + 1) * own] = (
                value[:, 0:own]
            )

    def fill(row):
        for part in range(0, K, step):
            ids = (cluster + (part + 1)).astype(F32)
            acc = jnp.zeros((step, lanes), F32)
            for side in range(6):
                hit = nbr[side, row:row + 1, :] == ids
                acc = acc + jnp.where(hit, weight[side, row:row + 1, :], 0.0)
            store(0, row, slice(part, part + step), acc)

    def power(order, row):
        source = powers[order - 1]
        at = row + order
        for part in range(0, K, step):
            cut = slice(part, part + step)
            mid = source[row + 1, cut, :]
            acc = diag[at:at + 1, :] * mid
            acc = acc - couple[0, at:at + 1, :] * source[row + 2, cut, :]
            acc = acc - couple[1, at:at + 1, :] * source[row, cut, :]
            acc = acc - couple[2, at:at + 1, :] * pltpu.roll(mid, lanes - NZ, 1)
            acc = acc - couple[3, at:at + 1, :] * pltpu.roll(mid, NZ, 1)
            acc = acc - couple[4, at:at + 1, :] * pltpu.roll(mid, lanes - 1, 1)
            acc = acc - couple[5, at:at + 1, :] * pltpu.roll(mid, 1, 1)
            store(order, row, cut, acc)

    for front in range(inner):
        fill(front)
        for order in range(1, ITERS + 1):
            if front >= 2 * order:
                power(order, front - 2 * order)
        at = front - 2 * ITERS
        if at >= 0:
            part = lax.dot_general(
                fields_ref[0:ITERS * K, at * own:(at + 1) * own],
                fields_ref[:, at * own:(at + 1) * own],
                (((1,), (1,)), ((), ())), precision=HIGH, preferred_element_type=F32,
            )
            gram[...] = part if at == 0 else gram[...] + part
    pack(gram, unit, keep_ref, send_ref)


def power_of_two(value):
    unit = jnp.full(value.shape, 2.0 ** -4, F32)
    inverse = jnp.full(value.shape, 2.0 ** 4, F32)
    for exponent in range(-4, 9):
        more = value > 2.0 ** (exponent + 0.5)
        unit = jnp.where(more, 2.0 ** (exponent + 1), unit)
        inverse = jnp.where(more, 2.0 ** (-exponent - 1), inverse)
    return unit, inverse


def pair_add(pair, value):
    high, low = pair
    total = high + value
    back = total - high
    return total, low + ((high - (total - back)) + (value - back))


EXPANSION = []
for k in range(2 * ITERS):
    first, second = k // 2, k - k // 2
    terms = {}
    for a in range(first + 1):
        for b in range(second + 1):
            terms[a, b] = math.comb(first, a) * math.comb(second, b)
    EXPANSION.append(sorted(terms.items(), reverse=True))


def pack(gram, unit, keep_ref, send_ref):
    row = lax.broadcasted_iota(jnp.int32, (K, K), 0)
    col = lax.broadcasted_iota(jnp.int32, (K, K), 1)
    blocks = {}
    lines = {}
    for k in range(2 * ITERS):
        for at, _ in EXPANSION[k]:
            if at not in blocks:
                a, b = at
                blocks[at] = gram[a * K:(a + 1) * K, b * K:(b + 1) * K]
                lines[at] = jnp.sum(jnp.where(row == col, blocks[at], 0.0), axis=0, keepdims=True)
    scale = jnp.ones_like(unit)
    moments, highs, lows = [], [], []
    for k in range(2 * ITERS):
        moment = jnp.zeros((K, K), F32)
        pair = (jnp.zeros((1, K), F32), jnp.zeros((1, K), F32))
        for at, factor in EXPANSION[k]:
            moment = moment + float(factor) * blocks[at]
            bit = 1
            while bit <= factor:
                if factor & bit:
                    pair = pair_add(pair, float(bit) * lines[at])
                bit *= 2
        moments.append(moment * scale)
        highs.append(pair[0] * scale)
        lows.append(pair[1] * scale)
        scale = scale * unit
    packs = [
        jnp.where(row > col, moments[i], jnp.where(row < col, moments[i + 1], 0.0))
        for i in range(0, 2 * ITERS, 2)
    ]
    first = jnp.concatenate(packs[:2], axis=1)
    second = jnp.concatenate([packs[2][:K // 2], packs[2][K // 2:]], axis=1)
    gap = jnp.zeros((1, K), F32)
    rest = jnp.zeros((2, 2 * K), F32)

    def tail(at):
        return [
            jnp.concatenate([highs[at], highs[at + 1]], axis=1),
            jnp.concatenate([highs[at + 2], gap], axis=1),
            rest,
            jnp.concatenate([lows[at], lows[at + 1]], axis=1),
            jnp.concatenate([lows[at + 2], gap], axis=1),
            rest,
        ]

    top = jnp.concatenate([first[:BODY]] + tail(0), axis=0)
    bottom = jnp.concatenate([first[BODY:], second] + tail(3), axis=0)
    low_core = lax.rem(lax.axis_index("gx"), 2) == 0
    keep_ref[...] = jnp.where(low_core, top, bottom)
    send_ref[...] = jnp.where(low_core, bottom, top)


def unpack(top, bottom):
    row = lax.broadcasted_iota(jnp.int32, (K, K), 0)
    col = lax.broadcasted_iota(jnp.int32, (K, K), 1)
    first = jnp.concatenate([top[:BODY], bottom[:K - BODY]], axis=0)
    second = bottom[K - BODY:BODY]
    packs = [first[:, :K], first[:, K:], jnp.concatenate([second[:, :K], second[:, K:]], axis=0)]
    moments, pairs = [], []
    for value in packs:
        flip = value.T
        moments.append(jnp.where(row > col, value, flip))
        moments.append(jnp.where(row < col, value, flip))
    for half in (top, bottom):
        for at in ((0, 0), (0, K), (1, 0)):
            pairs.append(tuple(
                half[BODY + shift + at[0]:BODY + shift + at[0] + 1, at[1]:at[1] + K]
                for shift in (0, TAIL // 2)
            ))
    return moments, pairs


def krylov(up, here, down):
    rows, lanes = here.shape[1:]
    own = lanes - 2 * DEEP * NZ
    tall = rows + 2 * DEEP
    inner = tall - 2
    return pl.pallas_call(
        krylov_kernel,
        out_shape=(
            jax.ShapeDtypeStruct(((ITERS + 1) * K, rows * own), F32),
            jax.ShapeDtypeStruct((BODY + TAIL, 2 * K), F32),
            jax.ShapeDtypeStruct((BODY + TAIL, 2 * K), F32),
            jax.ShapeDtypeStruct((8, 2 * K), F32),
        ),
        in_specs=[pl.BlockSpec(memory_space=pltpu.VMEM)] * 3,
        out_specs=[pl.BlockSpec(memory_space=pltpu.VMEM)] * 4,
        scratch_shapes=[
            pltpu.VMEM((tall, lanes), F32),
            pltpu.VMEM((tall, lanes), F32),
            pltpu.VMEM((6, inner, lanes), F32),
            pltpu.VMEM((6, inner, lanes), F32),
            pltpu.VMEM((6, inner, lanes), F32),
            pltpu.VMEM((inner, lanes), F32),
            pltpu.VMEM((inner, K, lanes), F32),
            pltpu.VMEM((inner - 2, K, lanes), F32),
            pltpu.VMEM((inner - 4, K, lanes), F32),
            pltpu.VMEM((ITERS * K, (ITERS + 1) * K), F32),
        ],
        compiler_params=pltpu.CompilerParams(vmem_limit_bytes=40 * 1024 * 1024),
    )(up, here, down)


def splat(value, j):
    return jnp.broadcast_to(value[:, j:j + 1], (value.shape[0], 128))


def line(value, j):
    return jnp.broadcast_to(value[j:j + 1], (PANEL, 128))


def gauss_jordan(work, start, stop):
    total = work.shape[1]
    sub = lax.broadcasted_iota(jnp.int32, (PANEL, 128), 0)
    small = None
    for at in range(start, stop, PANEL):
        base = at // 128 * 128
        column = work[start:stop, base:base + 128]
        spread = [splat(column, at - base + j) for j in range(PANEL)]
        if small is None:
            small = [value[at - start:at - start + PANEL] for value in spread]
        after = at + PANEL
        ahead, below = [], []
        if after < stop:
            base = after // 128 * 128
            strip = work[at:after, base:base + 128]
            ahead = [splat(strip, after - base + j) for j in range(PANEL)]
            strip = work[after:after + PANEL, base:base + 128]
            below = [splat(strip, after - base + j) for j in range(PANEL)]
        tiles = [t for t in range(0, total, 128) if t + 128 > after]
        values = small + ahead + [work[at:after, t:t + 128] for t in tiles]
        scale = jnp.ones((PANEL, 128), F32)
        for j in range(PANEL):
            inverse = 1.0 / line(values[j], j)
            scale = jnp.where(sub == j, inverse, scale)
            factor = jnp.where(sub == j, 0.0, values[j]) * inverse
            for i in range(j + 1, len(values)):
                values[i] = values[i] - factor * line(values[i], j)
        values = [value * scale for value in values]
        ahead = values[PANEL:PANEL + len(ahead)]
        rows = values[PANEL + len(ahead):]
        if after < stop:
            small = []
            for value, column in zip(below, ahead):
                for j in range(PANEL):
                    value = value - spread[j][after - start:after - start + PANEL] * line(column, j)
                small.append(value)
        for row, t in zip(rows, tiles):
            for first, last in ((after, min(after + PANEL, stop)), (after + PANEL, stop), (start, at)):
                if first >= last:
                    continue
                acc = work[first:last, t:t + 128]
                for j in range(PANEL):
                    acc = acc - spread[j][first - start:last - start] * row[j:j + 1]
                work[first:last, t:t + 128] = acc
            work[at:after, t:t + 128] = row


def solve(work, size):
    total = work.shape[1]
    for start in range(0, size, K):
        stop = start + K
        gauss_jordan(work, start, stop)
        if stop < size:
            base = stop // 128 * 128
            work[stop:size, base:total] = work[stop:size, base:total] - jnp.dot(
                work[stop:size, start:stop], work[start:stop, base:total],
                precision=HIGH, preferred_element_type=F32,
            )
    for start in range(size - 2 * K, -1, -K):
        stop = start + K
        work[start:stop, size:total] = work[start:stop, size:total] - jnp.dot(
            work[start:stop, stop:size], work[stop:size, size:total],
            precision=HIGH, preferred_element_type=F32,
        )


def finish_kernel(
    mine_ref, other_ref, unit_ref, fields_ref, solution_out, residual_out,
    work, coeff, mixed, solution_ref, residual_ref, sems,
):
    rows, cols = solution_ref.shape[:2]
    size = ITERS * K
    low_core = lax.rem(lax.axis_index("gx"), 2) == 0
    mine, other = mine_ref[...], other_ref[...]
    moments, pairs = unpack(
        jnp.where(low_core, mine, other), jnp.where(low_core, other, mine)
    )
    common, inverse = power_of_two(
        jnp.sum(pairs[1][0], keepdims=True) / jnp.sum(pairs[0][0], keepdims=True)
    )
    scale = jnp.ones_like(common)
    for k in range(2 * ITERS):
        moments[k] = moments[k] * scale
        pairs[k] = (pairs[k][0] * scale, pairs[k][1] * scale)
        scale = scale * inverse
    eye = (
        lax.broadcasted_iota(jnp.int32, (K, K), 0) == lax.broadcasted_iota(jnp.int32, (K, K), 1)
    )

    def whole(k):
        return jnp.where(eye, pairs[k][0] + pairs[k][1], moments[k])

    for level in range(2 * ITERS - 1):
        if level < ITERS:
            work[level * K:(level + 1) * K, size:size + K] = whole(0)
        block = whole(1)
        for i in range(ITERS):
            j = level - i
            if 0 <= j < ITERS:
                work[i * K:(i + 1) * K, j * K:(j + 1) * K] = block
        for k in range(len(moments) - 1):
            high, low = pair_add(pairs[k + 1], -pairs[k][0])
            pairs[k] = (high, low - pairs[k][1])
            moments[k] = moments[k + 1] - moments[k]
        moments.pop()
        pairs.pop()
    solve(work, size)
    unit = unit_ref[0:1, 0:1]
    ratio = unit * inverse
    shift = ratio - 1.0
    y0, y1, y2 = (work[i * K:(i + 1) * K, size:size + K] * inverse for i in range(ITERS))
    y0 = y0 + shift * y1 + (shift * shift) * y2
    y1 = ratio * y1 + (2.0 * ratio * shift) * y2
    y2 = (ratio * ratio) * y2
    coeff[0:K, 0:K] = y0
    coeff[K:2 * K, 0:K] = y1
    coeff[2 * K:3 * K, 0:K] = y2
    coeff[3 * K:4 * K, 0:K] = jnp.zeros((K, K), F32)
    coeff[0:K, K:2 * K] = eye.astype(F32) - unit * y0
    coeff[K:2 * K, K:2 * K] = -unit * (y0 + y1)
    coeff[2 * K:3 * K, K:2 * K] = -unit * (y1 + y2)
    coeff[3 * K:4 * K, K:2 * K] = -unit * y2
    own = cols * NZ
    low = lax.broadcasted_iota(jnp.int32, (cols, 2 * K), 1) < K
    copies = []
    for row in range(rows):
        mixed[...] = lax.dot_general(
            coeff[...], fields_ref[:, row * own:(row + 1) * own], (((0,), (0,)), ((), ())),
            precision=HIGH, preferred_element_type=F32,
        ).T
        for z in range(0, NZ, 2):
            even = mixed[pl.ds(z, cols, stride=NZ), :]
            odd = mixed[pl.ds(z + 1, cols, stride=NZ), :]
            solution_ref[row, :, z * K:(z + 2) * K] = jnp.where(low, even, pltpu.roll(odd, K, 1))
            residual_ref[row, :, z * K:(z + 2) * K] = jnp.where(low, pltpu.roll(even, K, 1), odd)
        for side, (here, there) in enumerate(
            ((solution_ref, solution_out), (residual_ref, residual_out))
        ):
            copy = pltpu.make_async_copy(here.at[row], there.at[row], sems.at[side, row])
            copy.start()
            copies.append(copy)
    for copy in copies:
        copy.wait()


def finish(mine, other, unit, fields, rows, cols):
    out = jax.ShapeDtypeStruct((rows, cols, NZ * K), F32)
    return pl.pallas_call(
        finish_kernel,
        out_shape=(out, out),
        in_specs=[pl.BlockSpec(memory_space=pltpu.VMEM)] * 4,
        out_specs=[pl.BlockSpec(memory_space=pl.ANY)] * 2,
        scratch_shapes=[
            pltpu.VMEM((ITERS * K, (ITERS + 1) * K), F32),
            pltpu.VMEM(((ITERS + 1) * K, 2 * K), F32),
            pltpu.VMEM((cols * NZ, 2 * K), F32),
            pltpu.VMEM((rows, cols, NZ * K), F32),
            pltpu.VMEM((rows, cols, NZ * K), F32),
            pltpu.SemaphoreType.DMA((2, rows)),
        ],
        compiler_params=pltpu.CompilerParams(vmem_limit_bytes=40 * 1024 * 1024),
    )(mine, other, unit, fields)


def add_parts(value, *others):
    half = BODY + TAIL // 2
    lost = jnp.zeros_like(value[BODY:half])
    for other in others:
        total = value + other
        old, new, add = value[BODY:half], total[BODY:half], other[BODY:half]
        back = new - old
        lost = lost + ((old - (new - back)) + (add - back))
        value = total
    return jnp.concatenate([value[:half], value[half:] + lost], axis=0)


def flipped(value, axis, *masks):
    count = lax.axis_size(axis)
    return [lax.ppermute(value, axis, [(i, i ^ mask) for i in range(count)]) for mask in masks]


def sum_of_all(value, axis):
    count = lax.axis_size(axis)
    parts = lax.all_to_all(jnp.broadcast_to(value[None], (count,) + value.shape), axis, 0, 0)
    return add_parts(*(parts[i] for i in range(count)))


def from_both(first, last, axis, outer):
    count = lax.axis_size(axis)
    here = lax.axis_index(axis)
    even = lax.rem(here, 2) == 0
    odd = ~even
    one = lax.ppermute(jnp.where(even, first, last), ("gx", "gy"), outer)
    two = lax.ppermute(jnp.where(even, last, first), axis, [(i, i ^ 1) for i in range(count)])
    before, after = jnp.where(odd, two, one), jnp.where(odd, one, two)
    return jnp.where(here == 0, 0.0, before), jnp.where(here == count - 1, 0.0, after)


def outer_pairs():
    wide, high = lax.axis_size("gx"), lax.axis_size("gy")
    along_x, along_y = [], []
    for i in range(wide):
        for j in range(high):
            here = i * high + j
            along_x.append((here, (((i + 1) ^ 1) - 1) % wide * high + j))
            if j in (0, high - 1):
                along_y.append((here, (i ^ 1) * high + j))
            else:
                along_y.append((here, i * high + ((j + 1) ^ 1) - 1))
    return along_x, along_y


def shards(diffusivity, labels, obstacles):
    rows, cols = diffusivity.shape[:2]
    diffusivity, labels, obstacles = (
        jnp.transpose(value, (0, 2, 1)) for value in (diffusivity, labels, obstacles)
    )
    conductive = diffusivity * (1 - obstacles).astype(F32)
    cells = jnp.concatenate([conductive, labels.astype(F32)], axis=0)
    cells = lax.optimization_barrier(cells).reshape(2, rows, NZ, cols)
    cells = jnp.transpose(cells, (0, 1, 3, 2))
    cells = cells.reshape(2, rows, cols * NZ)
    edge = DEEP * NZ
    along_x, along_y = outer_pairs()
    before, after = from_both(cells[:, :, :edge], cells[:, :, -edge:], "gy", along_y)
    here = jnp.concatenate([cells, after, before], axis=2)
    up, down = from_both(here[:, :DEEP], here[:, rows - DEEP:], "gx", along_x)
    fields, keep, send, unit = krylov(up, here, down)
    mine = add_parts(keep, *flipped(send, "gx", 1))
    mine = add_parts(mine, *flipped(mine, "gx", 2, 4, 6))
    mine = add_parts(mine, *flipped(mine, "gx", 12))
    mine = sum_of_all(mine, "gy")
    return finish(mine, *flipped(mine, "gx", 1), unit, fields, rows, cols)


def solution(mesh):
    in_specs = (P("gx", "gy", None), P("gx", "gy", None), P("gx", "gy", None))
    out_specs = (P("gx", "gy", None), P("gx", "gy", None))
    return jax.shard_map(shards, mesh=mesh, in_specs=in_specs, out_specs=out_specs, check_vma=False)
```

```python
import math

import jax
import jax.numpy as jnp
from jax import lax
from jax.experimental import pallas as pl
from jax.experimental.pallas import tpu as pltpu
from jax.sharding import PartitionSpec as P

NZ = 16
K = 64
ITERS = 3
DEEP = ITERS + 1

BODY = 3 * K // 4
TAIL = 8
PANEL = 8

HIGH = lax.Precision.HIGHEST
F32 = jnp.float32


def face(here, there):
    product = here * there
    return 2.0 * product / jnp.where(product > 0, here + there, 1.0)


def krylov_kernel(
    up_ref, here_ref, down_ref, fields_ref, keep_ref, send_ref, unit_ref,
    cond, label, couple, weight, nbr, diag, v0, v1, v2, gram,
):
    rows = here_ref.shape[1]
    lanes = here_ref.shape[2]
    own = fields_ref.shape[1] // rows
    tall = rows + 2 * DEEP
    for plane, ref in ((0, cond), (1, label)):
        ref[0:DEEP, :] = up_ref[plane]
        ref[DEEP:DEEP + rows, :] = here_ref[plane]
        ref[DEEP + rows:tall, :] = down_ref[plane]
    inner = tall - 2
    lane = lax.broadcasted_iota(jnp.int32, (inner, lanes), 1)
    depth = lane & (NZ - 1)
    center = cond[1:1 + inner, :]
    free = jnp.where((center > 0) & (label[1:1 + inner, :] == 0), 1.0, 0.0)

    def views(ref):
        mid = ref[1:1 + inner, :]
        return [
            ref[2:2 + inner, :],
            ref[0:inner, :],
            pltpu.roll(mid, lanes - NZ, 1),
            pltpu.roll(mid, NZ, 1),
            jnp.where(depth == NZ - 1, 0.0, pltpu.roll(mid, lanes - 1, 1)),
            jnp.where(depth == 0, 0.0, pltpu.roll(mid, 1, 1)),
        ]

    total = jnp.zeros((inner, lanes), F32)
    for side, (there, mark) in enumerate(zip(views(cond), views(label))):
        conduct = face(center, there)
        total = total + conduct
        weight[side] = free * conduct
        nbr[side] = mark
        couple[side] = jnp.where(mark == 0, free * conduct, 0.0)
    mean = jnp.sum(free * total, keepdims=True) / jnp.maximum(jnp.sum(free, keepdims=True), 1.0)
    unit, inverse = power_of_two(1.5 * mean)
    unit_ref[...] = jnp.broadcast_to(unit, unit_ref.shape)
    diag[...] = free * (total * inverse - 1.0)
    for side in range(6):
        couple[side] = couple[side] * inverse

    step = 32
    cluster = lax.broadcasted_iota(jnp.int32, (step, lanes), 0)
    powers = (v0, v1, v2)

    def store(order, row, cut, value):
        if order < ITERS:
            powers[order][row, cut, :] = value
        at = row - (ITERS - order)
        if 0 <= at < rows:
            fields_ref[order * K + cut.start:order * K + cut.stop, at * own:(at + 1) * own] = (
                value[:, 0:own]
            )

    def fill(row):
        for part in range(0, K, step):
            ids = (cluster + (part + 1)).astype(F32)
            acc = jnp.zeros((step, lanes), F32)
            for side in range(6):
                hit = nbr[side, row:row + 1, :] == ids
                acc = acc + jnp.where(hit, weight[side, row:row + 1, :], 0.0)
            store(0, row, slice(part, part + step), acc)

    def power(order, row):
        source = powers[order - 1]
        at = row + order
        for part in range(0, K, step):
            cut = slice(part, part + step)
            mid = source[row + 1, cut, :]
            acc = diag[at:at + 1, :] * mid
            acc = acc - couple[0, at:at + 1, :] * source[row + 2, cut, :]
            acc = acc - couple[1, at:at + 1, :] * source[row, cut, :]
            acc = acc - couple[2, at:at + 1, :] * pltpu.roll(mid, lanes - NZ, 1)
            acc = acc - couple[3, at:at + 1, :] * pltpu.roll(mid, NZ, 1)
            acc = acc - couple[4, at:at + 1, :] * pltpu.roll(mid, lanes - 1, 1)
            acc = acc - couple[5, at:at + 1, :] * pltpu.roll(mid, 1, 1)
            store(order, row, cut, acc)

    for front in range(inner):
        fill(front)
        for order in range(1, ITERS + 1):
            if front >= 2 * order:
                power(order, front - 2 * order)
        at = front - 2 * ITERS
        if at >= 0:
            part = lax.dot_general(
                fields_ref[0:ITERS * K, at * own:(at + 1) * own],
                fields_ref[:, at * own:(at + 1) * own],
                (((1,), (1,)), ((), ())), precision=HIGH, preferred_element_type=F32,
            )
            gram[...] = part if at == 0 else gram[...] + part
    pack(gram, unit, keep_ref, send_ref)


def power_of_two(value):
    unit = jnp.full(value.shape, 2.0 ** -4, F32)
    inverse = jnp.full(value.shape, 2.0 ** 4, F32)
    for exponent in range(-4, 9):
        more = value > 2.0 ** (exponent + 0.5)
        unit = jnp.where(more, 2.0 ** (exponent + 1), unit)
        inverse = jnp.where(more, 2.0 ** (-exponent - 1), inverse)
    return unit, inverse


def pair_add(pair, value):
    high, low = pair
    total = high + value
    back = total - high
    return total, low + ((high - (total - back)) + (value - back))


EXPANSION = []
for k in range(2 * ITERS):
    first, second = k // 2, k - k // 2
    terms = {}
    for a in range(first + 1):
        for b in range(second + 1):
            terms[a, b] = math.comb(first, a) * math.comb(second, b)
    EXPANSION.append(sorted(terms.items(), reverse=True))


def pack(gram, unit, keep_ref, send_ref):
    row = lax.broadcasted_iota(jnp.int32, (K, K), 0)
    col = lax.broadcasted_iota(jnp.int32, (K, K), 1)
    blocks = {}
    lines = {}
    for k in range(2 * ITERS):
        for at, _ in EXPANSION[k]:
            if at not in blocks:
                a, b = at
                blocks[at] = gram[a * K:(a + 1) * K, b * K:(b + 1) * K]
                lines[at] = jnp.sum(jnp.where(row == col, blocks[at], 0.0), axis=0, keepdims=True)
    scale = jnp.ones_like(unit)
    moments, highs, lows = [], [], []
    for k in range(2 * ITERS):
        moment = jnp.zeros((K, K), F32)
        pair = (jnp.zeros((1, K), F32), jnp.zeros((1, K), F32))
        for at, factor in EXPANSION[k]:
            moment = moment + float(factor) * blocks[at]
            bit = 1
            while bit <= factor:
                if factor & bit:
                    pair = pair_add(pair, float(bit) * lines[at])
                bit *= 2
        moments.append(moment * scale)
        highs.append(pair[0] * scale)
        lows.append(pair[1] * scale)
        scale = scale * unit
    packs = [
        jnp.where(row > col, moments[i], jnp.where(row < col, moments[i + 1], 0.0))
        for i in range(0, 2 * ITERS, 2)
    ]
    first = jnp.concatenate(packs[:2], axis=1)
    second = jnp.concatenate([packs[2][:K // 2], packs[2][K // 2:]], axis=1)
    gap = jnp.zeros((1, K), F32)
    rest = jnp.zeros((2, 2 * K), F32)

    def tail(at):
        return [
            jnp.concatenate([highs[at], highs[at + 1]], axis=1),
            jnp.concatenate([highs[at + 2], gap], axis=1),
            rest,
            jnp.concatenate([lows[at], lows[at + 1]], axis=1),
            jnp.concatenate([lows[at + 2], gap], axis=1),
            rest,
        ]

    top = jnp.concatenate([first[:BODY]] + tail(0), axis=0)
    bottom = jnp.concatenate([first[BODY:], second] + tail(3), axis=0)
    low_core = lax.rem(lax.axis_index("gx"), 2) == 0
    keep_ref[...] = jnp.where(low_core, top, bottom)
    send_ref[...] = jnp.where(low_core, bottom, top)


def unpack(top, bottom):
    row = lax.broadcasted_iota(jnp.int32, (K, K), 0)
    col = lax.broadcasted_iota(jnp.int32, (K, K), 1)
    first = jnp.concatenate([top[:BODY], bottom[:K - BODY]], axis=0)
    second = bottom[K - BODY:BODY]
    packs = [first[:, :K], first[:, K:], jnp.concatenate([second[:, :K], second[:, K:]], axis=0)]
    moments, pairs = [], []
    for value in packs:
        flip = value.T
        moments.append(jnp.where(row > col, value, flip))
        moments.append(jnp.where(row < col, value, flip))
    for half in (top, bottom):
        for at in ((0, 0), (0, K), (1, 0)):
            pairs.append(tuple(
                half[BODY + shift + at[0]:BODY + shift + at[0] + 1, at[1]:at[1] + K]
                for shift in (0, TAIL // 2)
            ))
    return moments, pairs


def krylov(up, here, down):
    rows, lanes = here.shape[1:]
    own = lanes - 2 * DEEP * NZ
    tall = rows + 2 * DEEP
    inner = tall - 2
    return pl.pallas_call(
        krylov_kernel,
        out_shape=(
            jax.ShapeDtypeStruct(((ITERS + 1) * K, rows * own), F32),
            jax.ShapeDtypeStruct((BODY + TAIL, 2 * K), F32),
            jax.ShapeDtypeStruct((BODY + TAIL, 2 * K), F32),
            jax.ShapeDtypeStruct((8, 2 * K), F32),
        ),
        in_specs=[pl.BlockSpec(memory_space=pltpu.VMEM)] * 3,
        out_specs=[pl.BlockSpec(memory_space=pltpu.VMEM)] * 4,
        scratch_shapes=[
            pltpu.VMEM((tall, lanes), F32),
            pltpu.VMEM((tall, lanes), F32),
            pltpu.VMEM((6, inner, lanes), F32),
            pltpu.VMEM((6, inner, lanes), F32),
            pltpu.VMEM((6, inner, lanes), F32),
            pltpu.VMEM((inner, lanes), F32),
            pltpu.VMEM((inner, K, lanes), F32),
            pltpu.VMEM((inner - 2, K, lanes), F32),
            pltpu.VMEM((inner - 4, K, lanes), F32),
            pltpu.VMEM((ITERS * K, (ITERS + 1) * K), F32),
        ],
        compiler_params=pltpu.CompilerParams(vmem_limit_bytes=40 * 1024 * 1024),
    )(up, here, down)


def splat(value, j):
    return jnp.broadcast_to(value[:, j:j + 1], (value.shape[0], 128))


def line(value, j):
    return jnp.broadcast_to(value[j:j + 1], (PANEL, 128))


def gauss_jordan(work, start, stop):
    total = work.shape[1]
    sub = lax.broadcasted_iota(jnp.int32, (PANEL, 128), 0)
    small = None
    for at in range(start, stop, PANEL):
        base = at // 128 * 128
        column = work[start:stop, base:base + 128]
        spread = [splat(column, at - base + j) for j in range(PANEL)]
        if small is None:
            small = [value[at - start:at - start + PANEL] for value in spread]
        after = at + PANEL
        ahead, below = [], []
        if after < stop:
            base = after // 128 * 128
            strip = work[at:after, base:base + 128]
            ahead = [splat(strip, after - base + j) for j in range(PANEL)]
            strip = work[after:after + PANEL, base:base + 128]
            below = [splat(strip, after - base + j) for j in range(PANEL)]
        tiles = [t for t in range(0, total, 128) if t + 128 > after]
        values = small + ahead + [work[at:after, t:t + 128] for t in tiles]
        scale = jnp.ones((PANEL, 128), F32)
        for j in range(PANEL):
            inverse = 1.0 / line(values[j], j)
            scale = jnp.where(sub == j, inverse, scale)
            factor = jnp.where(sub == j, 0.0, values[j]) * inverse
            for i in range(j + 1, len(values)):
                values[i] = values[i] - factor * line(values[i], j)
        values = [value * scale for value in values]
        ahead = values[PANEL:PANEL + len(ahead)]
        rows = values[PANEL + len(ahead):]
        if after < stop:
            small = []
            for value, column in zip(below, ahead):
                for j in range(PANEL):
                    value = value - spread[j][after - start:after - start + PANEL] * line(column, j)
                small.append(value)
        for row, t in zip(rows, tiles):
            for first, last in ((after, min(after + PANEL, stop)), (after + PANEL, stop), (start, at)):
                if first >= last:
                    continue
                acc = work[first:last, t:t + 128]
                for j in range(PANEL):
                    acc = acc - spread[j][first - start:last - start] * row[j:j + 1]
                work[first:last, t:t + 128] = acc
            work[at:after, t:t + 128] = row


def solve(work, size):
    total = work.shape[1]
    for start in range(0, size, K):
        stop = start + K
        gauss_jordan(work, start, stop)
        if stop < size:
            base = stop // 128 * 128
            work[stop:size, base:total] = work[stop:size, base:total] - jnp.dot(
                work[stop:size, start:stop], work[start:stop, base:total],
                precision=HIGH, preferred_element_type=F32,
            )
    for start in range(size - 2 * K, -1, -K):
        stop = start + K
        work[start:stop, size:total] = work[start:stop, size:total] - jnp.dot(
            work[start:stop, stop:size], work[stop:size, size:total],
            precision=HIGH, preferred_element_type=F32,
        )


def finish_kernel(
    mine_ref, other_ref, unit_ref, fields_ref, solution_out, residual_out,
    work, coeff, mixed, solution_ref, residual_ref, sems,
):
    rows, cols = solution_ref.shape[:2]
    size = ITERS * K
    low_core = lax.rem(lax.axis_index("gx"), 2) == 0
    mine, other = mine_ref[...], other_ref[...]
    moments, pairs = unpack(
        jnp.where(low_core, mine, other), jnp.where(low_core, other, mine)
    )
    common, inverse = power_of_two(
        jnp.sum(pairs[1][0], keepdims=True) / jnp.sum(pairs[0][0], keepdims=True)
    )
    scale = jnp.ones_like(common)
    for k in range(2 * ITERS):
        moments[k] = moments[k] * scale
        pairs[k] = (pairs[k][0] * scale, pairs[k][1] * scale)
        scale = scale * inverse
    eye = (
        lax.broadcasted_iota(jnp.int32, (K, K), 0) == lax.broadcasted_iota(jnp.int32, (K, K), 1)
    )

    def whole(k):
        return jnp.where(eye, pairs[k][0] + pairs[k][1], moments[k])

    for level in range(2 * ITERS - 1):
        if level < ITERS:
            work[level * K:(level + 1) * K, size:size + K] = whole(0)
        block = whole(1)
        for i in range(ITERS):
            j = level - i
            if 0 <= j < ITERS:
                work[i * K:(i + 1) * K, j * K:(j + 1) * K] = block
        for k in range(len(moments) - 1):
            high, low = pair_add(pairs[k + 1], -pairs[k][0])
            pairs[k] = (high, low - pairs[k][1])
            moments[k] = moments[k + 1] - moments[k]
        moments.pop()
        pairs.pop()
    solve(work, size)
    unit = unit_ref[0:1, 0:1]
    ratio = unit * inverse
    shift = ratio - 1.0
    y0, y1, y2 = (work[i * K:(i + 1) * K, size:size + K] * inverse for i in range(ITERS))
    y0 = y0 + shift * y1 + (shift * shift) * y2
    y1 = ratio * y1 + (2.0 * ratio * shift) * y2
    y2 = (ratio * ratio) * y2
    coeff[0:K, 0:K] = y0
    coeff[K:2 * K, 0:K] = y1
    coeff[2 * K:3 * K, 0:K] = y2
    coeff[3 * K:4 * K, 0:K] = jnp.zeros((K, K), F32)
    coeff[0:K, K:2 * K] = eye.astype(F32) - unit * y0
    coeff[K:2 * K, K:2 * K] = -unit * (y0 + y1)
    coeff[2 * K:3 * K, K:2 * K] = -unit * (y1 + y2)
    coeff[3 * K:4 * K, K:2 * K] = -unit * y2
    own = cols * NZ
    low = lax.broadcasted_iota(jnp.int32, (cols, 2 * K), 1) < K
    copies = []
    for row in range(rows):
        mixed[...] = lax.dot_general(
            coeff[...], fields_ref[:, row * own:(row + 1) * own], (((0,), (0,)), ((), ())),
            precision=HIGH, preferred_element_type=F32,
        ).T
        for z in range(0, NZ, 2):
            even = mixed[pl.ds(z, cols, stride=NZ), :]
            odd = mixed[pl.ds(z + 1, cols, stride=NZ), :]
            solution_ref[row, :, z * K:(z + 2) * K] = jnp.where(low, even, pltpu.roll(odd, K, 1))
            residual_ref[row, :, z * K:(z + 2) * K] = jnp.where(low, pltpu.roll(even, K, 1), odd)
        for side, (here, there) in enumerate(
            ((solution_ref, solution_out), (residual_ref, residual_out))
        ):
            copy = pltpu.make_async_copy(here.at[row], there.at[row], sems.at[side, row])
            copy.start()
            copies.append(copy)
    for copy in copies:
        copy.wait()


def finish(mine, other, unit, fields, rows, cols):
    out = jax.ShapeDtypeStruct((rows, cols, NZ * K), F32)
    return pl.pallas_call(
        finish_kernel,
        out_shape=(out, out),
        in_specs=[pl.BlockSpec(memory_space=pltpu.VMEM)] * 4,
        out_specs=[pl.BlockSpec(memory_space=pl.ANY)] * 2,
        scratch_shapes=[
            pltpu.VMEM((ITERS * K, (ITERS + 1) * K), F32),
            pltpu.VMEM(((ITERS + 1) * K, 2 * K), F32),
            pltpu.VMEM((cols * NZ, 2 * K), F32),
            pltpu.VMEM((rows, cols, NZ * K), F32),
            pltpu.VMEM((rows, cols, NZ * K), F32),
            pltpu.SemaphoreType.DMA((2, rows)),
        ],
        compiler_params=pltpu.CompilerParams(vmem_limit_bytes=40 * 1024 * 1024),
    )(mine, other, unit, fields)


def add_parts(value, *others):
    half = BODY + TAIL // 2
    lost = jnp.zeros_like(value[BODY:half])
    for other in others:
        total = value + other
        old, new, add = value[BODY:half], total[BODY:half], other[BODY:half]
        back = new - old
        lost = lost + ((old - (new - back)) + (add - back))
        value = total
    return jnp.concatenate([value[:half], value[half:] + lost], axis=0)


def flipped(value, axis, *masks):
    count = lax.axis_size(axis)
    return [lax.ppermute(value, axis, [(i, i ^ mask) for i in range(count)]) for mask in masks]


def sum_of_all(value, axis):
    count = lax.axis_size(axis)
    parts = lax.all_to_all(jnp.broadcast_to(value[None], (count,) + value.shape), axis, 0, 0)
    return add_parts(*(parts[i] for i in range(count)))


def from_both(first, last, axis, outer):
    count = lax.axis_size(axis)
    here = lax.axis_index(axis)
    even = lax.rem(here, 2) == 0
    odd = ~even
    one = lax.ppermute(jnp.where(even, first, last), ("gx", "gy"), outer)
    two = lax.ppermute(jnp.where(even, last, first), axis, [(i, i ^ 1) for i in range(count)])
    before, after = jnp.where(odd, two, one), jnp.where(odd, one, two)
    return jnp.where(here == 0, 0.0, before), jnp.where(here == count - 1, 0.0, after)


def outer_pairs():
    wide, high = lax.axis_size("gx"), lax.axis_size("gy")
    along_x, along_y = [], []
    for i in range(wide):
        for j in range(high):
            here = i * high + j
            along_x.append((here, (((i + 1) ^ 1) - 1) % wide * high + j))
            if j in (0, high - 1):
                along_y.append((here, (i ^ 1) * high + j))
            else:
                along_y.append((here, i * high + ((j + 1) ^ 1) - 1))
    return along_x, along_y


def shards(diffusivity, labels, obstacles):
    rows, cols = diffusivity.shape[:2]
    diffusivity, labels, obstacles = (
        jnp.transpose(value, (0, 2, 1)) for value in (diffusivity, labels, obstacles)
    )
    conductive = diffusivity * (1 - obstacles).astype(F32)
    cells = jnp.concatenate([conductive, labels.astype(F32)], axis=0)
    cells = lax.optimization_barrier(cells).reshape(2, rows, NZ, cols)
    cells = jnp.transpose(cells, (0, 1, 3, 2))
    cells = cells.reshape(2, rows, cols * NZ)
    edge = DEEP * NZ
    along_x, along_y = outer_pairs()
    before, after = from_both(cells[:, :, :edge], cells[:, :, -edge:], "gy", along_y)
    here = jnp.concatenate([cells, after, before], axis=2)
    up, down = from_both(here[:, :DEEP], here[:, rows - DEEP:], "gx", along_x)
    fields, keep, send, unit = krylov(up, here, down)
    mine = add_parts(keep, *flipped(send, "gx", 1))
    mine = add_parts(mine, *flipped(mine, "gx", 2, 6, 4))
    mine = add_parts(mine, *flipped(mine, "gx", 12))
    mine = sum_of_all(mine, "gy")
    return finish(mine, *flipped(mine, "gx", 1), unit, fields, rows, cols)


def solution(mesh):
    in_specs = (P("gx", "gy", None), P("gx", "gy", None), P("gx", "gy", None))
    out_specs = (P("gx", "gy", None), P("gx", "gy", None))
    return jax.shard_map(shards, mesh=mesh, in_specs=in_specs, out_specs=out_specs, check_vma=False)
```

```python
import math

import jax
import jax.numpy as jnp
from jax import lax
from jax.experimental import pallas as pl
from jax.experimental.pallas import tpu as pltpu
from jax.sharding import PartitionSpec as P

NZ = 16
K = 64
ITERS = 3
DEEP = ITERS + 1

BODY = 3 * K // 4
TAIL = 8
PANEL = 8

HIGH = lax.Precision.HIGHEST
F32 = jnp.float32


def face(here, there):
    product = here * there
    return 2.0 * product / jnp.where(product > 0, here + there, 1.0)


def krylov_kernel(
    up_ref, here_ref, down_ref, fields_ref, keep_ref, send_ref, unit_ref,
    cond, label, couple, weight, nbr, diag, v0, v1, v2, gram,
):
    rows = here_ref.shape[1]
    lanes = here_ref.shape[2]
    own = fields_ref.shape[1] // rows
    tall = rows + 2 * DEEP
    for plane, ref in ((0, cond), (1, label)):
        ref[0:DEEP, :] = up_ref[plane]
        ref[DEEP:DEEP + rows, :] = here_ref[plane]
        ref[DEEP + rows:tall, :] = down_ref[plane]
    inner = tall - 2
    lane = lax.broadcasted_iota(jnp.int32, (inner, lanes), 1)
    depth = lane & (NZ - 1)
    center = cond[1:1 + inner, :]
    free = jnp.where((center > 0) & (label[1:1 + inner, :] == 0), 1.0, 0.0)

    def views(ref):
        mid = ref[1:1 + inner, :]
        return [
            ref[2:2 + inner, :],
            ref[0:inner, :],
            pltpu.roll(mid, lanes - NZ, 1),
            pltpu.roll(mid, NZ, 1),
            jnp.where(depth == NZ - 1, 0.0, pltpu.roll(mid, lanes - 1, 1)),
            jnp.where(depth == 0, 0.0, pltpu.roll(mid, 1, 1)),
        ]

    total = jnp.zeros((inner, lanes), F32)
    for side, (there, mark) in enumerate(zip(views(cond), views(label))):
        conduct = face(center, there)
        total = total + conduct
        weight[side] = free * conduct
        nbr[side] = mark
        couple[side] = jnp.where(mark == 0, free * conduct, 0.0)
    mean = jnp.sum(free * total, keepdims=True) / jnp.maximum(jnp.sum(free, keepdims=True), 1.0)
    unit, inverse = power_of_two(1.5 * mean)
    unit_ref[...] = jnp.broadcast_to(unit, unit_ref.shape)
    diag[...] = free * (total * inverse - 1.0)
    for side in range(6):
        couple[side] = couple[side] * inverse

    step = 32
    cluster = lax.broadcasted_iota(jnp.int32, (step, lanes), 0)
    powers = (v0, v1, v2)

    def store(order, row, cut, value):
        if order < ITERS:
            powers[order][row, cut, :] = value
        at = row - (ITERS - order)
        if 0 <= at < rows:
            fields_ref[order * K + cut.start:order * K + cut.stop, at * own:(at + 1) * own] = (
                value[:, 0:own]
            )

    def fill(row):
        for part in range(0, K, step):
            ids = (cluster + (part + 1)).astype(F32)
            acc = jnp.zeros((step, lanes), F32)
            for side in range(6):
                hit = nbr[side, row:row + 1, :] == ids
                acc = acc + jnp.where(hit, weight[side, row:row + 1, :], 0.0)
            store(0, row, slice(part, part + step), acc)

    def power(order, row):
        source = powers[order - 1]
        at = row + order
        for part in range(0, K, step):
            cut = slice(part, part + step)
            mid = source[row + 1, cut, :]
            acc = diag[at:at + 1, :] * mid
            acc = acc - couple[0, at:at + 1, :] * source[row + 2, cut, :]
            acc = acc - couple[1, at:at + 1, :] * source[row, cut, :]
            acc = acc - couple[2, at:at + 1, :] * pltpu.roll(mid, lanes - NZ, 1)
            acc = acc - couple[3, at:at + 1, :] * pltpu.roll(mid, NZ, 1)
            acc = acc - couple[4, at:at + 1, :] * pltpu.roll(mid, lanes - 1, 1)
            acc = acc - couple[5, at:at + 1, :] * pltpu.roll(mid, 1, 1)
            store(order, row, cut, acc)

    for front in range(inner):
        fill(front)
        for order in range(1, ITERS + 1):
            if front >= 2 * order:
                power(order, front - 2 * order)
        at = front - 2 * ITERS
        if at >= 0:
            part = lax.dot_general(
                fields_ref[0:ITERS * K, at * own:(at + 1) * own],
                fields_ref[:, at * own:(at + 1) * own],
                (((1,), (1,)), ((), ())), precision=HIGH, preferred_element_type=F32,
            )
            gram[...] = part if at == 0 else gram[...] + part
    pack(gram, unit, keep_ref, send_ref)


def power_of_two(value):
    unit = jnp.full(value.shape, 2.0 ** -4, F32)
    inverse = jnp.full(value.shape, 2.0 ** 4, F32)
    for exponent in range(-4, 9):
        more = value > 2.0 ** (exponent + 0.5)
        unit = jnp.where(more, 2.0 ** (exponent + 1), unit)
        inverse = jnp.where(more, 2.0 ** (-exponent - 1), inverse)
    return unit, inverse


def pair_add(pair, value):
    high, low = pair
    total = high + value
    back = total - high
    return total, low + ((high - (total - back)) + (value - back))


EXPANSION = []
for k in range(2 * ITERS):
    first, second = k // 2, k - k // 2
    terms = {}
    for a in range(first + 1):
        for b in range(second + 1):
            terms[a, b] = math.comb(first, a) * math.comb(second, b)
    EXPANSION.append(sorted(terms.items(), reverse=True))


def pack(gram, unit, keep_ref, send_ref):
    row = lax.broadcasted_iota(jnp.int32, (K, K), 0)
    col = lax.broadcasted_iota(jnp.int32, (K, K), 1)
    blocks = {}
    lines = {}
    for k in range(2 * ITERS):
        for at, _ in EXPANSION[k]:
            if at not in blocks:
                a, b = at
                blocks[at] = gram[a * K:(a + 1) * K, b * K:(b + 1) * K]
                lines[at] = jnp.sum(jnp.where(row == col, blocks[at], 0.0), axis=0, keepdims=True)
    scale = jnp.ones_like(unit)
    moments, highs, lows = [], [], []
    for k in range(2 * ITERS):
        moment = jnp.zeros((K, K), F32)
        pair = (jnp.zeros((1, K), F32), jnp.zeros((1, K), F32))
        for at, factor in EXPANSION[k]:
            moment = moment + float(factor) * blocks[at]
            bit = 1
            while bit <= factor:
                if factor & bit:
                    pair = pair_add(pair, float(bit) * lines[at])
                bit *= 2
        moments.append(moment * scale)
        highs.append(pair[0] * scale)
        lows.append(pair[1] * scale)
        scale = scale * unit
    packs = [
        jnp.where(row > col, moments[i], jnp.where(row < col, moments[i + 1], 0.0))
        for i in range(0, 2 * ITERS, 2)
    ]
    first = jnp.concatenate(packs[:2], axis=1)
    second = jnp.concatenate([packs[2][:K // 2], packs[2][K // 2:]], axis=1)
    gap = jnp.zeros((1, K), F32)
    rest = jnp.zeros((2, 2 * K), F32)

    def tail(at):
        return [
            jnp.concatenate([highs[at], highs[at + 1]], axis=1),
            jnp.concatenate([highs[at + 2], gap], axis=1),
            rest,
            jnp.concatenate([lows[at], lows[at + 1]], axis=1),
            jnp.concatenate([lows[at + 2], gap], axis=1),
            rest,
        ]

    top = jnp.concatenate([first[:BODY]] + tail(0), axis=0)
    bottom = jnp.concatenate([first[BODY:], second] + tail(3), axis=0)
    low_core = lax.rem(lax.axis_index("gx"), 2) == 0
    keep_ref[...] = jnp.where(low_core, top, bottom)
    send_ref[...] = jnp.where(low_core, bottom, top)


def unpack(top, bottom):
    row = lax.broadcasted_iota(jnp.int32, (K, K), 0)
    col = lax.broadcasted_iota(jnp.int32, (K, K), 1)
    first = jnp.concatenate([top[:BODY], bottom[:K - BODY]], axis=0)
    second = bottom[K - BODY:BODY]
    packs = [first[:, :K], first[:, K:], jnp.concatenate([second[:, :K], second[:, K:]], axis=0)]
    moments, pairs = [], []
    for value in packs:
        flip = value.T
        moments.append(jnp.where(row > col, value, flip))
        moments.append(jnp.where(row < col, value, flip))
    for half in (top, bottom):
        for at in ((0, 0), (0, K), (1, 0)):
            pairs.append(tuple(
                half[BODY + shift + at[0]:BODY + shift + at[0] + 1, at[1]:at[1] + K]
                for shift in (0, TAIL // 2)
            ))
    return moments, pairs


def krylov(up, here, down):
    rows, lanes = here.shape[1:]
    own = lanes - 2 * DEEP * NZ
    tall = rows + 2 * DEEP
    inner = tall - 2
    return pl.pallas_call(
        krylov_kernel,
        out_shape=(
            jax.ShapeDtypeStruct(((ITERS + 1) * K, rows * own), F32),
            jax.ShapeDtypeStruct((BODY + TAIL, 2 * K), F32),
            jax.ShapeDtypeStruct((BODY + TAIL, 2 * K), F32),
            jax.ShapeDtypeStruct((8, 2 * K), F32),
        ),
        in_specs=[pl.BlockSpec(memory_space=pltpu.VMEM)] * 3,
        out_specs=[pl.BlockSpec(memory_space=pltpu.VMEM)] * 4,
        scratch_shapes=[
            pltpu.VMEM((tall, lanes), F32),
            pltpu.VMEM((tall, lanes), F32),
            pltpu.VMEM((6, inner, lanes), F32),
            pltpu.VMEM((6, inner, lanes), F32),
            pltpu.VMEM((6, inner, lanes), F32),
            pltpu.VMEM((inner, lanes), F32),
            pltpu.VMEM((inner, K, lanes), F32),
            pltpu.VMEM((inner - 2, K, lanes), F32),
            pltpu.VMEM((inner - 4, K, lanes), F32),
            pltpu.VMEM((ITERS * K, (ITERS + 1) * K), F32),
        ],
        compiler_params=pltpu.CompilerParams(vmem_limit_bytes=40 * 1024 * 1024),
    )(up, here, down)


def splat(value, j):
    return jnp.broadcast_to(value[:, j:j + 1], (value.shape[0], 128))


def line(value, j):
    return jnp.broadcast_to(value[j:j + 1], (PANEL, 128))


def gauss_jordan(work, start, stop):
    total = work.shape[1]
    sub = lax.broadcasted_iota(jnp.int32, (PANEL, 128), 0)
    small = None
    for at in range(start, stop, PANEL):
        base = at // 128 * 128
        column = work[start:stop, base:base + 128]
        spread = [splat(column, at - base + j) for j in range(PANEL)]
        if small is None:
            small = [value[at - start:at - start + PANEL] for value in spread]
        after = at + PANEL
        ahead, below = [], []
        if after < stop:
            base = after // 128 * 128
            strip = work[at:after, base:base + 128]
            ahead = [splat(strip, after - base + j) for j in range(PANEL)]
            strip = work[after:after + PANEL, base:base + 128]
            below = [splat(strip, after - base + j) for j in range(PANEL)]
        tiles = [t for t in range(0, total, 128) if t + 128 > after]
        values = small + ahead + [work[at:after, t:t + 128] for t in tiles]
        scale = jnp.ones((PANEL, 128), F32)
        for j in range(PANEL):
            inverse = 1.0 / line(values[j], j)
            scale = jnp.where(sub == j, inverse, scale)
            factor = jnp.where(sub == j, 0.0, values[j]) * inverse
            for i in range(j + 1, len(values)):
                values[i] = values[i] - factor * line(values[i], j)
        values = [value * scale for value in values]
        ahead = values[PANEL:PANEL + len(ahead)]
        rows = values[PANEL + len(ahead):]
        if after < stop:
            small = []
            for value, column in zip(below, ahead):
                for j in range(PANEL):
                    value = value - spread[j][after - start:after - start + PANEL] * line(column, j)
                small.append(value)
        for row, t in zip(rows, tiles):
            for first, last in ((after, min(after + PANEL, stop)), (after + PANEL, stop), (start, at)):
                if first >= last:
                    continue
                acc = work[first:last, t:t + 128]
                for j in range(PANEL):
                    acc = acc - spread[j][first - start:last - start] * row[j:j + 1]
                work[first:last, t:t + 128] = acc
            work[at:after, t:t + 128] = row


def solve(work, size):
    total = work.shape[1]
    for start in range(0, size, K):
        stop = start + K
        gauss_jordan(work, start, stop)
        if stop < size:
            base = stop // 128 * 128
            work[stop:size, base:total] = work[stop:size, base:total] - jnp.dot(
                work[stop:size, start:stop], work[start:stop, base:total],
                precision=HIGH, preferred_element_type=F32,
            )
    for start in range(size - 2 * K, -1, -K):
        stop = start + K
        work[start:stop, size:total] = work[start:stop, size:total] - jnp.dot(
            work[start:stop, stop:size], work[stop:size, size:total],
            precision=HIGH, preferred_element_type=F32,
        )


def finish_kernel(
    mine_ref, other_ref, unit_ref, fields_ref, solution_out, residual_out,
    work, coeff, mixed, solution_ref, residual_ref, sems,
):
    rows, cols = solution_ref.shape[:2]
    size = ITERS * K
    low_core = lax.rem(lax.axis_index("gx"), 2) == 0
    mine, other = mine_ref[...], other_ref[...]
    moments, pairs = unpack(
        jnp.where(low_core, mine, other), jnp.where(low_core, other, mine)
    )
    common, inverse = power_of_two(
        jnp.sum(pairs[1][0], keepdims=True) / jnp.sum(pairs[0][0], keepdims=True)
    )
    scale = jnp.ones_like(common)
    for k in range(2 * ITERS):
        moments[k] = moments[k] * scale
        pairs[k] = (pairs[k][0] * scale, pairs[k][1] * scale)
        scale = scale * inverse
    eye = (
        lax.broadcasted_iota(jnp.int32, (K, K), 0) == lax.broadcasted_iota(jnp.int32, (K, K), 1)
    )

    def whole(k):
        return jnp.where(eye, pairs[k][0] + pairs[k][1], moments[k])

    for level in range(2 * ITERS - 1):
        if level < ITERS:
            work[level * K:(level + 1) * K, size:size + K] = whole(0)
        block = whole(1)
        for i in range(ITERS):
            j = level - i
            if 0 <= j < ITERS:
                work[i * K:(i + 1) * K, j * K:(j + 1) * K] = block
        for k in range(len(moments) - 1):
            high, low = pair_add(pairs[k + 1], -pairs[k][0])
            pairs[k] = (high, low - pairs[k][1])
            moments[k] = moments[k + 1] - moments[k]
        moments.pop()
        pairs.pop()
    solve(work, size)
    unit = unit_ref[0:1, 0:1]
    ratio = unit * inverse
    shift = ratio - 1.0
    y0, y1, y2 = (work[i * K:(i + 1) * K, size:size + K] * inverse for i in range(ITERS))
    y0 = y0 + shift * y1 + (shift * shift) * y2
    y1 = ratio * y1 + (2.0 * ratio * shift) * y2
    y2 = (ratio * ratio) * y2
    coeff[0:K, 0:K] = y0
    coeff[K:2 * K, 0:K] = y1
    coeff[2 * K:3 * K, 0:K] = y2
    coeff[3 * K:4 * K, 0:K] = jnp.zeros((K, K), F32)
    coeff[0:K, K:2 * K] = eye.astype(F32) - unit * y0
    coeff[K:2 * K, K:2 * K] = -unit * (y0 + y1)
    coeff[2 * K:3 * K, K:2 * K] = -unit * (y1 + y2)
    coeff[3 * K:4 * K, K:2 * K] = -unit * y2
    own = cols * NZ
    low = lax.broadcasted_iota(jnp.int32, (cols, 2 * K), 1) < K
    copies = []
    for row in range(rows):
        mixed[...] = lax.dot_general(
            coeff[...], fields_ref[:, row * own:(row + 1) * own], (((0,), (0,)), ((), ())),
            precision=HIGH, preferred_element_type=F32,
        ).T
        for z in range(0, NZ, 2):
            even = mixed[pl.ds(z, cols, stride=NZ), :]
            odd = mixed[pl.ds(z + 1, cols, stride=NZ), :]
            solution_ref[row, :, z * K:(z + 2) * K] = jnp.where(low, even, pltpu.roll(odd, K, 1))
            residual_ref[row, :, z * K:(z + 2) * K] = jnp.where(low, pltpu.roll(even, K, 1), odd)
        for side, (here, there) in enumerate(
            ((solution_ref, solution_out), (residual_ref, residual_out))
        ):
            copy = pltpu.make_async_copy(here.at[row], there.at[row], sems.at[side, row])
            copy.start()
            copies.append(copy)
    for copy in copies:
        copy.wait()


def finish(mine, other, unit, fields, rows, cols):
    out = jax.ShapeDtypeStruct((rows, cols, NZ * K), F32)
    return pl.pallas_call(
        finish_kernel,
        out_shape=(out, out),
        in_specs=[pl.BlockSpec(memory_space=pltpu.VMEM)] * 4,
        out_specs=[pl.BlockSpec(memory_space=pl.ANY)] * 2,
        scratch_shapes=[
            pltpu.VMEM((ITERS * K, (ITERS + 1) * K), F32),
            pltpu.VMEM(((ITERS + 1) * K, 2 * K), F32),
            pltpu.VMEM((cols * NZ, 2 * K), F32),
            pltpu.VMEM((rows, cols, NZ * K), F32),
            pltpu.VMEM((rows, cols, NZ * K), F32),
            pltpu.SemaphoreType.DMA((2, rows)),
        ],
        compiler_params=pltpu.CompilerParams(vmem_limit_bytes=40 * 1024 * 1024),
    )(mine, other, unit, fields)


def add_parts(value, *others):
    half = BODY + TAIL // 2
    lost = jnp.zeros_like(value[BODY:half])
    for other in others:
        total = value + other
        old, new, add = value[BODY:half], total[BODY:half], other[BODY:half]
        back = new - old
        lost = lost + ((old - (new - back)) + (add - back))
        value = total
    return jnp.concatenate([value[:half], value[half:] + lost], axis=0)


def flipped(value, axis, *masks):
    count = lax.axis_size(axis)
    return [lax.ppermute(value, axis, [(i, i ^ mask) for i in range(count)]) for mask in masks]


def across(value, *steps):
    chips = lax.axis_size("gx") // 2

    def partner(i, step):
        chip, core = i // 2, i % 2
        return (chip + (step if chip % 2 == 0 else -step)) % chips * 2 + core

    return [
        lax.ppermute(value, "gx", [(i, partner(i, step)) for i in range(2 * chips)])
        for step in steps
    ]


def sum_of_all(value, axis):
    count = lax.axis_size(axis)
    parts = lax.all_to_all(jnp.broadcast_to(value[None], (count,) + value.shape), axis, 0, 0)
    return add_parts(*(parts[i] for i in range(count)))


def from_both(first, last, axis, outer):
    count = lax.axis_size(axis)
    here = lax.axis_index(axis)
    even = lax.rem(here, 2) == 0
    odd = ~even
    one = lax.ppermute(jnp.where(even, first, last), ("gx", "gy"), outer)
    two = lax.ppermute(jnp.where(even, last, first), axis, [(i, i ^ 1) for i in range(count)])
    before, after = jnp.where(odd, two, one), jnp.where(odd, one, two)
    return jnp.where(here == 0, 0.0, before), jnp.where(here == count - 1, 0.0, after)


def outer_pairs():
    wide, high = lax.axis_size("gx"), lax.axis_size("gy")
    along_x, along_y = [], []
    for i in range(wide):
        for j in range(high):
            here = i * high + j
            along_x.append((here, (((i + 1) ^ 1) - 1) % wide * high + j))
            if j in (0, high - 1):
                along_y.append((here, (i ^ 1) * high + j))
            else:
                along_y.append((here, i * high + ((j + 1) ^ 1) - 1))
    return along_x, along_y


def shards(diffusivity, labels, obstacles):
    rows, cols = diffusivity.shape[:2]
    diffusivity, labels, obstacles = (
        jnp.transpose(value, (0, 2, 1)) for value in (diffusivity, labels, obstacles)
    )
    conductive = diffusivity * (1 - obstacles).astype(F32)
    cells = jnp.concatenate([conductive, labels.astype(F32)], axis=0)
    cells = lax.optimization_barrier(cells).reshape(2, rows, NZ, cols)
    cells = jnp.transpose(cells, (0, 1, 3, 2))
    cells = cells.reshape(2, rows, cols * NZ)
    edge = DEEP * NZ
    along_x, along_y = outer_pairs()
    before, after = from_both(cells[:, :, :edge], cells[:, :, -edge:], "gy", along_y)
    here = jnp.concatenate([cells, after, before], axis=2)
    up, down = from_both(here[:, :DEEP], here[:, rows - DEEP:], "gx", along_x)
    fields, keep, send, unit = krylov(up, here, down)
    mine = add_parts(keep, *flipped(send, "gx", 1))
    mine = add_parts(mine, *across(mine, 1))
    mine = add_parts(mine, *across(mine, 3, -1, -3))
    mine = sum_of_all(mine, "gy")
    return finish(mine, *flipped(mine, "gx", 1), unit, fields, rows, cols)


def solution(mesh):
    in_specs = (P("gx", "gy", None), P("gx", "gy", None), P("gx", "gy", None))
    out_specs = (P("gx", "gy", None), P("gx", "gy", None))
    return jax.shard_map(shards, mesh=mesh, in_specs=in_specs, out_specs=out_specs, check_vma=False)
```
